32 devices in a mesh: seq: 8 (over z, y), batch: 4 (over x, core).
Axes of the slice: x: 2, y: 2, z: 4, core: 2. Of those that a mesh axis runs over, the one named last changes fastest.
Arguments:
- hidden: bfloat16 [4, 1024, 2048], P('batch', 'seq'), may hold values from -6 to 6
- segments: int32 [4, 1024], P('batch', 'seq'), may hold values from 0 to 3, as said below
- routes: int32 [4, 1024, 8], P('batch', 'seq'), may hold values from 0 to 63, all different within a row; in each aligned block of 128 rows (0 to 127, 128 to 255, ..., all dimensions but the last counted through in order) at most 32 rows name the same one
- w_in: bfloat16 [2048, 6144], P(('seq', 'batch')), may hold values from -0.125 to 0.125
- w_out: bfloat16 [2048, 2048], P(('seq', 'batch')), may hold values from -2 to 2
- w_router: bfloat16 [2048, 64], P(('seq', 'batch')), may hold values from -0.0625 to 0.0625
- gains: bfloat16 [4, 2048], P(None, ('seq', 'batch')), may hold values from 0.5 to 1.5
- w_expert: bfloat16 [64, 3, 2048, 1024], P('seq', None, None, 'batch')
- cotangent: bfloat16 [4, 1024, 2048], P('batch', 'seq'), may hold values from -6 to 6
Outputs:
- output: bfloat16 [4, 1024, 2048], P('batch', 'seq')
- input_grad: float32 [4, 1024, 2048], P('batch', 'seq')
- w_in_grad: float32 [2048, 6144], P(('seq', 'batch'))
- w_out_grad: float32 [2048, 2048], P(('seq', 'batch'))
- w_router_grad: float32 [2048, 64], P(('seq', 'batch'))
- gains_grad: float32 [4, 2048], P(None, ('seq', 'batch'))
- w_expert_grad: float32 [64, 3, 2048, 1024], P('seq', None, None, 'batch')
The draws below stay inside these ranges and needn't reach their ends.
Inputs may be any that keep to these rules, and one draw needn't show every extreme that they name: `segments`: ids never fall along a sequence and start at 0; in one sequence, chosen by the seed, all are 0; every other sequence ends at 3. `routes`: in the 128 rows of one device (aligned blocks) no expert is named more than 32 times, and in some device's rows some expert is named exactly 32 times.
All inputs are finite; a program needn't handle non-finite values.
Results may differ from the reference program's by a relative error of at most 0.025.
Values may be sent and summed in bfloat16 or wider, within the bound.
A program may use at most 448 MiB of HBM per device.

```python
import math
import jax
import jax.numpy as jnp
import numpy as np
from jax import lax

D = 2048
HEADS = 16
HEAD_DIM = 128
EXPERTS = 64
TOPK = 8
FF = 1024
TOK_DEV = 128
LENGTH = 1024
GROUPS = 4
CAP = 32


def draw_segments(key, part):
    key = jax.random.fold_in(key, 11)
    key_cut, key_whole = jax.random.split(key)
    cuts = jax.random.randint(key_cut, (GROUPS, 3), 1, LENGTH)
    whole = jax.random.randint(key_whole, (), 0, GROUPS)
    places = jnp.arange(LENGTH, dtype=jnp.int32)
    ids = jnp.sum((places[None, :, None] >= cuts[:, None, :]).astype(jnp.int32), axis=2).astype(jnp.int32)
    keep = (jnp.arange(GROUPS, dtype=jnp.int32) != whole).astype(jnp.int32)
    return ids * keep[:, None]


def draw_w_expert(key, part):
    key = jax.random.fold_in(key, 23)
    shape = (EXPERTS, 3, D, FF)
    base = jax.random.normal(key, shape, jnp.float32)
    factors = jnp.array([2.5 * D ** (-0.5), 2.5 * D ** (-0.5), 4.0 * FF ** (-0.5)], jnp.float32)
    return (base * factors[None, :, None, None]).astype(jnp.bfloat16)


def level_of(rng, dims, shards, smallest, high):
    level = 1.0
    for dim, parts in shards:
        draws = jax.random.uniform(jax.random.fold_in(jax.random.fold_in(rng, 6), dim), (parts,), jnp.float32, smallest / len(shards), high / len(shards))
        level = level * jnp.repeat(jnp.exp(draws), dims[dim] // parts).reshape((-1,) + (1,) * (len(dims) - 1 - dim))
    return level


def shared_out(key, own, number, rows, amount, top, limit, skew):
    sequence = jax.random.permutation(key, amount)
    crowded, usual = portions_of(amount, rows * top, limit, skew, True), portions_of(amount, rows * top, limit, skew, False)
    places = jnp.arange(amount)

    def named(lengths, turn):
        used = int((lengths > 0).sum())
        fixed = max(1, used // 4)
        moved = fixed + (places - fixed + turn * (used - fixed)) % max(1, amount - fixed)
        return jnp.zeros((amount,), jnp.int32).at[sequence[jnp.where(places < fixed, places, moved)]].set(jnp.asarray(lengths, jnp.int32))

    lengths = jnp.where(number % 4 == 0, named(crowded, number // 4), named(usual, number - number // 4 - 1))
    mixed = jax.random.permutation(jax.random.fold_in(own, 3), amount)
    donor, sink = mixed[0:amount // 2 * 2:2], mixed[1:amount // 2 * 2:2]
    slack = jnp.minimum(lengths[donor] - 1, limit - lengths[sink]) // 2
    slack = jnp.where((donor == sequence[0]) | (sink == sequence[0]) | (lengths[sink] == 0), 0, jnp.maximum(slack, 0))
    moved = jax.random.randint(jax.random.fold_in(own, 4), (amount // 2,), 0, 1 << 20) % (slack + 1)
    lengths = lengths.at[donor].add(-moved).at[sink].add(moved)
    members = jnp.searchsorted(jnp.cumsum(lengths), jnp.arange(rows * top), side="right").astype(jnp.int32)
    table = members.reshape(top, rows).T
    table = table[jax.random.permutation(jax.random.fold_in(own, 1), rows)]
    turn = jax.random.randint(jax.random.fold_in(own, 2), (rows, 1), 0, top)
    return jnp.take_along_axis(table, (jnp.arange(top)[None, :] + turn) % top, axis=1)


def portions_of(number_of, total, most, slope, full):
    loads = [(1 << 20) // math.isqrt(rank ** slope) + 1 for rank in range(1, number_of + 1)]
    largest = most if full else min(most, max(-(-total // number_of), total * loads[0] // sum(loads)))
    least = 1 if total - largest >= number_of - 1 else 0
    given, spare = [largest] + [least] * (number_of - 1), total - largest - least * (number_of - 1)
    while spare > 0:
        movable = [i for i in range(1, number_of) if given[i] < largest] or [i for i in range(1, number_of) if given[i] < most]
        pool, budget = sum([loads[i] for i in movable]), spare
        for i in movable:
            addition = min(most - given[i], max(1, budget * loads[i] // pool), spare)
            given[i] = given[i] + addition
            spare = spare - addition
    return np.array(given)


def scatter_about(own_key, dims, width, most, cuts=(), held_as=jnp.bfloat16):
    values = width * jax.random.normal(own_key, dims, jnp.float32)
    if cuts:
        values = values * level_of(own_key, dims, cuts, -0.22, 0.18)
    return jnp.clip(values, -most, most).astype(held_as)


def setup_inputs(seed: int = 0) -> dict:
    key_list = jax.random.split(jax.random.key(seed), 10)
    hidden = scatter_about(key_list[0], (GROUPS, LENGTH, D), 1.0, 6.0, ((0, 4), (1, 8)))
    segments = draw_segments(jax.random.fold_in(key_list[9], 71), 0)
    routes_keys = jax.random.split(jax.random.fold_in(key_list[2], 1), GROUPS * LENGTH // TOK_DEV)
    routes_turns = jax.random.permutation(jax.random.fold_in(key_list[2], 3), GROUPS * LENGTH // TOK_DEV)
    routes = jax.vmap(lambda own, number: shared_out(jax.random.fold_in(key_list[2], 2), own, number, TOK_DEV, EXPERTS, TOPK, CAP, 2))(routes_keys, routes_turns).reshape((GROUPS, LENGTH, TOPK))
    w_in = scatter_about(key_list[3], (D, 3 * D), D ** -0.5, 0.125, ((0, 32),))
    w_out = scatter_about(key_list[4], (D, D), (max(D // 256, 1)) ** -0.5, 2.0, ((0, 32),))
    w_router = scatter_about(key_list[5], (D, EXPERTS), (4 * D) ** -0.5, 0.0625, ((0, 32),))
    gains = jnp.clip(1.0 + 0.1 * jax.random.normal(key_list[6], (4, D), jnp.float32), 0.5, 1.5).astype(jnp.bfloat16)
    w_expert = draw_w_expert(jax.random.fold_in(key_list[9], 71), 0)
    cotangent = scatter_about(key_list[8], (GROUPS, LENGTH, D), 1.0, 6.0, ((0, 4), (1, 8)))
    return {"hidden": hidden, "segments": segments, "routes": routes, "w_in": w_in, "w_out": w_out, "w_router": w_router, "gains": gains, "w_expert": w_expert, "cotangent": cotangent}


epsilon = 1e-05
highest = lax.Precision.HIGHEST

@jax.custom_vjp
def low(v):
    return lax.optimization_barrier(v.astype(jnp.bfloat16)).astype(jnp.float32)

@jax.custom_vjp
def low_back(v):
    return v

def low_keep(v):
    return (low(v), None)

def low_pass(kept, grad):
    return (grad,)

def back_keep(v):
    return (v, None)

def back_low(kept, grad):
    return (low(grad),)
low.defvjp(low_keep, low_pass)
low_back.defvjp(back_keep, back_low)

def rms_scale(values):
    return lax.rsqrt(lax.optimization_barrier(jnp.mean(values * values, axis=-1, keepdims=True)) + epsilon)

def rotate_half(values):
    half = values.shape[-1] // 2
    return jnp.concatenate([-values[..., half:], values[..., :half]], axis=-1)

def rope_tables(length):
    steps = jnp.arange(HEAD_DIM // 2, dtype=jnp.float32)
    freqs = jnp.exp(steps * (-2.0 * jnp.log(10000.0) / HEAD_DIM))
    places = jnp.arange(length, dtype=jnp.float32)
    angles = places[:, None] * freqs[None, :]
    angles = jnp.concatenate([angles, angles], axis=-1)
    return (jnp.cos(angles)[:, None, :], jnp.sin(angles)[:, None, :])

def attend(query, key, value, segment):
    length = query.shape[0]
    block = min(512, length)
    scale = HEAD_DIM ** (-0.5)

    def one_block(start):
        rows_query = lax.dynamic_slice_in_dim(query, start, block, 0)
        rows_segment = lax.dynamic_slice_in_dim(segment, start, block, 0)
        scores = low_back(jnp.einsum('qhd,khd->hqk', rows_query, key, precision=highest) * scale)
        query_place = start + jnp.arange(block, dtype=jnp.int32)
        key_place = jnp.arange(length, dtype=jnp.int32)
        allowed = (key_place[None, :] <= query_place[:, None]) & (segment[None, :] == rows_segment[:, None])
        scores = jnp.where(allowed[None], scores, -1e+30)
        largest = lax.optimization_barrier(jnp.max(scores, axis=-1, keepdims=True))
        weights = jnp.exp(scores - largest)
        probs = low(weights / lax.optimization_barrier(jnp.sum(weights, axis=-1, keepdims=True)))
        return jnp.einsum('hqk,khd->qhd', probs, value, precision=highest)
    starts = jnp.arange(0, length, block, dtype=jnp.int32)
    pieces = lax.map(jax.checkpoint(one_block), starts)
    return pieces.reshape(length, HEADS, HEAD_DIM)

def slot_tables(route_blocks):
    blocks = route_blocks.shape[0]
    pairs = route_blocks.shape[1]
    onehot = (route_blocks[..., None] == jnp.arange(EXPERTS, dtype=jnp.int32)).astype(jnp.int32)
    rank = jnp.cumsum(onehot, axis=1, dtype=jnp.int32) - onehot
    slot = lax.optimization_barrier(jnp.sum(rank * onehot, axis=2)).astype(jnp.int32)
    target = (route_blocks * CAP + slot).astype(jnp.int32)
    source = jnp.full((blocks, EXPERTS * CAP), pairs, jnp.int32)
    block_index = jnp.arange(blocks, dtype=jnp.int32)[:, None]
    source = source.at[block_index, target].set(jnp.broadcast_to(jnp.arange(pairs, dtype=jnp.int32)[None, :], (blocks, pairs)))
    return (target, source)

def layer(inputs, w_in, w_out, w_router, gains, w_expert, segments, routes):
    cosine, sine = rope_tables(LENGTH)

    def attention_branch(item):
        rows_in, segment = item
        normed = low(rows_in * rms_scale(rows_in) * gains[0])
        projected = low_back(jnp.dot(normed, w_in, precision=highest))
        query_raw = projected[:, :D]
        key_raw = projected[:, D:2 * D]
        value_raw = projected[:, 2 * D:]
        query_norm = (query_raw * rms_scale(query_raw) * gains[1]).reshape(LENGTH, HEADS, HEAD_DIM)
        key_norm = (key_raw * rms_scale(key_raw) * gains[2]).reshape(LENGTH, HEADS, HEAD_DIM)
        query = low(query_norm * cosine + rotate_half(query_norm) * sine)
        key = low(key_norm * cosine + rotate_half(key_norm) * sine)
        value = low(value_raw.reshape(LENGTH, HEADS, HEAD_DIM))
        mixed = attend(query, key, value, segment).reshape(LENGTH, D)
        attn = low_back(low(mixed))
        return rows_in + low_back(jnp.dot(attn, w_out, precision=highest))
    middle = lax.map(attention_branch, (inputs, segments))
    flat = middle.reshape(-1, D)
    normed = low(flat * rms_scale(flat) * gains[3])
    logits = low_back(jnp.dot(normed, w_router, precision=highest))
    router = jax.nn.softmax(logits, axis=-1)
    chosen = routes.reshape(-1, TOPK)
    gates = jnp.take_along_axis(router, chosen, axis=1)
    blocks = flat.shape[0] // TOK_DEV
    target, source = slot_tables(chosen.reshape(blocks, TOK_DEV * TOPK))
    padded = jnp.concatenate([normed.reshape(blocks, TOK_DEV, D), jnp.zeros((blocks, 1, D), jnp.float32)], axis=1)
    rows_of = jnp.transpose((source // TOPK).reshape(blocks, EXPERTS, CAP), (1, 0, 2))
    block_index = jnp.arange(blocks, dtype=jnp.int32)[:, None]

    def expert(item):
        slot_rows, weight = item
        slot_in = low_back(padded[block_index, slot_rows]).reshape(blocks * CAP, D)
        gate = jnp.dot(slot_in, weight[0], precision=highest)
        up = jnp.dot(slot_in, weight[1], precision=highest)
        both = low_back(jnp.stack([gate, up]))
        act = low(jax.nn.silu(both[0]) * both[1])
        result = jnp.dot(act, weight[2].T, precision=highest)
        return low_back(low(result)).reshape(blocks, CAP, D)
    results = lax.map(jax.checkpoint(expert), (rows_of, w_expert))
    flat_results = jnp.transpose(results, (1, 0, 2, 3)).reshape(blocks, EXPERTS * CAP, D)
    picked = flat_results[block_index, target].reshape(-1, TOPK, D)
    mixture = lax.optimization_barrier(jnp.sum(gates[..., None] * picked, axis=1))
    return (flat + mixture).reshape(inputs.shape)

def reference(hidden, segments, routes, w_in, w_out, w_router, gains, w_expert, cotangent):

    def forward(inputs, weight_in, weight_out, weight_router, gain_rows, weight_expert):
        return layer(inputs, weight_in, weight_out, weight_router, gain_rows, weight_expert, segments, routes)
    primal = (hidden.astype(jnp.float32), w_in.astype(jnp.float32), w_out.astype(jnp.float32), w_router.astype(jnp.float32), gains.astype(jnp.float32), w_expert.astype(jnp.float32))
    result, pullback = jax.vjp(forward, *primal)
    grads = pullback(cotangent.astype(jnp.float32))
    return (result.astype(jnp.bfloat16), grads[0], grads[1], grads[2], grads[3], grads[4], grads[5])
```

```python
import jax
import jax.numpy as jnp
from jax import lax
from jax.sharding import PartitionSpec as P

HEADS = 16
CAP = 32
epsilon = 1e-05
BOTH = ("seq", "batch")
f32 = jnp.float32
bf16 = jnp.bfloat16


def rms_scale(values):
    return lax.rsqrt(jnp.mean(values * values, axis=-1, keepdims=True) + epsilon)


def rotate_half(values):
    half = values.shape[-1] // 2
    return jnp.concatenate([-values[..., half:], values[..., :half]], axis=-1)


def rope_tables(positions, head_size):
    steps = jnp.arange(head_size // 2, dtype=f32)
    freqs = jnp.exp(steps * (-2.0 * jnp.log(10000.0) / head_size))
    angles = positions.astype(f32)[:, None] * freqs[None, :]
    angles = jnp.concatenate([angles, angles], axis=-1)
    return (jnp.cos(angles)[:, None, :], jnp.sin(angles)[:, None, :])


def norm_back(grad_out, normal, scale, gain):
    scaled = grad_out * gain
    return scale * (scaled - normal * jnp.mean(scaled * normal, axis=-1, keepdims=True))


def dot(a, b, dims):
    return lax.dot_general(a, b, (dims, ((), ())), preferred_element_type=f32)


class HeadsAttention:
    def __init__(self, hidden, segment_all, w_in, w_out, gains_all):
        seq = lax.axis_size("seq")
        batch = lax.axis_size("batch")
        place = lax.axis_index("seq")
        self.rows = hidden.shape[0]
        width = hidden.shape[1]
        self.width = width
        self.hs = width // HEADS
        self.hl = HEADS // seq
        cols = self.hl * self.hs
        self.cols = cols
        own = w_in.shape[0]
        hidden_all = lax.all_gather(hidden, "seq", axis=0, tiled=True)
        length = hidden_all.shape[0]
        self.length = length
        parts = w_in.reshape(own, 3, seq, cols)
        parts = lax.all_to_all(parts, "seq", split_axis=2, concat_axis=2, tiled=True)
        parts = jnp.transpose(parts, (2, 0, 1, 3)).reshape(seq, own, 3 * cols)
        self.w_cols = lax.all_gather(parts, "batch", axis=1, tiled=True).reshape(width, 3 * cols)
        self.w_rows = lax.all_gather(w_out, "batch", axis=0, tiled=True)
        inputs = hidden_all.astype(f32)
        normed = (inputs * rms_scale(inputs) * gains_all[0]).astype(bf16)
        self.normed = normed
        projected = jnp.dot(normed, self.w_cols, preferred_element_type=f32)
        query_raw = projected[:, :cols]
        key_raw = projected[:, cols : 2 * cols]
        squares = jnp.stack([jnp.sum(query_raw * query_raw, -1), jnp.sum(key_raw * key_raw, -1)], 0)
        scales = lax.rsqrt(lax.psum(squares, "seq") / width + epsilon)
        self.query_scale = scales[0][:, None]
        self.key_scale = scales[1][:, None]
        self.query_normal = query_raw * self.query_scale
        self.key_normal = key_raw * self.key_scale
        mine = lax.dynamic_slice_in_dim(gains_all, place * cols, cols, 1)
        self.query_gain, self.key_gain = mine[1], mine[2]
        positions = jnp.arange(length, dtype=jnp.int32)
        self.cosine, self.sine = rope_tables(positions, self.hs)
        shape = (length, self.hl, self.hs)

        def rot(u):
            u = u.reshape(shape)
            return (u * self.cosine + rotate_half(u) * self.sine).astype(bf16)

        self.query = rot(self.query_normal * self.query_gain)
        self.key = rot(self.key_normal * self.key_gain)
        self.value = projected[:, 2 * cols :].astype(bf16).reshape(shape)
        self.allowed = (positions[None, :] <= positions[:, None]) & (
            segment_all[None, :] == segment_all[:, None]
        )
        scores = self.scores()
        top = jnp.max(scores, axis=-1, keepdims=True)
        weights = jnp.exp(scores - top)
        total = jnp.sum(weights, axis=-1, keepdims=True)
        acc = jnp.einsum("hqk,khd->hqd", weights.astype(bf16), self.value, preferred_element_type=f32)
        self.log_total = top + jnp.log(total)
        self.attended = jnp.transpose(acc / total, (1, 0, 2))
        self.attn_low = self.attended.reshape(length, cols).astype(bf16)
        partial = jnp.dot(self.attn_low, self.w_rows, preferred_element_type=f32).astype(bf16)
        self.mixed = lax.psum_scatter(partial, "seq", scatter_dimension=0, tiled=True).astype(f32)

    def scores(self):
        scale = self.hs ** (-0.5)
        scores = jnp.einsum("qhd,khd->hqk", self.query, self.key, preferred_element_type=f32) * scale
        return jnp.where(self.allowed[None], scores, -jnp.inf)

    def back(self, middle_low):
        seq = lax.axis_size("seq")
        batch = lax.axis_size("batch")
        length, cols, width = self.length, self.cols, self.width
        scale = self.hs ** (-0.5)
        shape = (length, self.hl, self.hs)
        grad_all = lax.all_gather(middle_low, "seq", axis=0, tiled=True)
        out_grad = dot(self.attn_low, grad_all, ((0,), (0,))).astype(bf16)
        out_shard = lax.psum_scatter(out_grad, "batch", scatter_dimension=0, tiled=True).astype(f32)
        attn_grad = dot(grad_all, self.w_rows, ((1,), (1,))).astype(bf16).reshape(shape)
        delta = jnp.sum(attn_grad.astype(f32) * self.attended, axis=-1)
        probs = jnp.exp(self.scores() - self.log_total)
        prob_grad = jnp.einsum("qhd,khd->hqk", attn_grad, self.value, preferred_element_type=f32)
        score_grad = (probs * (prob_grad - delta.T[..., None])).astype(bf16)
        query_grad = jnp.einsum("hqk,khd->qhd", score_grad, self.key, preferred_element_type=f32) * scale
        key_grad = jnp.einsum("hqk,qhd->khd", score_grad, self.query, preferred_element_type=f32) * scale
        value_grad = jnp.einsum("hqk,qhd->khd", probs.astype(bf16), attn_grad, preferred_element_type=f32)

        def rot_back(u):
            return (u * self.cosine - rotate_half(u * self.sine)).reshape(length, cols)

        query_norm_grad = rot_back(query_grad)
        key_norm_grad = rot_back(key_grad)
        query_gain_grad = jnp.sum(query_norm_grad * self.query_normal, axis=0)
        key_gain_grad = jnp.sum(key_norm_grad * self.key_normal, axis=0)
        query_scaled = query_norm_grad * self.query_gain
        key_scaled = key_norm_grad * self.key_gain
        means = lax.psum(
            jnp.stack([jnp.sum(query_scaled * self.query_normal, -1), jnp.sum(key_scaled * self.key_normal, -1)], 0),
            "seq",
        ) / width
        query_raw_grad = self.query_scale * (query_scaled - self.query_normal * means[0][:, None])
        key_raw_grad = self.key_scale * (key_scaled - self.key_normal * means[1][:, None])
        projected_grad = jnp.concatenate(
            [query_raw_grad, key_raw_grad, value_grad.reshape(length, cols)], axis=1
        ).astype(bf16)
        partial = dot(projected_grad, self.w_cols, ((1,), (1,))).astype(bf16)
        normed_grad = lax.psum_scatter(partial, "seq", scatter_dimension=0, tiled=True).astype(f32)
        in_grad = dot(self.normed, projected_grad, ((0,), (0,))).astype(bf16)
        own = width // (seq * batch)
        in_grad = lax.psum_scatter(
            in_grad.reshape(seq, batch * own, 3 * cols), "batch", scatter_dimension=1, tiled=True
        )
        in_grad = lax.all_to_all(in_grad, "seq", split_axis=0, concat_axis=0, tiled=True)
        in_shard = jnp.transpose(in_grad.reshape(seq, own, 3, cols), (1, 2, 0, 3)).reshape(own, 3 * width)
        pair = lax.psum_scatter(
            jnp.stack([query_gain_grad, key_gain_grad], 1), "batch", scatter_dimension=0, tiled=True
        )
        return normed_grad, in_shard.astype(f32), out_shard, pair


class TokensAttention:
    def __init__(self, hidden, segment_all, w_in, w_out, gains_all):
        place = lax.axis_index("seq")
        rows, width = hidden.shape
        self.rows, self.width = rows, width
        self.hs = width // HEADS
        self.sources = w_in, w_out
        self.gather_weights(w_in, w_out)
        inputs = hidden.astype(f32)
        self.normed = (inputs * rms_scale(inputs) * gains_all[0]).astype(bf16)
        projected = jnp.dot(self.normed, self.in_all, preferred_element_type=f32)
        query_raw = projected[:, :width]
        key_raw = projected[:, width : 2 * width]
        self.query_scale = rms_scale(query_raw)
        self.query_normal = query_raw * self.query_scale
        self.key_scale = rms_scale(key_raw)
        self.key_normal = key_raw * self.key_scale
        self.query_gain, self.key_gain = gains_all[1], gains_all[2]
        self.positions = place * rows + jnp.arange(rows, dtype=jnp.int32)
        self.cosine, self.sine = rope_tables(self.positions, self.hs)
        shape = (rows, HEADS, self.hs)

        def rot(u):
            u = u.reshape(shape)
            return (u * self.cosine + rotate_half(u) * self.sine).astype(bf16)

        self.query = rot(self.query_normal * self.query_gain)
        key = rot(self.key_normal * self.key_gain).reshape(rows, width)
        value = projected[:, 2 * width :].astype(bf16)
        self.kept = key, value
        self.gather_keys(key, value)
        self.segment_all = segment_all
        self.segment_own = lax.dynamic_slice_in_dim(segment_all, place * rows, rows, 0)
        length = self.key_all.shape[0]
        scores = self.scores(self.key_all.reshape(length, HEADS, self.hs), segment_all, 0)
        top = jnp.max(scores, axis=-1, keepdims=True)
        weights = jnp.exp(scores - top)
        total = jnp.sum(weights, axis=-1, keepdims=True)
        acc = jnp.einsum(
            "hqk,khd->hqd",
            weights.astype(bf16),
            self.value_all.reshape(length, HEADS, self.hs),
            preferred_element_type=f32,
        )
        self.log_total = top + jnp.log(total)
        self.attended = jnp.transpose(acc / total, (1, 0, 2))
        self.attn_low = self.attended.reshape(rows, width).astype(bf16)
        self.mixed = jnp.dot(self.attn_low, self.out_all, preferred_element_type=f32)

    def gather_weights(self, w_in, w_out):
        self.in_all = lax.all_gather(w_in, BOTH, axis=0, tiled=True)
        self.out_all = lax.all_gather(w_out, BOTH, axis=0, tiled=True)

    def gather_keys(self, key, value):
        self.key_all = lax.all_gather(key, "seq", axis=0, tiled=True)
        self.value_all = lax.all_gather(value, "seq", axis=0, tiled=True)

    def scores(self, key, segment, start):
        scale = self.hs ** (-0.5)
        scores = jnp.einsum("qhd,khd->hqk", self.query, key, preferred_element_type=f32) * scale
        key_positions = start + jnp.arange(key.shape[0], dtype=jnp.int32)
        allowed = (key_positions[None, :] <= self.positions[:, None]) & (
            segment[None, :] == self.segment_own[:, None]
        )
        return jnp.where(allowed[None], scores, -jnp.inf)

    def back(self, middle_low):
        again = lax.optimization_barrier((middle_low, *self.sources, *self.kept))
        middle_low = again[0]
        self.gather_weights(*again[1:3])
        self.gather_keys(*again[3:])
        rows, width = self.rows, self.width
        scale = self.hs ** (-0.5)
        out_grad = dot(self.attn_low, middle_low, ((0,), (0,))).astype(bf16)
        out_shard = lax.psum_scatter(out_grad, BOTH, scatter_dimension=0, tiled=True).astype(f32)
        attn_grad = dot(middle_low, self.out_all, ((1,), (1,))).astype(bf16).reshape(rows, HEADS, self.hs)
        delta = jnp.sum(attn_grad.astype(f32) * self.attended, axis=-1).T
        length = self.key_all.shape[0]
        block = min(512, length)
        count = length // block

        def step(query_grad, item):
            key, value, segment, start = item
            probs = jnp.exp(self.scores(key, segment, start) - self.log_total)
            prob_grad = jnp.einsum("qhd,khd->hqk", attn_grad, value, preferred_element_type=f32)
            score_grad = (probs * (prob_grad - delta[..., None])).astype(bf16)
            query_grad = (
                query_grad + jnp.einsum("hqk,khd->qhd", score_grad, key, preferred_element_type=f32) * scale
            )
            key_grad = jnp.einsum("hqk,qhd->khd", score_grad, self.query, preferred_element_type=f32) * scale
            value_grad = jnp.einsum("hqk,qhd->khd", probs.astype(bf16), attn_grad, preferred_element_type=f32)
            return query_grad, jnp.concatenate(
                [key_grad.reshape(block, width), value_grad.reshape(block, width)], axis=1
            ).astype(bf16)

        query_grad, terms = lax.scan(
            step,
            jnp.zeros((rows, HEADS, self.hs), f32),
            (
                self.key_all.reshape(count, block, HEADS, self.hs),
                self.value_all.reshape(count, block, HEADS, self.hs),
                self.segment_all.reshape(count, block),
                jnp.arange(count, dtype=jnp.int32) * block,
            ),
        )
        kv_grad = lax.psum_scatter(
            terms.reshape(length, 2 * width), "seq", scatter_dimension=0, tiled=True
        ).astype(f32)
        key_grad = kv_grad[:, :width].reshape(rows, HEADS, self.hs)

        def rot_back(u):
            return (u * self.cosine - rotate_half(u * self.sine)).reshape(rows, width)

        query_norm_grad = rot_back(query_grad)
        key_norm_grad = rot_back(key_grad)
        query_gain_grad = jnp.sum(query_norm_grad * self.query_normal, axis=0)
        key_gain_grad = jnp.sum(key_norm_grad * self.key_normal, axis=0)
        query_raw_grad = norm_back(query_norm_grad, self.query_normal, self.query_scale, self.query_gain)
        key_raw_grad = norm_back(key_norm_grad, self.key_normal, self.key_scale, self.key_gain)
        projected_grad = jnp.concatenate([query_raw_grad, key_raw_grad, kv_grad[:, width:]], axis=1).astype(bf16)
        in_grad = dot(self.normed, projected_grad, ((0,), (0,))).astype(bf16)
        in_shard = lax.psum_scatter(in_grad, BOTH, scatter_dimension=0, tiled=True).astype(f32)
        normed_grad = dot(projected_grad, self.in_all, ((1,), (1,)))
        pair = lax.psum_scatter(
            jnp.stack([query_gain_grad, key_gain_grad], 1), BOTH, scatter_dimension=0, tiled=True
        )
        return normed_grad, in_shard, out_shard, pair


def expert_math(slots, grads, gate_slot, w_expert):
    w_gate, w_up, w_down = w_expert[:, 0], w_expert[:, 1], w_expert[:, 2]
    gate = jnp.einsum("esd,edf->esf", slots, w_gate, preferred_element_type=f32)
    up = jnp.einsum("esd,edf->esf", slots, w_up, preferred_element_type=f32)
    sigma = jax.nn.sigmoid(gate)
    silu = gate * sigma
    act = (silu * up).astype(bf16).astype(f32)
    act_gated = (act * gate_slot).astype(bf16)
    act_raw = jnp.einsum("esd,edf->esf", grads, w_down, preferred_element_type=f32)
    gate_grad = jnp.sum(act_raw * act, axis=-1)
    act_grad = act_raw * gate_slot
    gate_low = (act_grad * up * sigma * (1.0 + gate * (1.0 - sigma))).astype(bf16)
    up_low = (act_grad * silu).astype(bf16)
    slot_grad = (
        jnp.einsum("esf,edf->esd", gate_low, w_gate, preferred_element_type=f32)
        + jnp.einsum("esf,edf->esd", up_low, w_up, preferred_element_type=f32)
    ).astype(bf16)
    result = jnp.einsum("esf,edf->esd", act_gated, w_down, preferred_element_type=f32).astype(bf16)
    expert_grad = jnp.stack(
        [
            jnp.einsum("esd,esf->edf", slots, gate_low, preferred_element_type=f32),
            jnp.einsum("esd,esf->edf", slots, up_low, preferred_element_type=f32),
            jnp.einsum("esd,esf->edf", grads, act_gated, preferred_element_type=f32),
        ],
        axis=1,
    )
    return result, slot_grad, gate_grad, expert_grad


def slot_places(hit):
    count = hit.astype(jnp.int32)
    rank = jnp.where(hit, jnp.cumsum(count, axis=1) - count, -1)
    return rank[:, :, :, None] == jnp.arange(CAP, dtype=jnp.int32)


def experts_by_tokens(ffn_in, cotangent, routes, w_expert, router_all):
    seq, batch = lax.axis_size("seq"), lax.axis_size("batch")
    place = lax.axis_index("seq")
    everyone = seq * batch
    experts = w_expert.shape[0]
    rows, width = ffn_in.shape
    routes_all = lax.all_gather(routes, BOTH, axis=0, tiled=True)
    cotangent_all = lax.all_gather(cotangent, BOTH, axis=0, tiled=True)
    ffn_all = lax.all_gather(ffn_in, BOTH, axis=0, tiled=True)
    mine = place * experts + jnp.arange(experts, dtype=jnp.int32)
    hit = jnp.any(routes_all[:, :, None] == mine[None, None, :], axis=1).reshape(everyone, rows, experts)
    hot = slot_places(hit)
    place_hot = jnp.transpose(hot, (0, 2, 3, 1)).astype(bf16).reshape(everyone, experts * CAP, rows)
    router_every = jax.nn.softmax(jnp.dot(ffn_all, router_all, preferred_element_type=f32), axis=-1)
    router_mine = lax.dynamic_slice_in_dim(router_every, place * experts, experts, 1)
    gate_slot = jnp.sum(jnp.where(hot, router_mine.reshape(everyone, rows, experts, 1), 0.0), axis=1)
    gate_slot = jnp.transpose(gate_slot, (1, 0, 2)).reshape(experts, everyone * CAP, 1)

    def dispatch(tokens):
        slots = jnp.einsum(
            "dst,dth->dsh", place_hot, tokens.reshape(everyone, rows, width), preferred_element_type=f32
        ).astype(bf16)
        slots = jnp.transpose(slots.reshape(everyone, experts, CAP, width), (1, 0, 2, 3))
        return slots.reshape(experts, everyone * CAP, width)

    def combine(values):
        values = jnp.transpose(values.reshape(experts, everyone, CAP, width), (1, 0, 2, 3))
        values = values.reshape(everyone, experts * CAP, width)
        return (
            jnp.einsum("dst,dsh->dth", place_hot, values, preferred_element_type=f32)
            .astype(bf16)
            .reshape(everyone * rows, width)
        )

    result, slot_grad, gate_grad, expert_grad = expert_math(
        dispatch(ffn_all), dispatch(cotangent_all), gate_slot, w_expert
    )
    gate_grad = jnp.transpose(gate_grad.reshape(experts, everyone, CAP), (1, 0, 2))
    gate_part = jnp.sum(jnp.where(hot, gate_grad[:, None], 0.0), axis=-1)
    gate_part = gate_part.reshape(seq, batch * rows, experts)
    gate_part = lax.psum_scatter(gate_part, "batch", scatter_dimension=1, tiled=True)
    gate_part = lax.all_to_all(gate_part, "seq", split_axis=0, concat_axis=0, tiled=True)
    prob_grad = jnp.transpose(gate_part, (1, 0, 2)).reshape(rows, seq * experts)
    ffn_in_grad = lax.psum_scatter(combine(slot_grad), BOTH, scatter_dimension=0, tiled=True).astype(f32)
    mixture = lax.psum_scatter(combine(result), BOTH, scatter_dimension=0, tiled=True).astype(f32)
    return mixture, ffn_in_grad, prob_grad, expert_grad


def experts_by_slots(ffn_in, cotangent, routes, w_expert, router_all):
    seq, batch = lax.axis_size("seq"), lax.axis_size("batch")
    experts = w_expert.shape[0]
    total = experts * seq
    rows, width = ffn_in.shape
    hit = jnp.any(routes[:, :, None] == jnp.arange(total, dtype=jnp.int32), axis=1)[None]
    hot = slot_places(hit)[0]
    place_hot = hot.astype(bf16).reshape(rows, total * CAP)
    router = jax.nn.softmax(jnp.dot(ffn_in, router_all, preferred_element_type=f32), axis=-1)
    gate_slot = jnp.sum(jnp.where(hot, router[:, :, None], 0.0), axis=0).reshape(seq, experts, CAP, 1)

    def there(values):
        values = lax.all_to_all(values, "seq", split_axis=0, concat_axis=0, tiled=True)
        values = lax.all_gather(values, "batch", axis=0, tiled=True)
        values = jnp.transpose(values, (1, 0, 2, 3))
        return values.reshape(experts, batch * seq * CAP, values.shape[-1])

    def back(values):
        values = values.reshape(experts, batch * seq, CAP, values.shape[-1])
        values = jnp.transpose(values, (1, 0, 2, 3))
        values = lax.psum_scatter(values, "batch", scatter_dimension=0, tiled=True)
        values = lax.all_to_all(values, "seq", split_axis=0, concat_axis=0, tiled=True)
        return values.reshape(total * CAP, values.shape[-1])

    def slots_of(tokens):
        slots = dot(place_hot, tokens, ((0,), (0,))).astype(bf16)
        return there(slots.reshape(seq, experts, CAP, width))

    def tokens_of(slots):
        return jnp.dot(place_hot, back(slots), preferred_element_type=f32)

    result, slot_grad, gate_grad, expert_grad = expert_math(
        slots_of(ffn_in), slots_of(cotangent), there(gate_slot), w_expert
    )
    gate_grad = back(gate_grad[..., None]).reshape(1, total, CAP)
    prob_grad = jnp.sum(jnp.where(hot, gate_grad, 0.0), axis=-1)
    return tokens_of(result), tokens_of(slot_grad), prob_grad, expert_grad


def local(hidden, segments, routes, w_in, w_out, w_router, gains, w_expert, cotangent):
    seq = lax.axis_size("seq")
    total_experts = w_expert.shape[0] * seq

    small = lax.all_gather(jnp.concatenate([w_router, gains.T], axis=1), BOTH, axis=0, tiled=True)
    router_all = small[:, :total_experts]
    gains_all = small[:, total_experts:].T.astype(f32)
    segment_all = lax.all_gather(segments[0], "seq", axis=0, tiled=True)

    inputs = hidden[0].astype(f32)
    first_scale = rms_scale(inputs)
    first_normal = inputs * first_scale

    by_heads = HEADS % seq == 0
    attend = HeadsAttention if by_heads else TokensAttention
    mix = experts_by_tokens if by_heads else experts_by_slots
    attention = attend(hidden[0], segment_all, w_in, w_out, gains_all)

    middle = inputs + attention.mixed
    second_scale = rms_scale(middle)
    second_normal = middle * second_scale
    ffn_in = (second_normal * gains_all[3]).astype(bf16)
    mixture, ffn_in_grad, prob_grad, expert_grad = mix(
        ffn_in, cotangent[0], routes[0], w_expert, router_all
    )
    output = middle + mixture

    grad_out = cotangent[0].astype(f32)
    router = jax.nn.softmax(jnp.dot(ffn_in, router_all, preferred_element_type=f32), axis=-1)
    logit_grad = router * (prob_grad - jnp.sum(router * prob_grad, axis=-1, keepdims=True))
    logit_low = logit_grad.astype(bf16)
    router_grad = dot(ffn_in, logit_low, ((0,), (0,)))
    ffn_in_grad = ffn_in_grad + dot(logit_low, router_all, ((1,), (1,)))
    ffn_gain_grad = jnp.sum(ffn_in_grad * second_normal, axis=0)
    middle_grad = grad_out + norm_back(ffn_in_grad, second_normal, second_scale, gains_all[3])
    normed_grad, in_shard, out_shard, pair_shard = attention.back(middle_grad.astype(bf16))
    attn_gain_grad = jnp.sum(normed_grad * first_normal, axis=0)
    input_grad = middle_grad + norm_back(normed_grad, first_normal, first_scale, gains_all[0])
    sums = jnp.concatenate([router_grad, attn_gain_grad[:, None], ffn_gain_grad[:, None]], axis=1)
    sums = lax.psum_scatter(sums, BOTH, scatter_dimension=0, tiled=True)
    router_shard = sums[:, :total_experts]
    ends = sums[:, total_experts:]
    gains_shard = jnp.stack([ends[:, 0], pair_shard[:, 0], pair_shard[:, 1], ends[:, 1]], axis=0)
    return (
        output.astype(bf16)[None],
        input_grad[None],
        in_shard,
        out_shard,
        router_shard,
        gains_shard,
        expert_grad,
    )


def solution(mesh):
    placed = (
        P("batch", "seq", None),
        P("batch", "seq"),
        P("batch", "seq", None),
        P(BOTH, None),
        P(BOTH, None),
        P(BOTH, None),
        P(None, BOTH),
        P("seq", None, None, "batch"),
        P("batch", "seq", None),
    )
    return jax.shard_map(
        local,
        mesh=mesh,
        in_specs=placed,
        out_specs=(
            P("batch", "seq", None),
            P("batch", "seq", None),
            P(BOTH, None),
            P(BOTH, None),
            P(BOTH, None),
            P(None, BOTH),
            P("seq", None, None, "batch"),
        ),
        check_vma=False,
    )
```

```python
import functools

import jax
import jax.numpy as jnp
from jax import lax
from jax.experimental import pallas as pl
from jax.experimental.pallas import tpu as pltpu
from jax.sharding import PartitionSpec as P

HEADS = 16
CAP = 32
epsilon = 1e-05
BOTH = ("seq", "batch")
f32 = jnp.float32
bf16 = jnp.bfloat16
MESH = pl.DeviceIdType.MESH


def rms_scale(values):
    return lax.rsqrt(jnp.mean(values * values, axis=-1, keepdims=True) + epsilon)


def rotate_half(values):
    half = values.shape[-1] // 2
    return jnp.concatenate([-values[..., half:], values[..., :half]], axis=-1)


def rope_tables(positions, head_size):
    steps = jnp.arange(head_size // 2, dtype=f32)
    freqs = jnp.exp(steps * (-2.0 * jnp.log(10000.0) / head_size))
    angles = positions.astype(f32)[:, None] * freqs[None, :]
    angles = jnp.concatenate([angles, angles], axis=-1)
    return (jnp.cos(angles)[:, None, :], jnp.sin(angles)[:, None, :])


def norm_back(grad_out, normal, scale, gain):
    scaled = grad_out * gain
    return scale * (scaled - normal * jnp.mean(scaled * normal, axis=-1, keepdims=True))


def dot(a, b, dims):
    return lax.dot_general(a, b, (dims, ((), ())), preferred_element_type=f32)


ANY = pl.BlockSpec(memory_space=pl.ANY)
WHOLE = pl.BlockSpec(memory_space=pltpu.VMEM)


class Place:
    def __init__(self):
        s, b = lax.axis_index("seq"), lax.axis_index("batch")
        self.z, self.y = s // 2, lax.rem(s, 2)
        self.x, self.c = b // 2, lax.rem(b, 2)

    def at(self, r=0, y=0, x=0, c=0):
        z = lax.rem(self.z + r, 4)
        yy = 1 - self.y if y else self.y
        xx = 1 - self.x if x else self.x
        cc = 1 - self.c if c else self.c
        return (z * 2 + yy, xx * 2 + cc)

    def index(self, r=0, y=0, x=0, c=0):
        s, b = self.at(r, y, x, c)
        return s * 4 + b


def barrier(peers):
    sem = pltpu.get_barrier_semaphore()
    for peer in peers:
        pl.semaphore_signal(sem, inc=1, device_id=peer, device_id_type=MESH)
    pl.semaphore_wait(sem, len(peers))


class Sends:
    def __init__(self, send_sem, recv_sem):
        self.send_sem, self.recv_sem, self.copies = send_sem, recv_sem, []

    def start(self, src, dst, peer):
        k = len(self.copies)
        copy = pltpu.make_async_remote_copy(
            src_ref=src,
            dst_ref=dst,
            send_sem=self.send_sem.at[k],
            recv_sem=self.recv_sem.at[k],
            device_id=peer,
            device_id_type=MESH,
        )
        copy.start()
        self.copies.append(copy)
        return copy

    def finish(self):
        for copy in self.copies:
            copy.wait_send()


def gather_all_kernel(x_ref, out_ref, send_sem, recv_sem, own_sem):
    p = Place()
    rows = x_ref.shape[0]
    half = rows // 2
    barrier([p.at(1), p.at(2), p.at(3), p.at(y=1), p.at(x=1), p.at(c=1)])
    own = pltpu.make_async_copy(x_ref, out_ref.at[p.index()], own_sem)
    own.start()
    sends = Sends(send_sem, recv_sem)
    A, B = pl.ds(0, half), pl.ds(half, half)

    def forward(index, peer, part=None):
        ref = out_ref.at[index] if part is None else out_ref.at[index, part]
        return sends.start(ref, ref, peer)

    mine = p.index()
    along = [None] + [sends.start(x_ref, out_ref.at[mine], p.at(r)) for r in (1, 3, 2)]
    along = {0: None, 1: along[1], 3: along[2], 2: along[3]}
    from_x, from_y, from_core, diag = {}, {}, [], []
    order = (0, 1, 3, 2)
    for r in order:
        index = p.index(-r % 4)
        if r:
            along[r].wait_recv()
        src = x_ref if r == 0 else out_ref.at[index]
        from_x[r] = sends.start(src, out_ref.at[index], p.at(x=1))
        from_y[r] = sends.start(src, out_ref.at[index], p.at(y=1))
        from_core.append(sends.start(src, out_ref.at[index], p.at(c=1)))
    for r in order:
        ix, iy = p.index(-r % 4, x=1), p.index(-r % 4, y=1)
        from_x[r].wait_recv()
        diag.append(forward(ix, p.at(y=1), A))
        from_y[r].wait_recv()
        diag.append(forward(iy, p.at(x=1), B))
        from_core.append(forward(ix, p.at(c=1)))
        from_core.append(forward(iy, p.at(c=1)))
    for n, r in enumerate(order):
        index = p.index(-r % 4, x=1, y=1)
        diag[2 * n].wait_recv()
        diag[2 * n + 1].wait_recv()
        from_core.append(forward(index, p.at(c=1)))
    for copy in from_core:
        copy.wait_recv()
    sends.finish()
    own.wait()


def gather_all(x, collective_id):
    n = 3 + 12 + 8 + 12
    return pl.pallas_call(
        gather_all_kernel,
        name="gather_all",
        out_shape=jax.ShapeDtypeStruct((32,) + x.shape, x.dtype),
        in_specs=[ANY],
        out_specs=ANY,
        scratch_shapes=[
            pltpu.SemaphoreType.DMA((n,)),
            pltpu.SemaphoreType.DMA((n,)),
            pltpu.SemaphoreType.DMA,
        ],
        compiler_params=pltpu.CompilerParams(collective_id=collective_id, has_side_effects=True),
    )(x)


def add_rows(dst, src, start, rows):
    step = 16

    def body(i, _):
        at = pl.ds(pl.multiple_of(start + i * step, step), step)
        dst[at] = (dst[at].astype(f32) + src[at].astype(f32)).astype(dst.dtype)
        return 0

    lax.fori_loop(0, rows // step, body, 0)


def scatter_all_kernel(p_ref, out_ref, acc, rc, rdx, rdy, rx, ry, rz, send_sem, recv_sem, own_sem):
    p = Place()
    rows = acc.shape[1]
    half = rows // 2
    A, B = pl.ds(0, half), pl.ds(half, half)
    barrier([p.at(1), p.at(2), p.at(3), p.at(y=1), p.at(x=1), p.at(c=1)])
    sends = Sends(send_sem, recv_sem)
    order = (2, 1, 3, 0)
    slots = [(r, y, x) for (y, x) in ((1, 1), (0, 1), (1, 0), (0, 0)) for r in order]
    loads, cores = [], []
    for k, (r, y, x) in enumerate(slots):
        load = pltpu.make_async_copy(p_ref.at[p.index(r, y, x)], acc.at[k], own_sem.at[k])
        load.start()
        loads.append(load)
        cores.append(sends.start(p_ref.at[p.index(r, y, x, 1)], rc.at[k], p.at(c=1)))

    def core_sum(k):
        loads[k].wait()
        cores[k].wait_recv()
        add_rows(acc.at[k], rc.at[k], 0, rows)

    dx, dy, fx, fy, fz = [], [], [], [], []
    for n in range(4):
        core_sum(n)
        dy.append(sends.start(acc.at[n, A], rdy.at[n], p.at(y=1)))
        dx.append(sends.start(acc.at[n, B], rdx.at[n], p.at(x=1)))
    for n in range(4):
        core_sum(4 + n)
        dy[n].wait_recv()
        add_rows(acc.at[4 + n], rdy.at[n], 0, half)
        fx.append(sends.start(acc.at[4 + n], rx.at[n], p.at(x=1)))
        core_sum(8 + n)
        dx[n].wait_recv()
        add_rows(acc.at[8 + n, B], rdx.at[n], 0, half)
        fy.append(sends.start(acc.at[8 + n], ry.at[n], p.at(y=1)))
    for n, r in enumerate(order):
        core_sum(12 + n)
        fx[n].wait_recv()
        add_rows(acc.at[12 + n], rx.at[n], 0, rows)
        fy[n].wait_recv()
        add_rows(acc.at[12 + n], ry.at[n], 0, rows)
        if r:
            fz.append(sends.start(acc.at[12 + n], rz.at[n], p.at(r)))
    for copy in fz:
        copy.wait_recv()

    def total(i, _):
        at = pl.ds(pl.multiple_of(i * 16, 16), 16)
        value = acc[15, at].astype(f32)
        for n in range(3):
            value = value + rz[n, at].astype(f32)
        out_ref[at] = value.astype(out_ref.dtype)
        return 0

    lax.fori_loop(0, rows // 16, total, 0)
    sends.finish()


def scatter_all(parts, collective_id, dtype=bf16):
    block = parts.shape[1:]
    half = (block[0] // 2,) + block[1:]
    n = 16 + 8 + 8 + 3
    return pl.pallas_call(
        scatter_all_kernel,
        name="scatter_all",
        out_shape=jax.ShapeDtypeStruct(block, dtype),
        in_specs=[ANY],
        out_specs=WHOLE,
        scratch_shapes=[
            pltpu.VMEM((16,) + block, parts.dtype),
            pltpu.VMEM((16,) + block, parts.dtype),
            pltpu.VMEM((4,) + half, parts.dtype),
            pltpu.VMEM((4,) + half, parts.dtype),
            pltpu.VMEM((4,) + block, parts.dtype),
            pltpu.VMEM((4,) + block, parts.dtype),
            pltpu.VMEM((3,) + block, parts.dtype),
            pltpu.SemaphoreType.DMA((n,)),
            pltpu.SemaphoreType.DMA((n,)),
            pltpu.SemaphoreType.DMA((16,)),
        ],
        compiler_params=pltpu.CompilerParams(
            collective_id=collective_id, has_side_effects=True, vmem_limit_bytes=48 << 20
        ),
    )(parts)


def call(kernel, name, collective_id, out_shape, in_specs, out_specs, scratch, copies, local=1, vmem=32):
    return pl.pallas_call(
        kernel,
        name=name,
        out_shape=out_shape,
        in_specs=in_specs,
        out_specs=out_specs,
        scratch_shapes=[
            *scratch,
            pltpu.SemaphoreType.DMA((copies,)),
            pltpu.SemaphoreType.DMA((copies,)),
            pltpu.SemaphoreType.DMA((local,)),
        ],
        compiler_params=pltpu.CompilerParams(
            collective_id=collective_id, has_side_effects=True, vmem_limit_bytes=vmem << 20
        ),
    )


Z_ORDER = (1, 3, 2)


def gather_first_kernel(
    h_ref, wi_ref, wo_ref, ints_ref, small_ref,
    h_out, wi_out, wo_out, ints_out, small_out,
    ints, small, send_sem, recv_sem, own_sem,
):
    p = Place()
    seq, b = p.at()
    x, c = p.x, p.c
    others = [p.at(r, y) for y in (0, 1) for r in range(4) if r or y]
    barrier(others + [p.at(x=1), p.at(c=1)])
    sends = Sends(send_sem, recv_sem)
    owns = [
        pltpu.make_async_copy(h_ref, h_out.at[seq], own_sem.at[0]),
        pltpu.make_async_copy(wi_ref.at[seq], wi_out.at[seq, b], own_sem.at[1]),
        pltpu.make_async_copy(wo_ref, wo_out.at[b], own_sem.at[2]),
    ]
    for own in owns:
        own.start()
    me = p.index()
    pairs = ((ints_ref, ints), (small_ref, small))
    for src, dst in pairs:
        dst[me] = src[...]
    first = [sends.start(dst.at[me], dst.at[me], p.at(c=1)) for _, dst in pairs]
    h_z = {r: sends.start(h_ref, h_out.at[seq], p.at(r)) for r in Z_ORDER}
    h_y = [sends.start(h_ref, h_out.at[seq], p.at(y=1))]
    w_s = {}
    for r, y in ((0, 1), (1, 0), (3, 0), (2, 0), (1, 1), (3, 1), (2, 1)):
        to = p.at(r, y)
        w_s[r, y] = sends.start(wi_ref.at[to[0]], wi_out.at[seq, b], to)
    w_x = [sends.start(wi_ref.at[seq], wi_out.at[seq, b], p.at(x=1))]
    w_c = [sends.start(wi_ref.at[seq], wi_out.at[seq, b], p.at(c=1))]
    o_x = sends.start(wo_ref, wo_out.at[b], p.at(x=1))
    w_c.append(sends.start(wo_ref, wo_out.at[b], p.at(c=1)))
    for copy in first:
        copy.wait_recv()
    base = me - c
    second = [sends.start(dst.at[pl.ds(base, 2)], dst.at[pl.ds(base, 2)], p.at(x=1)) for _, dst in pairs]
    for copy in second:
        copy.wait_recv()
    base = me - b
    third = [sends.start(dst.at[pl.ds(base, 4)], dst.at[pl.ds(base, 4)], p.at(y=1)) for _, dst in pairs]
    for copy in third:
        copy.wait_recv()
    base = p.z * 8
    fourth = [
        sends.start(dst.at[pl.ds(base, 8)], dst.at[pl.ds(base, 8)], p.at(r)) for _, dst in pairs for r in Z_ORDER
    ]
    for r in Z_ORDER:
        h_z[r].wait_recv()
        s = p.at(-r % 4)[0]
        h_y.append(sends.start(h_out.at[s], h_out.at[s], p.at(y=1)))
    for r, y in ((0, 1), (1, 0), (3, 0), (2, 0), (1, 1), (3, 1), (2, 1)):
        w_s[r, y].wait_recv()
        s = p.at(-r % 4, y)[0]
        w_x.append(sends.start(wi_out.at[s, b], wi_out.at[s, b], p.at(x=1)))
        w_c.append(sends.start(wi_out.at[s, b], wi_out.at[s, b], p.at(c=1)))
    bx = p.at(x=1)[1]
    o_x.wait_recv()
    w_c.append(sends.start(wo_out.at[bx], wo_out.at[bx], p.at(c=1)))
    places = [(0, 0), (0, 1), (1, 0), (3, 0), (2, 0), (1, 1), (3, 1), (2, 1)]
    for copy, (r, y) in zip(w_x, places):
        copy.wait_recv()
        s = p.at(-r % 4, y)[0]
        w_c.append(sends.start(wi_out.at[s, bx], wi_out.at[s, bx], p.at(c=1)))
    for copy in fourth + h_y + w_c:
        copy.wait_recv()
    ints_out[...] = ints[...]
    small_out[...] = small[...]
    sends.finish()
    for own in owns:
        own.wait()


def gather_first(hidden, w_in, w_out, ints, small, collective_id):
    own = w_in.shape[0]
    parts = jnp.transpose(w_in.reshape(own, 3, 8, -1), (2, 0, 1, 3)).reshape(8, own, -1)
    struct = jax.ShapeDtypeStruct
    outs = call(
        gather_first_kernel,
        "gather_first",
        collective_id,
        (
            struct((8,) + hidden.shape, bf16),
            struct((8, 4) + parts.shape[1:], bf16),
            struct((4,) + w_out.shape, bf16),
            struct((32,) + ints.shape, ints.dtype),
            struct((32,) + small.shape, small.dtype),
        ),
        [ANY, ANY, ANY, WHOLE, WHOLE],
        (ANY, ANY, ANY, WHOLE, WHOLE),
        [pltpu.VMEM((32,) + ints.shape, ints.dtype), pltpu.VMEM((32,) + small.shape, small.dtype)],
        2 + 3 + 1 + 7 + 1 + 1 + 2 + 2 + 2 + 6 + 3 + 14 + 1 + 8,
        3,
    )(hidden, parts, w_out, ints, small)
    return outs


def gather_seq_kernel(h_ref, h_out, send_sem, recv_sem, own_sem):
    p = Place()
    seq, b = p.at()
    barrier([p.at(1), p.at(2), p.at(3), p.at(y=1)])
    sends = Sends(send_sem, recv_sem)
    own = pltpu.make_async_copy(h_ref, h_out.at[seq], own_sem.at[0])
    own.start()
    h_z = {r: sends.start(h_ref, h_out.at[seq], p.at(r)) for r in Z_ORDER}
    h_y = [sends.start(h_ref, h_out.at[seq], p.at(y=1))]
    for r in Z_ORDER:
        h_z[r].wait_recv()
        s = p.at(-r % 4)[0]
        h_y.append(sends.start(h_out.at[s], h_out.at[s], p.at(y=1)))
    for copy in h_y:
        copy.wait_recv()
    sends.finish()
    own.wait()


def gather_seq(x, collective_id):
    return call(
        gather_seq_kernel,
        "gather_seq",
        collective_id,
        jax.ShapeDtypeStruct((8,) + x.shape, x.dtype),
        [ANY],
        ANY,
        [],
        7,
    )(x)


def scatter_seq_kernel(p_ref, out_ref, acc, ry, rz, send_sem, recv_sem, own_sem):
    p = Place()
    barrier([p.at(1), p.at(2), p.at(3), p.at(y=1)])
    sends = Sends(send_sem, recv_sem)
    order = (2, 1, 3, 0)
    loads, fy, fz = [], [], []
    for n, r in enumerate(order):
        fy.append(sends.start(p_ref.at[p.at(r, 1)[0]], ry.at[n], p.at(y=1)))
        load = pltpu.make_async_copy(p_ref.at[p.at(r)[0]], acc.at[n], own_sem.at[n])
        load.start()
        loads.append(load)
    rows = acc.shape[1]
    for n, r in enumerate(order):
        loads[n].wait()
        fy[n].wait_recv()
        add_rows(acc.at[n], ry.at[n], 0, rows)
        if r:
            fz.append(sends.start(acc.at[n], rz.at[n], p.at(r)))
    for copy in fz:
        copy.wait_recv()

    def total(i, _):
        at = pl.ds(pl.multiple_of(i * 16, 16), 16)
        value = acc[3, at].astype(f32)
        for n in range(3):
            value = value + rz[n, at].astype(f32)
        out_ref[at] = value.astype(out_ref.dtype)
        return 0

    lax.fori_loop(0, rows // 16, total, 0)
    sends.finish()


def scatter_seq(parts, collective_id, dtype=bf16):
    block = parts.shape[1:]
    return call(
        scatter_seq_kernel,
        "scatter_seq",
        collective_id,
        jax.ShapeDtypeStruct(block, dtype),
        [ANY],
        WHOLE,
        [pltpu.VMEM((n,) + block, parts.dtype) for n in (4, 4, 3)],
        7,
        4,
    )(parts)


def sum_seq_kernel(x_ref, out_ref, got, send_sem, recv_sem, own_sem):
    p = Place()
    others = [p.at(r, y) for y in (0, 1) for r in range(4) if r or y]
    barrier(others)
    sends = Sends(send_sem, recv_sem)
    me = p.at()[0]
    got[me] = x_ref[...]
    copies = [sends.start(x_ref, got.at[me], to) for to in others]
    for copy in copies:
        copy.wait_recv()
    total = got[0]
    for n in range(1, 8):
        total = total + got[n]
    out_ref[...] = total
    sends.finish()


def sum_seq(x, collective_id):
    return call(
        sum_seq_kernel,
        "sum_seq",
        collective_id,
        jax.ShapeDtypeStruct(x.shape, x.dtype),
        [WHOLE],
        WHOLE,
        [pltpu.VMEM((8,) + x.shape, x.dtype)],
        7,
    )(x)


def scatter_probs_kernel(p_ref, out_ref, sum_x, sum_s, r1, r2, got, send_sem, recv_sem, own_sem):
    p = Place()
    others = [p.at(r, y) for y in (0, 1) for r in range(4) if r or y]
    barrier(others + [p.at(x=1), p.at(c=1)])
    sends = Sends(send_sem, recv_sem)
    first = sends.start(p_ref.at[1 - p.c], r1, p.at(c=1))
    first.wait_recv()
    sum_x[...] = p_ref[p.c] + r1[...]
    second = sends.start(sum_x.at[1 - p.x], r2, p.at(x=1))
    second.wait_recv()
    sum_s[...] = sum_x[p.x] + r2[...]
    copies = []
    for r, y in ((0, 1), (1, 0), (3, 0), (2, 0), (1, 1), (3, 1), (2, 1)):
        to = lax.rem(p.z + r, 4)
        yy = 1 - p.y if y else p.y
        copies.append(sends.start(sum_s.at[yy, to], got.at[p.z, p.y], p.at(r, y)))
    got[p.z, p.y] = sum_s[p.y, p.z]
    for copy in copies:
        copy.wait_recv()
    out_ref[...] = got[...]
    sends.finish()


def scatter_probs(parts, collective_id):
    experts, rows = parts.shape[-2:]
    block = (experts, rows)
    out = call(
        scatter_probs_kernel,
        "scatter_probs",
        collective_id,
        jax.ShapeDtypeStruct((4, 2) + block, f32),
        [WHOLE],
        WHOLE,
        [
            pltpu.VMEM((2, 2, 4) + block, f32),
            pltpu.VMEM((2, 4) + block, f32),
            pltpu.VMEM((2, 2, 4) + block, f32),
            pltpu.VMEM((2, 4) + block, f32),
            pltpu.VMEM((4, 2) + block, f32),
        ],
        9,
    )(parts)
    return out.reshape(8 * experts, rows)


def add_blocks(dst, src):
    def body(i, _):
        dst[i] = (dst[i].astype(f32) + src[i].astype(f32)).astype(dst.dtype)
        return 0

    lax.fori_loop(0, dst.shape[0], body, 0)


def scatter_last_kernel(
    n_ref, wi_ref, wo_ref, sm_ref,
    n_out, wi_out, wo_out, sm_out,
    n_acc, n_y, n_z, wi_acc, wi_c, wi_x, wi_got, wo_acc, wo_c, wo_x, sm_acc, sm_c, sm_x, sm_y, sm_z,
    send_sem, recv_sem, own_sem,
):
    p = Place()
    c, x, y, z = p.c, p.x, p.y, p.z
    others = [p.at(r, yy) for yy in (0, 1) for r in range(4) if r or yy]
    barrier(others + [p.at(x=1), p.at(c=1)])
    sends = Sends(send_sem, recv_sem)
    core, nbr_x, nbr_y = p.at(c=1), p.at(x=1), p.at(y=1)
    order = (2, 1, 3, 0)
    loads = [
        pltpu.make_async_copy(wi_ref.at[c], wi_acc, own_sem.at[4]),
        pltpu.make_async_copy(wo_ref.at[c], wo_acc, own_sem.at[5]),
        pltpu.make_async_copy(sm_ref.at[c], sm_acc, own_sem.at[6]),
    ]
    for load in loads:
        load.start()
    wi1 = sends.start(wi_ref.at[1 - c, 1 - x], wi_c.at[0], core)
    sm1 = sends.start(sm_ref.at[1 - c], sm_c, core)
    wo1 = sends.start(wo_ref.at[1 - c], wo_c, core)
    wi2 = sends.start(wi_ref.at[1 - c, x], wi_c.at[1], core)
    fy, n_loads, fz = [], [], []
    for n, r in enumerate(order):
        fy.append(sends.start(n_ref.at[p.at(r, 1)[0]], n_y.at[n], nbr_y))
        load = pltpu.make_async_copy(n_ref.at[p.at(r)[0]], n_acc.at[n], own_sem.at[n])
        load.start()
        n_loads.append(load)
    for load in loads:
        load.wait()
    wi1.wait_recv()
    add_blocks(wi_acc.at[1 - x], wi_c.at[0])
    wi3 = sends.start(wi_acc.at[1 - x], wi_x, nbr_x)
    sm1.wait_recv()
    sm_acc[...] = sm_acc[...] + sm_c[...]
    sm2 = sends.start(sm_acc.at[1 - x], sm_x, nbr_x)
    wo1.wait_recv()
    add_blocks(wo_acc, wo_c)
    wo2 = sends.start(wo_acc.at[1 - x], wo_x, nbr_x)
    wi2.wait_recv()
    add_blocks(wi_acc.at[x], wi_c.at[1])
    rows = n_acc.shape[1]
    for n, r in enumerate(order):
        n_loads[n].wait()
        fy[n].wait_recv()
        add_rows(n_acc.at[n], n_y.at[n], 0, rows)
        if r:
            fz.append(sends.start(n_acc.at[n], n_z.at[n], p.at(r)))
    wi3.wait_recv()
    add_blocks(wi_acc.at[x], wi_x)
    me = p.at()[0]
    wi4 = []
    for r, yy in ((0, 1), (1, 0), (3, 0), (2, 0), (1, 1), (3, 1), (2, 1)):
        to = p.at(r, yy)
        wi4.append(sends.start(wi_acc.at[x, to[0]], wi_got.at[me], to))
    sm2.wait_recv()
    sm_acc[x] = sm_acc[x] + sm_x[...]
    sm3 = sends.start(sm_acc.at[x, 1 - y], sm_y, nbr_y)
    wi_got[me] = wi_acc[x, me]
    wo2.wait_recv()
    wo_out[...] = wo_acc[x].astype(f32) + wo_x[...].astype(f32)
    sm3.wait_recv()
    sm_acc[x, y] = sm_acc[x, y] + sm_y[...]
    sm4 = [
        sends.start(sm_acc.at[x, y, lax.rem(z + r, 4)], sm_z.at[n], p.at(r)) for n, r in enumerate(Z_ORDER)
    ]
    for copy in wi4:
        copy.wait_recv()
    wi_out[...] = wi_got[...].astype(f32)
    for copy in sm4:
        copy.wait_recv()
    sm_out[...] = sm_acc[x, y, z] + sm_z[0] + sm_z[1] + sm_z[2]
    for copy in fz:
        copy.wait_recv()

    def total(i, _):
        at = pl.ds(pl.multiple_of(i * 16, 16), 16)
        value = n_acc[3, at].astype(f32)
        for n in range(3):
            value = value + n_z[n, at].astype(f32)
        n_out[at] = value
        return 0

    lax.fori_loop(0, rows // 16, total, 0)
    sends.finish()


def scatter_last(normed, w_in, w_out, small, collective_id):
    struct = jax.ShapeDtypeStruct
    nb, ib, ob, sb = normed.shape[1:], w_in.shape[2:], w_out.shape[2:], small.shape[4:]
    V = pltpu.VMEM
    return call(
        scatter_last_kernel,
        "scatter_last",
        collective_id,
        (struct(nb, f32), struct(ib, f32), struct(ob, f32), struct(sb, f32)),
        [ANY] * 4,
        (WHOLE,) * 4,
        [
            V((4,) + nb, bf16), V((4,) + nb, bf16), V((3,) + nb, bf16),
            V((2,) + ib, bf16), V((2,) + ib, bf16), V(ib, bf16), V(ib, bf16),
            V((2,) + ob, bf16), V((2,) + ob, bf16), V(ob, bf16),
            V((2, 2, 4) + sb, f32), V((2, 2, 4) + sb, f32), V((2, 4) + sb, f32), V((4,) + sb, f32), V((3,) + sb, f32),
        ],
        4 + 4 + 3 + 1 + 1 + 1 + 7 + 1 + 3,
        7,
        48,
    )(normed, w_in, w_out, small)


def slots_of_rows(ranks):
    experts, rows = ranks.shape
    slot = lax.broadcasted_iota(jnp.int32, (experts, CAP, rows), 1)
    return ranks[:, None, :] == slot


def one_hot(hot):
    experts, _, rows = hot.shape
    return jnp.where(hot, 1.0, 0.0).reshape(experts * CAP, rows).astype(bf16)


def dispatch_kernel(first_ref, routes_ref, x_ref, g_ref, router_ref, xs_ref, gs_ref, gate_ref, rank_ref, probs):
    experts = rank_ref.shape[1]
    rows = x_ref.shape[1]
    first = pl.multiple_of(first_ref[0], experts)
    routes = routes_ref[0]
    hits = []
    for e in range(experts):
        same = jnp.where(routes == first + e, 1.0, 0.0)
        hits.append(jnp.max(same, axis=0, keepdims=True))
    hit = jnp.concatenate(hits, axis=0)
    before = lax.broadcasted_iota(jnp.int32, (rows, rows), 0) < lax.broadcasted_iota(jnp.int32, (rows, rows), 1)
    rank = jnp.dot(hit.astype(bf16), jnp.where(before, 1.0, 0.0).astype(bf16), preferred_element_type=f32)
    rank = jnp.where(hit > 0.5, rank.astype(jnp.int32), -1)
    rank_ref[0] = rank
    hot = slots_of_rows(rank)
    place = one_hot(hot)
    x = x_ref[0]
    logits = dot(router_ref[...], x, ((1,), (1,)))
    weights = jnp.exp(logits - jnp.max(logits, axis=0, keepdims=True))
    probs[...] = weights / jnp.sum(weights, axis=0, keepdims=True)
    mine = probs[pl.ds(first, experts)]
    gate = jnp.sum(jnp.where(hot, mine[:, None, :], 0.0), axis=-1, keepdims=True)
    gate_ref[...] = jnp.broadcast_to(gate, gate_ref.shape)
    xs_ref[...] = jnp.dot(place, x, preferred_element_type=f32).astype(bf16).reshape(xs_ref.shape)
    gs_ref[...] = jnp.dot(place, g_ref[0], preferred_element_type=f32).astype(bf16).reshape(gs_ref.shape)


def dispatch(first, routes_all, x_all, g_all, router_rows, experts):
    groups, rows, width = x_all.shape
    slots = groups * CAP
    return pl.pallas_call(
        dispatch_kernel,
        name="dispatch",
        grid=(groups,),
        out_shape=(
            jax.ShapeDtypeStruct((experts, slots, width), bf16),
            jax.ShapeDtypeStruct((experts, slots, width), bf16),
            jax.ShapeDtypeStruct((experts, slots, 128), f32),
            jax.ShapeDtypeStruct((groups, experts, rows), jnp.int32),
        ),
        in_specs=[
            pl.BlockSpec(memory_space=pltpu.SMEM),
            pl.BlockSpec((1,) + routes_all.shape[1:], lambda d: (d, 0, 0)),
            pl.BlockSpec((1, rows, width), lambda d: (d, 0, 0)),
            pl.BlockSpec((1, rows, width), lambda d: (d, 0, 0)),
            pl.BlockSpec(router_rows.shape, lambda d: (0, 0)),
        ],
        out_specs=(
            pl.BlockSpec((experts, CAP, width), lambda d: (0, d, 0)),
            pl.BlockSpec((experts, CAP, width), lambda d: (0, d, 0)),
            pl.BlockSpec((experts, CAP, 128), lambda d: (0, d, 0)),
            pl.BlockSpec((1, experts, rows), lambda d: (d, 0, 0)),
        ),
        scratch_shapes=[pltpu.VMEM((router_rows.shape[0], rows), f32)],
        compiler_params=pltpu.CompilerParams(vmem_limit_bytes=40 << 20),
    )(first, routes_all, x_all, g_all, router_rows)


def experts_kernel(w_ref, xs_ref, gs_ref, gate_ref, y_ref, z_ref, wg_ref, gg_ref):
    x, g = xs_ref[0], gs_ref[0]
    gain = gate_ref[0][:, :1]
    gate = jnp.dot(x, w_ref[0, 0], preferred_element_type=f32)
    up = jnp.dot(x, w_ref[0, 1], preferred_element_type=f32)
    raw = jnp.dot(g, w_ref[0, 2], preferred_element_type=f32)
    sigma = 1.0 / (1.0 + jnp.exp(-gate))
    silu = gate * sigma
    act = (silu * up).astype(bf16).astype(f32)
    gg_ref[0] = jnp.broadcast_to(jnp.sum(raw * act, axis=-1, keepdims=True), gg_ref.shape[1:])
    act_gated = (act * gain).astype(bf16)
    act_grad = raw * gain
    gate_low = (act_grad * up * sigma * (1.0 + gate * (1.0 - sigma))).astype(bf16)
    up_low = (act_grad * silu).astype(bf16)
    y_ref[0] = dot(act_gated, w_ref[0, 2], ((1,), (1,))).astype(bf16)
    z = dot(gate_low, w_ref[0, 0], ((1,), (1,))) + dot(up_low, w_ref[0, 1], ((1,), (1,)))
    z_ref[0] = z.astype(bf16)
    first = pl.program_id(1) == 0
    for n, (left, right) in enumerate(((x, gate_low), (x, up_low), (g, act_gated))):
        term = dot(left, right, ((0,), (0,)))

        @pl.when(first)
        def _():
            wg_ref[0, n] = term

        @pl.when(jnp.logical_not(first))
        def _():
            wg_ref[0, n] += term


def experts_all(w_expert, xs, gs, gates, tile=512):
    experts, slots, width = xs.shape
    hidden = w_expert.shape[-1]
    row = pl.BlockSpec((1, tile, width), lambda e, t: (e, t, 0))
    thin = pl.BlockSpec((1, tile, 128), lambda e, t: (e, t, 0))
    weight = pl.BlockSpec((1, 3, width, hidden), lambda e, t: (e, 0, 0, 0))
    return pl.pallas_call(
        experts_kernel,
        name="experts",
        grid=(experts, slots // tile),
        out_shape=(
            jax.ShapeDtypeStruct(xs.shape, bf16),
            jax.ShapeDtypeStruct(xs.shape, bf16),
            jax.ShapeDtypeStruct(w_expert.shape, f32),
            jax.ShapeDtypeStruct((experts, slots, 128), f32),
        ),
        in_specs=[weight, row, row, thin],
        out_specs=(row, row, weight, thin),
        compiler_params=pltpu.CompilerParams(vmem_limit_bytes=60 << 20),
    )(w_expert, xs, gs, gates)


def combine_kernel(rank_ref, y_ref, z_ref, gg_ref, my_ref, mz_ref, pg_ref):
    hot = slots_of_rows(rank_ref[0])
    place = one_hot(hot)
    flat = (place.shape[0], y_ref.shape[-1])
    my_ref[0] = dot(place, y_ref[...].reshape(flat), ((0,), (0,))).astype(bf16)
    mz_ref[0] = dot(place, z_ref[...].reshape(flat), ((0,), (0,))).astype(bf16)
    pg_ref[0] = jnp.sum(jnp.where(hot, gg_ref[:, :, :1], 0.0), axis=1)


def combine(ranks, y, z, gate_grads):
    groups, experts, rows = ranks.shape
    width = y.shape[-1]
    part = pl.BlockSpec((experts, CAP, width), lambda d: (0, d, 0))
    whole = pl.BlockSpec((1, rows, width), lambda d: (d, 0, 0))
    thin = pl.BlockSpec((1, experts, rows), lambda d: (d, 0, 0))
    return pl.pallas_call(
        combine_kernel,
        name="combine",
        grid=(groups,),
        out_shape=(
            jax.ShapeDtypeStruct((groups, rows, width), bf16),
            jax.ShapeDtypeStruct((groups, rows, width), bf16),
            jax.ShapeDtypeStruct((groups, experts, rows), f32),
        ),
        in_specs=[thin, part, part, pl.BlockSpec((experts, CAP, 128), lambda d: (0, d, 0))],
        out_specs=(whole, whole, thin),
        compiler_params=pltpu.CompilerParams(vmem_limit_bytes=40 << 20),
    )(ranks, y, z, gate_grads)


class HeadsAttention:
    def __init__(self, hidden, segments, routes, w_in, w_out, w_router, gains, experts):
        seq, batch = 8, 4
        place, b = lax.axis_index("seq"), lax.axis_index("batch")
        self.rows, self.width = hidden.shape
        width = self.width
        self.hs = width // HEADS
        self.hl = HEADS // seq
        cols = self.hl * self.hs
        self.cols = cols
        top = routes.shape[1]
        total = experts * seq
        ints = jnp.concatenate([routes.T, segments[None], jnp.zeros((7, self.rows), jnp.int32)], axis=0)
        small = jnp.concatenate(
            [w_router, gains.T, jnp.zeros((w_router.shape[0], 128 - total - gains.shape[0]), bf16)], axis=1
        )
        hidden_all, w_cols, w_rows, ints, small = gather_first(hidden, w_in, w_out, ints, small, 0)
        length = seq * self.rows
        self.length = length
        self.w_cols = w_cols.reshape(width, 3 * cols)
        self.w_rows = w_rows.reshape(cols, width)
        small = small.reshape(width, 128)
        self.router_all = small[:, :total]
        self.gains_all = small[:, total : total + 4].T.astype(f32)
        self.routes_all = ints[:, :top]
        segment_all = lax.dynamic_slice_in_dim(ints.reshape(seq, batch, -1, self.rows), b, 1, 1)
        segment_all = segment_all[:, 0, top].reshape(length)
        gains_all = self.gains_all
        inputs = hidden_all.reshape(length, width).astype(f32)
        self.first_normal = inputs * rms_scale(inputs)
        normed = (self.first_normal * gains_all[0]).astype(bf16)
        self.normed = normed
        projected = jnp.dot(normed, self.w_cols, preferred_element_type=f32)
        query_raw = projected[:, :cols]
        key_raw = projected[:, cols : 2 * cols]
        squares = jnp.stack([jnp.sum(query_raw * query_raw, -1), jnp.sum(key_raw * key_raw, -1)], 0)
        scales = lax.rsqrt(self.over_heads(squares, 1) / width + epsilon)
        self.query_scale = scales[0][:, None]
        self.key_scale = scales[1][:, None]
        self.query_normal = query_raw * self.query_scale
        self.key_normal = key_raw * self.key_scale
        mine = lax.dynamic_slice_in_dim(gains_all, place * cols, cols, 1)
        self.query_gain, self.key_gain = mine[1], mine[2]
        positions = jnp.arange(length, dtype=jnp.int32)
        self.cosine, self.sine = rope_tables(positions, self.hs)
        shape = (length, self.hl, self.hs)

        def rot(u):
            u = u.reshape(shape)
            return (u * self.cosine + rotate_half(u) * self.sine).astype(bf16)

        self.query = rot(self.query_normal * self.query_gain)
        self.key = rot(self.key_normal * self.key_gain)
        self.value = projected[:, 2 * cols :].astype(bf16).reshape(shape)
        self.allowed = (positions[None, :] <= positions[:, None]) & (
            segment_all[None, :] == segment_all[:, None]
        )
        scores = self.scores()
        top = jnp.max(scores, axis=-1, keepdims=True)
        weights = jnp.exp(scores - top)
        total = jnp.sum(weights, axis=-1, keepdims=True)
        acc = jnp.einsum("hqk,khd->hqd", weights.astype(bf16), self.value, preferred_element_type=f32)
        self.log_total = top + jnp.log(total)
        self.attended = jnp.transpose(acc / total, (1, 0, 2))
        self.attn_low = self.attended.reshape(length, cols).astype(bf16)
        partial = jnp.dot(self.attn_low, self.w_rows, preferred_element_type=f32).astype(bf16)
        self.mixed = scatter_seq(partial.reshape(seq, self.rows, width), 2, f32)

    def over_heads(self, sums, collective_id):
        return sum_seq(sums.reshape(2, -1, 128), collective_id).reshape(2, self.length)

    def scores(self):
        scale = self.hs ** (-0.5)
        scores = jnp.einsum("qhd,khd->hqk", self.query, self.key, preferred_element_type=f32) * scale
        return jnp.where(self.allowed[None], scores, -jnp.inf)

    def back(self, middle_low, router_grad, ffn_gain_grad):
        seq, batch = 8, 4
        length, cols, width = self.length, self.cols, self.width
        scale = self.hs ** (-0.5)
        shape = (length, self.hl, self.hs)
        grad_all = gather_seq(middle_low, 3).reshape(length, width)
        out_grad = dot(self.attn_low, grad_all, ((0,), (0,))).astype(bf16)
        attn_grad = dot(grad_all, self.w_rows, ((1,), (1,))).astype(bf16).reshape(shape)
        delta = jnp.sum(attn_grad.astype(f32) * self.attended, axis=-1)
        probs = jnp.exp(self.scores() - self.log_total)
        prob_grad = jnp.einsum("qhd,khd->hqk", attn_grad, self.value, preferred_element_type=f32)
        score_grad = (probs * (prob_grad - delta.T[..., None])).astype(bf16)
        query_grad = jnp.einsum("hqk,khd->qhd", score_grad, self.key, preferred_element_type=f32) * scale
        key_grad = jnp.einsum("hqk,qhd->khd", score_grad, self.query, preferred_element_type=f32) * scale
        value_grad = jnp.einsum("hqk,qhd->khd", probs.astype(bf16), attn_grad, preferred_element_type=f32)

        def rot_back(u):
            return (u * self.cosine - rotate_half(u * self.sine)).reshape(length, cols)

        query_norm_grad = rot_back(query_grad)
        key_norm_grad = rot_back(key_grad)
        query_gain_grad = jnp.sum(query_norm_grad * self.query_normal, axis=0)
        key_gain_grad = jnp.sum(key_norm_grad * self.key_normal, axis=0)
        query_scaled = query_norm_grad * self.query_gain
        key_scaled = key_norm_grad * self.key_gain
        dots = jnp.stack(
            [jnp.sum(query_scaled * self.query_normal, -1), jnp.sum(key_scaled * self.key_normal, -1)], 0
        )
        means = self.over_heads(dots, 4) / width
        query_raw_grad = self.query_scale * (query_scaled - self.query_normal * means[0][:, None])
        key_raw_grad = self.key_scale * (key_scaled - self.key_normal * means[1][:, None])
        projected_grad = jnp.concatenate(
            [query_raw_grad, key_raw_grad, value_grad.reshape(length, cols)], axis=1
        ).astype(bf16)
        partial = dot(projected_grad, self.w_cols, ((1,), (1,)))
        attn_gain_grad = jnp.sum(partial * self.first_normal, axis=0)
        in_grad = dot(self.normed, projected_grad, ((0,), (0,))).astype(bf16)
        own = width // (seq * batch)

        def by_batch(value, *shape):
            return jnp.swapaxes(value.reshape(2, 2, *shape), 0, 1)

        in_grad = jnp.transpose(in_grad.reshape(seq, 2, 2, own, 3 * cols), (2, 1, 0, 3, 4))
        out_grad = by_batch(out_grad, own, width)
        mine = jnp.arange(seq)[:, None] == lax.axis_index("seq")

        def own_columns(value):
            return jnp.where(mine, value[None], 0.0).reshape(width)

        gains_grad = jnp.stack(
            [attn_gain_grad, own_columns(query_gain_grad), own_columns(key_gain_grad), ffn_gain_grad], axis=1
        )
        total = router_grad.shape[1]
        small = jnp.concatenate([router_grad, gains_grad, jnp.zeros((width, 128 - total - 4), f32)], axis=1)
        small = jnp.transpose(small.reshape(4, 2, 2, 2, own, 128), (3, 2, 1, 0, 4, 5))
        normed_grad, in_shard, out_shard, small = scatter_last(
            partial.astype(bf16).reshape(seq, self.rows, width), in_grad, out_grad, small, 5
        )
        in_shard = jnp.transpose(in_shard.reshape(seq, own, 3, cols), (1, 2, 0, 3)).reshape(own, 3 * width)
        return normed_grad, in_shard, out_shard, small[:, :total], small[:, total : total + 4].T


def experts_by_tokens(ffn_in, cotangent_all, routes_all, w_expert, router_all):
    experts = w_expert.shape[0]
    rows, width = ffn_in.shape
    first = (lax.axis_index("seq") * experts).astype(jnp.int32).reshape(1)
    ffn_all = gather_all(ffn_in, 6)
    xs, gs, gates, ranks = dispatch(
        first, routes_all, ffn_all, cotangent_all.reshape(32, rows, width), router_all.T, experts
    )
    y, z, expert_grad, gate_grads = experts_all(w_expert, xs, gs, gates)
    mixture, ffn_in_grad, probs = combine(ranks, y, z, gate_grads)
    prob_grad = scatter_probs(jnp.transpose(probs.reshape(4, 2, 2, 2, experts, rows), (3, 2, 1, 0, 4, 5)), 7).T
    ffn_in_grad = scatter_all(ffn_in_grad, 8, f32)
    mixture = scatter_all(mixture, 9, f32)
    return mixture, ffn_in_grad, prob_grad, expert_grad


class TokensAttention:
    def __init__(self, hidden, segment_all, w_in, w_out, gains_all):
        place = lax.axis_index("seq")
        rows, width = hidden.shape
        self.rows, self.width = rows, width
        self.hs = width // HEADS
        self.sources = w_in, w_out
        self.gather_weights(w_in, w_out)
        inputs = hidden.astype(f32)
        self.normed = (inputs * rms_scale(inputs) * gains_all[0]).astype(bf16)
        projected = jnp.dot(self.normed, self.in_all, preferred_element_type=f32)
        query_raw = projected[:, :width]
        key_raw = projected[:, width : 2 * width]
        self.query_scale = rms_scale(query_raw)
        self.query_normal = query_raw * self.query_scale
        self.key_scale = rms_scale(key_raw)
        self.key_normal = key_raw * self.key_scale
        self.query_gain, self.key_gain = gains_all[1], gains_all[2]
        self.positions = place * rows + jnp.arange(rows, dtype=jnp.int32)
        self.cosine, self.sine = rope_tables(self.positions, self.hs)
        shape = (rows, HEADS, self.hs)

        def rot(u):
            u = u.reshape(shape)
            return (u * self.cosine + rotate_half(u) * self.sine).astype(bf16)

        self.query = rot(self.query_normal * self.query_gain)
        key = rot(self.key_normal * self.key_gain).reshape(rows, width)
        value = projected[:, 2 * width :].astype(bf16)
        self.kept = key, value
        self.gather_keys(key, value)
        self.segment_all = segment_all
        self.segment_own = lax.dynamic_slice_in_dim(segment_all, place * rows, rows, 0)
        length = self.key_all.shape[0]
        scores = self.scores(self.key_all.reshape(length, HEADS, self.hs), segment_all, 0)
        top = jnp.max(scores, axis=-1, keepdims=True)
        weights = jnp.exp(scores - top)
        total = jnp.sum(weights, axis=-1, keepdims=True)
        acc = jnp.einsum(
            "hqk,khd->hqd",
            weights.astype(bf16),
            self.value_all.reshape(length, HEADS, self.hs),
            preferred_element_type=f32,
        )
        self.log_total = top + jnp.log(total)
        self.attended = jnp.transpose(acc / total, (1, 0, 2))
        self.attn_low = self.attended.reshape(rows, width).astype(bf16)
        self.mixed = jnp.dot(self.attn_low, self.out_all, preferred_element_type=f32)

    def gather_weights(self, w_in, w_out):
        self.in_all = lax.all_gather(w_in, BOTH, axis=0, tiled=True)
        self.out_all = lax.all_gather(w_out, BOTH, axis=0, tiled=True)

    def gather_keys(self, key, value):
        self.key_all = lax.all_gather(key, "seq", axis=0, tiled=True)
        self.value_all = lax.all_gather(value, "seq", axis=0, tiled=True)

    def scores(self, key, segment, start):
        scale = self.hs ** (-0.5)
        scores = jnp.einsum("qhd,khd->hqk", self.query, key, preferred_element_type=f32) * scale
        key_positions = start + jnp.arange(key.shape[0], dtype=jnp.int32)
        allowed = (key_positions[None, :] <= self.positions[:, None]) & (
            segment[None, :] == self.segment_own[:, None]
        )
        return jnp.where(allowed[None], scores, -jnp.inf)

    def back(self, middle_low, router_grad, ffn_gain_grad):
        again = lax.optimization_barrier((middle_low, *self.sources, *self.kept))
        middle_low = again[0]
        self.gather_weights(*again[1:3])
        self.gather_keys(*again[3:])
        rows, width = self.rows, self.width
        scale = self.hs ** (-0.5)
        out_grad = dot(self.attn_low, middle_low, ((0,), (0,))).astype(bf16)
        out_shard = lax.psum_scatter(out_grad, BOTH, scatter_dimension=0, tiled=True).astype(f32)
        attn_grad = dot(middle_low, self.out_all, ((1,), (1,))).astype(bf16).reshape(rows, HEADS, self.hs)
        delta = jnp.sum(attn_grad.astype(f32) * self.attended, axis=-1).T
        length = self.key_all.shape[0]
        block = min(512, length)
        count = length // block

        def step(query_grad, item):
            key, value, segment, start = item
            probs = jnp.exp(self.scores(key, segment, start) - self.log_total)
            prob_grad = jnp.einsum("qhd,khd->hqk", attn_grad, value, preferred_element_type=f32)
            score_grad = (probs * (prob_grad - delta[..., None])).astype(bf16)
            query_grad = (
                query_grad + jnp.einsum("hqk,khd->qhd", score_grad, key, preferred_element_type=f32) * scale
            )
            key_grad = jnp.einsum("hqk,qhd->khd", score_grad, self.query, preferred_element_type=f32) * scale
            value_grad = jnp.einsum("hqk,qhd->khd", probs.astype(bf16), attn_grad, preferred_element_type=f32)
            return query_grad, jnp.concatenate(
                [key_grad.reshape(block, width), value_grad.reshape(block, width)], axis=1
            ).astype(bf16)

        query_grad, terms = lax.scan(
            step,
            jnp.zeros((rows, HEADS, self.hs), f32),
            (
                self.key_all.reshape(count, block, HEADS, self.hs),
                self.value_all.reshape(count, block, HEADS, self.hs),
                self.segment_all.reshape(count, block),
                jnp.arange(count, dtype=jnp.int32) * block,
            ),
        )
        kv_grad = lax.psum_scatter(
            terms.reshape(length, 2 * width), "seq", scatter_dimension=0, tiled=True
        ).astype(f32)
        key_grad = kv_grad[:, :width].reshape(rows, HEADS, self.hs)

        def rot_back(u):
            return (u * self.cosine - rotate_half(u * self.sine)).reshape(rows, width)

        query_norm_grad = rot_back(query_grad)
        key_norm_grad = rot_back(key_grad)
        query_gain_grad = jnp.sum(query_norm_grad * self.query_normal, axis=0)
        key_gain_grad = jnp.sum(key_norm_grad * self.key_normal, axis=0)
        query_raw_grad = norm_back(query_norm_grad, self.query_normal, self.query_scale, self.query_gain)
        key_raw_grad = norm_back(key_norm_grad, self.key_normal, self.key_scale, self.key_gain)
        projected_grad = jnp.concatenate([query_raw_grad, key_raw_grad, kv_grad[:, width:]], axis=1).astype(bf16)
        in_grad = dot(self.normed, projected_grad, ((0,), (0,))).astype(bf16)
        in_shard = lax.psum_scatter(in_grad, BOTH, scatter_dimension=0, tiled=True).astype(f32)
        normed_grad = dot(projected_grad, self.in_all, ((1,), (1,)))
        pair = lax.psum_scatter(
            jnp.stack([query_gain_grad, key_gain_grad], 1), BOTH, scatter_dimension=0, tiled=True
        )
        return normed_grad, in_shard, out_shard, router_grad, pair


def expert_math(slots, grads, gate_slot, w_expert):
    w_gate, w_up, w_down = w_expert[:, 0], w_expert[:, 1], w_expert[:, 2]
    gate = jnp.einsum("esd,edf->esf", slots, w_gate, preferred_element_type=f32)
    up = jnp.einsum("esd,edf->esf", slots, w_up, preferred_element_type=f32)
    sigma = jax.nn.sigmoid(gate)
    silu = gate * sigma
    act = (silu * up).astype(bf16).astype(f32)
    act_gated = (act * gate_slot).astype(bf16)
    act_raw = jnp.einsum("esd,edf->esf", grads, w_down, preferred_element_type=f32)
    gate_grad = jnp.sum(act_raw * act, axis=-1)
    act_grad = act_raw * gate_slot
    gate_low = (act_grad * up * sigma * (1.0 + gate * (1.0 - sigma))).astype(bf16)
    up_low = (act_grad * silu).astype(bf16)
    slot_grad = (
        jnp.einsum("esf,edf->esd", gate_low, w_gate, preferred_element_type=f32)
        + jnp.einsum("esf,edf->esd", up_low, w_up, preferred_element_type=f32)
    ).astype(bf16)
    result = jnp.einsum("esf,edf->esd", act_gated, w_down, preferred_element_type=f32).astype(bf16)
    expert_grad = jnp.stack(
        [
            jnp.einsum("esd,esf->edf", slots, gate_low, preferred_element_type=f32),
            jnp.einsum("esd,esf->edf", slots, up_low, preferred_element_type=f32),
            jnp.einsum("esd,esf->edf", grads, act_gated, preferred_element_type=f32),
        ],
        axis=1,
    )
    return result, slot_grad, gate_grad, expert_grad


def slot_places(hit):
    count = hit.astype(jnp.int32)
    rank = jnp.where(hit, jnp.cumsum(count, axis=1) - count, -1)
    return rank[:, :, :, None] == jnp.arange(CAP, dtype=jnp.int32)


def experts_by_slots(ffn_in, cotangent, routes, w_expert, router_all):
    seq, batch = lax.axis_size("seq"), lax.axis_size("batch")
    experts = w_expert.shape[0]
    total = experts * seq
    rows, width = ffn_in.shape
    hit = jnp.any(routes[:, :, None] == jnp.arange(total, dtype=jnp.int32), axis=1)[None]
    hot = slot_places(hit)[0]
    place_hot = hot.astype(bf16).reshape(rows, total * CAP)
    router = jax.nn.softmax(jnp.dot(ffn_in, router_all, preferred_element_type=f32), axis=-1)
    gate_slot = jnp.sum(jnp.where(hot, router[:, :, None], 0.0), axis=0).reshape(seq, experts, CAP, 1)

    def there(values):
        values = lax.all_to_all(values, "seq", split_axis=0, concat_axis=0, tiled=True)
        values = lax.all_gather(values, "batch", axis=0, tiled=True)
        values = jnp.transpose(values, (1, 0, 2, 3))
        return values.reshape(experts, batch * seq * CAP, values.shape[-1])

    def back(values):
        values = values.reshape(experts, batch * seq, CAP, values.shape[-1])
        values = jnp.transpose(values, (1, 0, 2, 3))
        values = lax.psum_scatter(values, "batch", scatter_dimension=0, tiled=True)
        values = lax.all_to_all(values, "seq", split_axis=0, concat_axis=0, tiled=True)
        return values.reshape(total * CAP, values.shape[-1])

    def slots_of(tokens):
        slots = dot(place_hot, tokens, ((0,), (0,))).astype(bf16)
        return there(slots.reshape(seq, experts, CAP, width))

    def tokens_of(slots):
        return jnp.dot(place_hot, back(slots), preferred_element_type=f32)

    result, slot_grad, gate_grad, expert_grad = expert_math(
        slots_of(ffn_in), slots_of(cotangent), there(gate_slot), w_expert
    )
    gate_grad = back(gate_grad[..., None]).reshape(1, total, CAP)
    prob_grad = jnp.sum(jnp.where(hot, gate_grad, 0.0), axis=-1)
    return tokens_of(result), tokens_of(slot_grad), prob_grad, expert_grad


def local(hidden, segments, routes, w_in, w_out, w_router, gains, w_expert, cotangent):
    seq = lax.axis_size("seq")
    total_experts = w_expert.shape[0] * seq
    by_heads = seq == 8 and lax.axis_size("batch") == 4

    inputs = hidden[0].astype(f32)
    first_scale = rms_scale(inputs)
    first_normal = inputs * first_scale
    if by_heads:
        cotangent_all = lax.all_gather(cotangent[0], BOTH, axis=0, tiled=True)
        attention = HeadsAttention(
            hidden[0], segments[0], routes[0], w_in, w_out, w_router, gains, w_expert.shape[0]
        )
        gains_all, router_all = attention.gains_all, attention.router_all
    else:
        small = lax.all_gather(jnp.concatenate([w_router, gains.T], axis=1), BOTH, axis=0, tiled=True)
        router_all = small[:, :total_experts]
        gains_all = small[:, total_experts:].T.astype(f32)
        segment_all = lax.all_gather(segments[0], "seq", axis=0, tiled=True)
        attention = TokensAttention(hidden[0], segment_all, w_in, w_out, gains_all)

    middle = inputs + attention.mixed
    second_scale = rms_scale(middle)
    second_normal = middle * second_scale
    ffn_in = (second_normal * gains_all[3]).astype(bf16)
    if by_heads:
        mixture, ffn_in_grad, prob_grad, expert_grad = experts_by_tokens(
            ffn_in, cotangent_all, attention.routes_all, w_expert, router_all
        )
    else:
        mixture, ffn_in_grad, prob_grad, expert_grad = experts_by_slots(
            ffn_in, cotangent[0], routes[0], w_expert, router_all
        )
    output = middle + mixture

    grad_out = cotangent[0].astype(f32)
    router = jax.nn.softmax(jnp.dot(ffn_in, router_all, preferred_element_type=f32), axis=-1)
    logit_grad = router * (prob_grad - jnp.sum(router * prob_grad, axis=-1, keepdims=True))
    logit_low = logit_grad.astype(bf16)
    router_grad = dot(ffn_in, logit_low, ((0,), (0,)))
    ffn_in_grad = ffn_in_grad + dot(logit_low, router_all, ((1,), (1,)))
    ffn_gain_grad = jnp.sum(ffn_in_grad * second_normal, axis=0)
    middle_grad = grad_out + norm_back(ffn_in_grad, second_normal, second_scale, gains_all[3])
    normed_grad, in_shard, out_shard, router_shard, gains_shard = attention.back(
        middle_grad.astype(bf16), router_grad, ffn_gain_grad
    )
    if not by_heads:
        attn_gain_grad = jnp.sum(normed_grad * first_normal, axis=0)
        ends = jnp.stack([attn_gain_grad, ffn_gain_grad], axis=1)
        sums = lax.psum_scatter(
            jnp.concatenate([router_shard, ends], axis=1), BOTH, scatter_dimension=0, tiled=True
        )
        router_shard, ends = sums[:, :total_experts], sums[:, total_experts:]
        gains_shard = jnp.stack([ends[:, 0], gains_shard[:, 0], gains_shard[:, 1], ends[:, 1]], axis=0)
    input_grad = middle_grad + norm_back(normed_grad, first_normal, first_scale, gains_all[0])
    return (
        output.astype(bf16)[None],
        input_grad[None],
        in_shard,
        out_shard,
        router_shard,
        gains_shard,
        expert_grad,
    )


def solution(mesh):
    placed = (
        P("batch", "seq", None),
        P("batch", "seq"),
        P("batch", "seq", None),
        P(BOTH, None),
        P(BOTH, None),
        P(BOTH, None),
        P(None, BOTH),
        P("seq", None, None, "batch"),
        P("batch", "seq", None),
    )
    return jax.shard_map(
        local,
        mesh=mesh,
        in_specs=placed,
        out_specs=(
            P("batch", "seq", None),
            P("batch", "seq", None),
            P(BOTH, None),
            P(BOTH, None),
            P(BOTH, None),
            P(None, BOTH),
            P("seq", None, None, "batch"),
        ),
        check_vma=False,
    )
```

```python
import functools

import jax
import jax.numpy as jnp
from jax import lax
from jax.experimental import pallas as pl
from jax.experimental.pallas import tpu as pltpu
from jax.sharding import PartitionSpec as P

HEADS = 16
CAP = 32
epsilon = 1e-05
BOTH = ("seq", "batch")
f32 = jnp.float32
bf16 = jnp.bfloat16
MESH = pl.DeviceIdType.MESH


def rms_scale(values):
    return lax.rsqrt(jnp.mean(values * values, axis=-1, keepdims=True) + epsilon)


def rotate_half(values):
    half = values.shape[-1] // 2
    return jnp.concatenate([-values[..., half:], values[..., :half]], axis=-1)


def rope_tables(positions, head_size):
    steps = jnp.arange(head_size // 2, dtype=f32)
    freqs = jnp.exp(steps * (-2.0 * jnp.log(10000.0) / head_size))
    angles = positions.astype(f32)[:, None] * freqs[None, :]
    angles = jnp.concatenate([angles, angles], axis=-1)
    return (jnp.cos(angles)[:, None, :], jnp.sin(angles)[:, None, :])


def norm_back(grad_out, normal, scale, gain):
    scaled = grad_out * gain
    return scale * (scaled - normal * jnp.mean(scaled * normal, axis=-1, keepdims=True))


def dot(a, b, dims):
    return lax.dot_general(a, b, (dims, ((), ())), preferred_element_type=f32)


ANY = pl.BlockSpec(memory_space=pl.ANY)
WHOLE = pl.BlockSpec(memory_space=pltpu.VMEM)


class Place:
    def __init__(self):
        s, b = lax.axis_index("seq"), lax.axis_index("batch")
        self.z, self.y = s // 2, lax.rem(s, 2)
        self.x, self.c = b // 2, lax.rem(b, 2)

    def at(self, r=0, y=0, x=0, c=0):
        z = lax.rem(self.z + r, 4)
        yy = 1 - self.y if y else self.y
        xx = 1 - self.x if x else self.x
        cc = 1 - self.c if c else self.c
        return (z * 2 + yy, xx * 2 + cc)

    def index(self, r=0, y=0, x=0, c=0):
        s, b = self.at(r, y, x, c)
        return s * 4 + b


def barrier(peers):
    sem = pltpu.get_barrier_semaphore()
    for peer in peers:
        pl.semaphore_signal(sem, inc=1, device_id=peer, device_id_type=MESH)
    pl.semaphore_wait(sem, len(peers))


class Sends:
    def __init__(self, send_sem, recv_sem):
        self.send_sem, self.recv_sem, self.copies = send_sem, recv_sem, []

    def start(self, src, dst, peer):
        k = len(self.copies)
        copy = pltpu.make_async_remote_copy(
            src_ref=src,
            dst_ref=dst,
            send_sem=self.send_sem.at[k],
            recv_sem=self.recv_sem.at[k],
            device_id=peer,
            device_id_type=MESH,
        )
        copy.start()
        self.copies.append(copy)
        return copy

    def finish(self):
        for copy in self.copies:
            copy.wait_send()


def add_rows(dst, src, start, rows):
    step = 16

    def body(i, _):
        at = pl.ds(pl.multiple_of(start + i * step, step), step)
        dst[at] = (dst[at].astype(f32) + src[at].astype(f32)).astype(dst.dtype)
        return 0

    lax.fori_loop(0, rows // step, body, 0)


def call(kernel, name, collective_id, out_shape, in_specs, out_specs, scratch, copies, local=1, vmem=32):
    return pl.pallas_call(
        kernel,
        name=name,
        out_shape=out_shape,
        in_specs=in_specs,
        out_specs=out_specs,
        scratch_shapes=[
            *scratch,
            pltpu.SemaphoreType.DMA((copies,)),
            pltpu.SemaphoreType.DMA((copies,)),
            pltpu.SemaphoreType.DMA((local,)),
        ],
        compiler_params=pltpu.CompilerParams(
            collective_id=collective_id, has_side_effects=True, vmem_limit_bytes=vmem << 20
        ),
    )


Z_ORDER = (1, 3, 2)


def gather_first_kernel(
    h_ref, wi_ref, wo_ref, ints_ref, small_ref,
    h_out, wi_out, wo_out, ints_out, small_out,
    ints, small, send_sem, recv_sem, own_sem,
):
    p = Place()
    seq, b = p.at()
    x, c = p.x, p.c
    others = [p.at(r, y) for y in (0, 1) for r in range(4) if r or y]
    barrier(others + [p.at(x=1), p.at(c=1)])
    sends = Sends(send_sem, recv_sem)
    owns = [
        pltpu.make_async_copy(h_ref, h_out.at[seq], own_sem.at[0]),
        pltpu.make_async_copy(wi_ref.at[seq], wi_out.at[seq, b], own_sem.at[1]),
        pltpu.make_async_copy(wo_ref, wo_out.at[b], own_sem.at[2]),
    ]
    for own in owns:
        own.start()
    me = p.index()
    pairs = ((ints_ref, ints), (small_ref, small))
    for src, dst in pairs:
        dst[me] = src[...]
    first = [sends.start(dst.at[me], dst.at[me], p.at(c=1)) for _, dst in pairs]
    h_z = {r: sends.start(h_ref, h_out.at[seq], p.at(r)) for r in Z_ORDER}
    h_y = [sends.start(h_ref, h_out.at[seq], p.at(y=1))]
    w_s = {}
    for r, y in ((0, 1), (1, 0), (3, 0), (2, 0), (1, 1), (3, 1), (2, 1)):
        to = p.at(r, y)
        w_s[r, y] = sends.start(wi_ref.at[to[0]], wi_out.at[seq, b], to)
    w_x = [sends.start(wi_ref.at[seq], wi_out.at[seq, b], p.at(x=1))]
    w_c = [sends.start(wi_ref.at[seq], wi_out.at[seq, b], p.at(c=1))]
    o_x = sends.start(wo_ref, wo_out.at[b], p.at(x=1))
    w_c.append(sends.start(wo_ref, wo_out.at[b], p.at(c=1)))
    for copy in first:
        copy.wait_recv()
    base = me - c
    second = [sends.start(dst.at[pl.ds(base, 2)], dst.at[pl.ds(base, 2)], p.at(x=1)) for _, dst in pairs]
    for copy in second:
        copy.wait_recv()
    base = me - b
    third = [sends.start(dst.at[pl.ds(base, 4)], dst.at[pl.ds(base, 4)], p.at(y=1)) for _, dst in pairs]
    for copy in third:
        copy.wait_recv()
    base = p.z * 8
    fourth = [
        sends.start(dst.at[pl.ds(base, 8)], dst.at[pl.ds(base, 8)], p.at(r)) for _, dst in pairs for r in Z_ORDER
    ]
    for r in Z_ORDER:
        h_z[r].wait_recv()
        s = p.at(-r % 4)[0]
        h_y.append(sends.start(h_out.at[s], h_out.at[s], p.at(y=1)))
    for r, y in ((0, 1), (1, 0), (3, 0), (2, 0), (1, 1), (3, 1), (2, 1)):
        w_s[r, y].wait_recv()
        s = p.at(-r % 4, y)[0]
        w_x.append(sends.start(wi_out.at[s, b], wi_out.at[s, b], p.at(x=1)))
        w_c.append(sends.start(wi_out.at[s, b], wi_out.at[s, b], p.at(c=1)))
    bx = p.at(x=1)[1]
    o_x.wait_recv()
    w_c.append(sends.start(wo_out.at[bx], wo_out.at[bx], p.at(c=1)))
    places = [(0, 0), (0, 1), (1, 0), (3, 0), (2, 0), (1, 1), (3, 1), (2, 1)]
    for copy, (r, y) in zip(w_x, places):
        copy.wait_recv()
        s = p.at(-r % 4, y)[0]
        w_c.append(sends.start(wi_out.at[s, bx], wi_out.at[s, bx], p.at(c=1)))
    for copy in fourth + h_y + w_c:
        copy.wait_recv()
    ints_out[...] = ints[...]
    small_out[...] = small[...]
    sends.finish()
    for own in owns:
        own.wait()


def gather_first(hidden, w_in, w_out, ints, small, collective_id):
    own = w_in.shape[0]
    parts = jnp.transpose(w_in.reshape(own, 3, 8, -1), (2, 0, 1, 3)).reshape(8, own, -1)
    struct = jax.ShapeDtypeStruct
    outs = call(
        gather_first_kernel,
        "gather_first",
        collective_id,
        (
            struct((8,) + hidden.shape, bf16),
            struct((8, 4) + parts.shape[1:], bf16),
            struct((4,) + w_out.shape, bf16),
            struct((32,) + ints.shape, ints.dtype),
            struct((32,) + small.shape, small.dtype),
        ),
        [ANY, ANY, ANY, WHOLE, WHOLE],
        (ANY, ANY, ANY, WHOLE, WHOLE),
        [pltpu.VMEM((32,) + ints.shape, ints.dtype), pltpu.VMEM((32,) + small.shape, small.dtype)],
        2 + 3 + 1 + 7 + 1 + 1 + 2 + 2 + 2 + 6 + 3 + 14 + 1 + 8,
        3,
    )(hidden, parts, w_out, ints, small)
    return outs


def gather_seq_kernel(h_ref, h_out, send_sem, recv_sem, own_sem):
    p = Place()
    seq, b = p.at()
    barrier([p.at(1), p.at(2), p.at(3), p.at(y=1)])
    sends = Sends(send_sem, recv_sem)
    own = pltpu.make_async_copy(h_ref, h_out.at[seq], own_sem.at[0])
    own.start()
    h_z = {r: sends.start(h_ref, h_out.at[seq], p.at(r)) for r in Z_ORDER}
    h_y = [sends.start(h_ref, h_out.at[seq], p.at(y=1))]
    for r in Z_ORDER:
        h_z[r].wait_recv()
        s = p.at(-r % 4)[0]
        h_y.append(sends.start(h_out.at[s], h_out.at[s], p.at(y=1)))
    for copy in h_y:
        copy.wait_recv()
    sends.finish()
    own.wait()


def gather_seq(x, collective_id):
    return call(
        gather_seq_kernel,
        "gather_seq",
        collective_id,
        jax.ShapeDtypeStruct((8,) + x.shape, x.dtype),
        [ANY],
        ANY,
        [],
        7,
    )(x)


def scatter_seq_kernel(p_ref, out_ref, acc, ry, rz, send_sem, recv_sem, own_sem):
    p = Place()
    barrier([p.at(1), p.at(2), p.at(3), p.at(y=1)])
    sends = Sends(send_sem, recv_sem)
    order = (2, 1, 3, 0)
    loads, fy, fz = [], [], []
    for n, r in enumerate(order):
        fy.append(sends.start(p_ref.at[p.at(r, 1)[0]], ry.at[n], p.at(y=1)))
        load = pltpu.make_async_copy(p_ref.at[p.at(r)[0]], acc.at[n], own_sem.at[n])
        load.start()
        loads.append(load)
    rows = acc.shape[1]
    for n, r in enumerate(order):
        loads[n].wait()
        fy[n].wait_recv()
        add_rows(acc.at[n], ry.at[n], 0, rows)
        if r:
            fz.append(sends.start(acc.at[n], rz.at[n], p.at(r)))
    for copy in fz:
        copy.wait_recv()

    def total(i, _):
        at = pl.ds(pl.multiple_of(i * 16, 16), 16)
        value = acc[3, at].astype(f32)
        for n in range(3):
            value = value + rz[n, at].astype(f32)
        out_ref[at] = value.astype(out_ref.dtype)
        return 0

    lax.fori_loop(0, rows // 16, total, 0)
    sends.finish()


def scatter_seq(parts, collective_id, dtype=bf16):
    block = parts.shape[1:]
    return call(
        scatter_seq_kernel,
        "scatter_seq",
        collective_id,
        jax.ShapeDtypeStruct(block, dtype),
        [ANY],
        WHOLE,
        [pltpu.VMEM((n,) + block, parts.dtype) for n in (4, 4, 3)],
        7,
        4,
    )(parts)


def sum_seq_kernel(x_ref, out_ref, got, send_sem, recv_sem, own_sem):
    p = Place()
    others = [p.at(r, y) for y in (0, 1) for r in range(4) if r or y]
    barrier(others)
    sends = Sends(send_sem, recv_sem)
    me = p.at()[0]
    got[me] = x_ref[...]
    copies = [sends.start(x_ref, got.at[me], to) for to in others]
    for copy in copies:
        copy.wait_recv()
    total = got[0]
    for n in range(1, 8):
        total = total + got[n]
    out_ref[...] = total
    sends.finish()


def sum_seq(x, collective_id):
    return call(
        sum_seq_kernel,
        "sum_seq",
        collective_id,
        jax.ShapeDtypeStruct(x.shape, x.dtype),
        [WHOLE],
        WHOLE,
        [pltpu.VMEM((8,) + x.shape, x.dtype)],
        7,
    )(x)


def add_blocks(dst, src):
    def body(i, _):
        dst[i] = (dst[i].astype(f32) + src[i].astype(f32)).astype(dst.dtype)
        return 0

    lax.fori_loop(0, dst.shape[0], body, 0)


def scatter_last_kernel(
    n_ref, wi_ref, wo_ref, sm_ref,
    n_out, wi_out, wo_out, sm_out,
    n_acc, n_y, n_z, wi_acc, wi_c, wi_x, wi_got, wo_acc, wo_c, wo_x, sm_acc, sm_c, sm_x, sm_y, sm_z,
    send_sem, recv_sem, own_sem,
):
    p = Place()
    c, x, y, z = p.c, p.x, p.y, p.z
    others = [p.at(r, yy) for yy in (0, 1) for r in range(4) if r or yy]
    barrier(others + [p.at(x=1), p.at(c=1)])
    sends = Sends(send_sem, recv_sem)
    core, nbr_x, nbr_y = p.at(c=1), p.at(x=1), p.at(y=1)
    order = (2, 1, 3, 0)
    loads = [
        pltpu.make_async_copy(wi_ref.at[c], wi_acc, own_sem.at[4]),
        pltpu.make_async_copy(wo_ref.at[c], wo_acc, own_sem.at[5]),
        pltpu.make_async_copy(sm_ref.at[c], sm_acc, own_sem.at[6]),
    ]
    for load in loads:
        load.start()
    wi1 = sends.start(wi_ref.at[1 - c, 1 - x], wi_c.at[0], core)
    sm1 = sends.start(sm_ref.at[1 - c], sm_c, core)
    wo1 = sends.start(wo_ref.at[1 - c], wo_c, core)
    wi2 = sends.start(wi_ref.at[1 - c, x], wi_c.at[1], core)
    fy, n_loads, fz = [], [], []
    for n, r in enumerate(order):
        fy.append(sends.start(n_ref.at[p.at(r, 1)[0]], n_y.at[n], nbr_y))
        load = pltpu.make_async_copy(n_ref.at[p.at(r)[0]], n_acc.at[n], own_sem.at[n])
        load.start()
        n_loads.append(load)
    for load in loads:
        load.wait()
    wi1.wait_recv()
    add_blocks(wi_acc.at[1 - x], wi_c.at[0])
    wi3 = sends.start(wi_acc.at[1 - x], wi_x, nbr_x)
    sm1.wait_recv()
    sm_acc[...] = sm_acc[...] + sm_c[...]
    sm2 = sends.start(sm_acc.at[1 - x], sm_x, nbr_x)
    wo1.wait_recv()
    add_blocks(wo_acc, wo_c)
    wo2 = sends.start(wo_acc.at[1 - x], wo_x, nbr_x)
    wi2.wait_recv()
    add_blocks(wi_acc.at[x], wi_c.at[1])
    rows = n_acc.shape[1]
    for n, r in enumerate(order):
        n_loads[n].wait()
        fy[n].wait_recv()
        add_rows(n_acc.at[n], n_y.at[n], 0, rows)
        if r:
            fz.append(sends.start(n_acc.at[n], n_z.at[n], p.at(r)))
    wi3.wait_recv()
    add_blocks(wi_acc.at[x], wi_x)
    me = p.at()[0]
    wi4 = []
    for r, yy in ((0, 1), (1, 0), (3, 0), (2, 0), (1, 1), (3, 1), (2, 1)):
        to = p.at(r, yy)
        wi4.append(sends.start(wi_acc.at[x, to[0]], wi_got.at[me], to))
    sm2.wait_recv()
    sm_acc[x] = sm_acc[x] + sm_x[...]
    sm3 = sends.start(sm_acc.at[x, 1 - y], sm_y, nbr_y)
    wi_got[me] = wi_acc[x, me]
    wo2.wait_recv()
    wo_out[...] = wo_acc[x].astype(f32) + wo_x[...].astype(f32)
    sm3.wait_recv()
    sm_acc[x, y] = sm_acc[x, y] + sm_y[...]
    sm4 = [
        sends.start(sm_acc.at[x, y, lax.rem(z + r, 4)], sm_z.at[n], p.at(r)) for n, r in enumerate(Z_ORDER)
    ]
    for copy in wi4:
        copy.wait_recv()
    wi_out[...] = wi_got[...].astype(f32)
    for copy in sm4:
        copy.wait_recv()
    sm_out[...] = sm_acc[x, y, z] + sm_z[0] + sm_z[1] + sm_z[2]
    for copy in fz:
        copy.wait_recv()

    def total(i, _):
        at = pl.ds(pl.multiple_of(i * 16, 16), 16)
        value = n_acc[3, at].astype(f32)
        for n in range(3):
            value = value + n_z[n, at].astype(f32)
        n_out[at] = value
        return 0

    lax.fori_loop(0, rows // 16, total, 0)
    sends.finish()


def scatter_last(normed, w_in, w_out, small, collective_id):
    struct = jax.ShapeDtypeStruct
    nb, ib, ob, sb = normed.shape[1:], w_in.shape[2:], w_out.shape[2:], small.shape[4:]
    V = pltpu.VMEM
    return call(
        scatter_last_kernel,
        "scatter_last",
        collective_id,
        (struct(nb, f32), struct(ib, f32), struct(ob, f32), struct(sb, f32)),
        [ANY] * 4,
        (WHOLE,) * 4,
        [
            V((4,) + nb, bf16), V((4,) + nb, bf16), V((3,) + nb, bf16),
            V((2,) + ib, bf16), V((2,) + ib, bf16), V(ib, bf16), V(ib, bf16),
            V((2,) + ob, bf16), V((2,) + ob, bf16), V(ob, bf16),
            V((2, 2, 4) + sb, f32), V((2, 2, 4) + sb, f32), V((2, 4) + sb, f32), V((4,) + sb, f32), V((3,) + sb, f32),
        ],
        4 + 4 + 3 + 1 + 1 + 1 + 7 + 1 + 3,
        7,
        48,
    )(normed, w_in, w_out, small)


def slots_of_rows(ranks):
    experts, rows = ranks.shape
    slot = lax.broadcasted_iota(jnp.int32, (experts, CAP, rows), 1)
    return ranks[:, None, :] == slot


def one_hot(hot):
    experts, _, rows = hot.shape
    return jnp.where(hot, 1.0, 0.0).reshape(experts * CAP, rows).astype(bf16)


BACK = (1, 3, 2, 0)


class Flip(Place):
    def block(self, r=0, y=0, x=0, c=0):
        z = lax.rem(self.z + 4 - r, 4)
        yy, xx, cc = lax.rem(self.y + y, 2), lax.rem(self.x + x, 2), lax.rem(self.c + c, 2)
        return ((z * 2 + yy) * 2 + xx) * 2 + cc


def remote(src, dst, send, recv, peer):
    return pltpu.make_async_remote_copy(
        src_ref=src, dst_ref=dst, send_sem=send, recv_sem=recv, device_id=peer, device_id_type=MESH
    )


class Gather:
    @staticmethod
    def scratch():
        S = pltpu.SemaphoreType.DMA
        return [S((35,)), S((35,)), S]

    def __init__(self, p, x_ref, x_all, refs):
        send, recv, own_sem = refs
        rows = x_ref.shape[0]
        A, B = pl.ds(0, rows // 2), pl.ds(rows // 2, rows // 2)
        nx, ny, core = p.at(x=1), p.at(y=1), p.at(c=1)
        self.peers = [p.at(1), p.at(2), p.at(3), nx, ny, core]
        mine = p.block()
        self.own = pltpu.make_async_copy(x_ref, x_all.at[mine], own_sem)
        count = [0]

        def copy(src, dst, peer):
            i = count[0]
            count[0] += 1
            return remote(src, dst, send.at[i], recv.at[i], peer)

        self.along, self.to_x, self.to_y, self.to_core, self.by_y, self.by_x = [], [], [], [], [], []
        for k, r in enumerate(BACK):
            at, ix, iy, far = p.block(r), p.block(r, x=1), p.block(r, y=1), p.block(r, y=1, x=1)
            src = x_all.at[at]
            if r:
                self.along.append(copy(x_ref, x_all.at[mine], p.at(r)))
            else:
                src = x_ref
            self.to_x.append(copy(src, x_all.at[at], nx))
            self.to_y.append(copy(src, x_all.at[at], ny))
            self.by_y.append(copy(x_all.at[ix, A], x_all.at[ix, A], ny))
            self.by_x.append(copy(x_all.at[iy, B], x_all.at[iy, B], nx))
            self.to_core.append(
                [copy(src, x_all.at[at], core)]
                + [copy(x_all.at[i], x_all.at[i], core) for i in (ix, iy, far)]
            )

    def start(self):
        self.own.start()
        for copy in self.along:
            copy.start()
        self.own.wait()

    def spread(self, k):
        if BACK[k]:
            self.along[k].wait_recv()
        self.to_x[k].start()
        self.to_y[k].start()
        self.to_core[k][0].start()

    def cross(self, k):
        self.to_x[k].wait_recv()
        self.by_y[k].start()
        self.to_core[k][1].start()
        self.to_y[k].wait_recv()
        self.by_x[k].start()
        self.to_core[k][2].start()

    def close(self, k):
        self.by_y[k].wait_recv()
        self.by_x[k].wait_recv()
        self.to_core[k][3].start()

    def finish(self):
        for copy in self.along:
            copy.wait_send()
        for k in range(4):
            for copy in [self.to_x[k], self.to_y[k], self.by_y[k], self.by_x[k]] + self.to_core[k]:
                copy.wait_send()


class Scatter:
    @staticmethod
    def scratch(rows, width):
        V, S = pltpu.VMEM, pltpu.SemaphoreType.DMA
        block, half = (rows, width), (rows // 2, width)
        return [
            V((2, 4) + block, bf16), V((2, 2, 3) + block, bf16), V((2, 4) + block, bf16), V((2, 2) + half, bf16),
            V((2, 2) + block, bf16), V((4, 2) + block, bf16), V((3, 2) + block, bf16),
            S((32,)), S((32,)), S((38,)), S((38,)), pltpu.SemaphoreType.REGULAR((5,)),
        ]

    def __init__(self, p, refs):
        self.give, self.stage, self.pair, self.half, self.near, self.acc, self.far = refs[:7]
        self.core_send, self.core_recv, send, recv, self.free = refs[7:]
        self.p = p
        rows = self.give.shape[2]
        self.parts = A, B = pl.ds(0, rows // 2), pl.ds(rows // 2, rows // 2)
        nx, ny = p.at(x=1), p.at(y=1)
        self.core, self.nx, self.ny = p.at(c=1), nx, ny
        count = [0]

        def copy(src, dst, peer):
            i = count[0]
            count[0] += 1
            return remote(src, dst, send.at[i], recv.at[i], peer)

        self.by_y, self.by_x, self.to_x, self.to_y, self.to_z = [], [], [], [], []
        for k in range(4):
            out = [self.stage.at[k % 2, i] for i in (0, 1)]
            self.by_y.append([copy(out[i].at[2, A], self.half.at[i, 0], ny) for i in (0, 1)])
            self.by_x.append([copy(out[i].at[2, B], self.half.at[i, 1], nx) for i in (0, 1)])
            self.to_x.append([copy(out[i].at[0], self.near.at[i, 0], nx) for i in (0, 1)])
            self.to_y.append([copy(out[i].at[1], self.near.at[i, 1], ny) for i in (0, 1)])
            if BACK[k]:
                to = p.at((4 - BACK[k]) % 4)
                self.to_z.append([copy(self.acc.at[k, i], self.far.at[k, i], to) for i in (0, 1)])

    def to_core(self, k, i, pos):
        at = k * 8 + i * 4 + pos
        return remote(
            self.give.at[i, pos], self.pair.at[i, pos], self.core_send.at[at], self.core_recv.at[at], self.core
        )

    def add(self, dst, terms):
        step = 32

        def body(i, _):
            at = pl.ds(pl.multiple_of(i * step, step), step)
            if len(terms) == 2 and dst.dtype == bf16:
                dst[at] = terms[0][at] + terms[1][at]
                return 0
            value = terms[0][at].astype(f32)
            for term in terms[1:]:
                value = value + term[at].astype(f32)
            dst[at] = value.astype(dst.dtype)
            return 0

        lax.fori_loop(0, dst.shape[0] // step, body, 0)

    def signal(self, n, peer):
        pl.semaphore_signal(self.free.at[n], inc=1, device_id=peer, device_id_type=MESH)

    def diagonal(self, k, i):
        if k and not i:
            pl.semaphore_wait(self.free.at[1], 1)
            pl.semaphore_wait(self.free.at[2], 1)
        self.to_core(k, i, 3).wait_recv()
        at = self.stage.at[k % 2, i, 2]
        self.add(at, [at, self.pair.at[i, 3]])
        self.by_y[k][i].start()
        self.by_x[k][i].start()

    def across(self, k, i):
        A, B = self.parts
        for_x, for_y = self.stage.at[k % 2, i, 0], self.stage.at[k % 2, i, 1]
        if k and not i:
            pl.semaphore_wait(self.free.at[3], 1)
            pl.semaphore_wait(self.free.at[4], 1)
        self.to_core(k, i, 1).wait_recv()
        self.add(for_x.at[B], [for_x.at[B], self.pair.at[i, 1, B]])
        self.by_y[k][i].wait_recv()
        self.add(for_x.at[A], [for_x.at[A], self.pair.at[i, 1, A], self.half.at[i, 0]])
        self.to_x[k][i].start()
        self.to_core(k, i, 2).wait_recv()
        self.add(for_y.at[A], [for_y.at[A], self.pair.at[i, 2, A]])
        self.by_x[k][i].wait_recv()
        self.add(for_y.at[B], [for_y.at[B], self.pair.at[i, 2, B], self.half.at[i, 1]])
        self.to_y[k][i].start()
        self.to_core(k, i, 0).wait_recv()
        self.add(self.acc.at[k, i], [self.acc.at[k, i], self.pair.at[i, 0]])
        if k < 3 and i:
            self.signal(0, self.core)
            self.signal(1, self.nx)
            self.signal(2, self.ny)

    def line(self, k, i):
        self.to_x[k][i].wait_recv()
        self.to_y[k][i].wait_recv()
        self.add(self.acc.at[k, i], [self.acc.at[k, i], self.near.at[i, 0], self.near.at[i, 1]])
        if BACK[k]:
            self.to_z[k][i].start()
        if k < 3 and i:
            self.signal(3, self.nx)
            self.signal(4, self.ny)

    def settle_core(self, k):
        for i in (0, 1):
            for pos in range(4):
                self.to_core(k, i, pos).wait_send()

    def settle(self, k):
        for i in (0, 1):
            for copies in (self.by_y, self.by_x, self.to_x, self.to_y):
                copies[k][i].wait_send()

    def finish(self, i, out_ref):
        for copies in self.to_z:
            copies[i].wait_recv()
        self.add(out_ref, [self.acc.at[3, i]] + [self.far.at[n, i] for n in range(3)])

    def end(self):
        self.settle_core(3)
        self.settle(2)
        self.settle(3)
        for copies in self.to_z:
            for copy in copies:
                copy.wait_send()


class Probs:
    TURNS = ((0, 1), (1, 0), (3, 0), (2, 0), (1, 1), (3, 1), (2, 1))

    @staticmethod
    def scratch(block):
        V, S = pltpu.VMEM, pltpu.SemaphoreType.DMA
        return [
            V((2, 2, 2, 4) + block, f32), V((2, 2, 4) + block, f32), V((2, 4) + block, f32), V((2, 2, 4) + block, f32),
            V((2, 4) + block, f32), V((4, 2) + block, f32), S((9,)), S((9,)),
        ]

    def __init__(self, p, refs):
        self.p = p
        self.own, self.sum_x, self.sum_s, self.r1, self.r2, self.got, send, recv = refs
        self.peers = [p.at(r, y) for r, y in self.TURNS]
        self.first = remote(self.own.at[1 - p.c], self.r1, send.at[0], recv.at[0], p.at(c=1))
        self.second = remote(self.sum_x.at[1 - p.x], self.r2, send.at[1], recv.at[1], p.at(x=1))
        self.third = []
        for n, (r, y) in enumerate(self.TURNS):
            to = lax.rem(p.z + r, 4)
            yy = 1 - p.y if y else p.y
            self.third.append(
                remote(self.sum_s.at[yy, to], self.got.at[p.z, p.y], send.at[2 + n], recv.at[2 + n], p.at(r, y))
            )

    def start(self):
        self.first.start()

    def over_x(self):
        self.first.wait_recv()
        self.sum_x[...] = self.own[self.p.c] + self.r1[...]
        self.second.start()

    def over_seq(self):
        p = self.p
        self.second.wait_recv()
        self.sum_s[...] = self.sum_x[p.x] + self.r2[...]
        for copy in self.third:
            copy.start()
        self.got[p.z, p.y] = self.sum_s[p.y, p.z]

    def finish(self, out_ref):
        for copy in self.third:
            copy.wait_recv()
        out_ref[...] = self.got[...]
        for copy in [self.first, self.second] + self.third:
            copy.wait_send()


GATHER, SCATTER, PROBS = 3, 12, 8


def mixture_kernel(
    routes_ref, router_ref, x_ref, g_ref, w_ref,
    x_all, xs_out, gs_out, st_ref, grad_out, sum_out, probs_out,
    tx, tg, xs, gs, gates, grads, ranks, weights, load_sem, save_sem, *rest,
):
    p = Flip()
    chunk, e = pl.program_id(0), pl.program_id(1)
    experts, slots, width = xs.shape
    rows = tx.shape[1]
    gather = Gather(p, x_ref, x_all, rest[:GATHER])
    scatter = Scatter(p, rest[GATHER : GATHER + SCATTER])
    probs = Probs(p, rest[GATHER + SCATTER :])
    last = experts - 1

    def at_step(k, step, *events):
        def run():
            for event, *args in events:
                event(*args)

        pl.when((chunk == k) & (e == step))(run)

    def begin():
        barrier(gather.peers + [peer for peer, (r, y) in zip(probs.peers, probs.TURNS) if r and y])
        gather.start()
        gather.spread(3)
        gather.spread(0)
        gather.spread(1)
        gather.cross(0)
        gather.spread(2)
        gather.close(0)

    at_step(0, 0, (begin,))
    at_step(0, 1, (gather.cross, 1))
    at_step(0, 4, (gather.close, 1), (gather.cross, 2))
    at_step(0, 6, (gather.close, 2), (gather.cross, 3))
    at_step(1, 1, (gather.close, 3))
    for k in range(3):
        before = [(scatter.line, k - 1, 1)] if k else []
        at_step(k + 1, 0, *before, (scatter.diagonal, k, 0), (scatter.diagonal, k, 1))
        at_step(k + 1, 1, (scatter.across, k, 0))
        at_step(k + 1, 2, (scatter.across, k, 1))
        at_step(k + 1, 6, (scatter.line, k, 0))

    back = jnp.where(chunk == 0, BACK[0], jnp.where(chunk == 1, BACK[1], jnp.where(chunk == 2, BACK[2], BACK[3])))
    first = p.at()[0] * experts

    def save(k, i):
        src, dst = ((xs, xs_out), (gs, gs_out))[i]
        return pltpu.make_async_copy(src.at[k], dst.at[chunk, k], save_sem.at[i, k])

    def place_rows(j):
        y, x, c = j // 4, (j // 2) % 2, j % 2
        routes = routes_ref[p.block(back, y, x, c)]
        hits = []
        for k in range(experts):
            same = jnp.where(routes == first + k, 1.0, 0.0)
            hits.append(jnp.max(same, axis=0, keepdims=True))
        hit = jnp.concatenate(hits, axis=0)
        before = lax.broadcasted_iota(jnp.int32, (rows, rows), 0) < lax.broadcasted_iota(
            jnp.int32, (rows, rows), 1
        )
        rank = jnp.dot(hit.astype(bf16), jnp.where(before, 1.0, 0.0).astype(bf16), preferred_element_type=f32)
        rank = jnp.where(hit > 0.5, rank.astype(jnp.int32), -1)
        ranks[j] = rank
        hot = slots_of_rows(rank)
        place = one_hot(hot)
        b = j % 2
        rows_x = tx[b]
        logits = dot(router_ref[...], rows_x, ((1,), (1,)))
        powers = jnp.exp(logits - jnp.max(logits, axis=0, keepdims=True))
        weights[...] = powers / jnp.sum(powers, axis=0, keepdims=True)
        chosen = weights[pl.ds(pl.multiple_of(first, experts), experts)]
        gate = jnp.sum(jnp.where(hot, chosen[:, None, :], 0.0), axis=-1, keepdims=True)
        at = pl.ds(j * CAP, CAP)
        gates[:, at] = jnp.broadcast_to(gate, (experts, CAP, 128))
        shape = (experts, CAP, width)
        xs[:, at] = jnp.dot(place, rows_x, preferred_element_type=f32).astype(bf16).reshape(shape)
        gs[:, at] = jnp.dot(place, tg[b], preferred_element_type=f32).astype(bf16).reshape(shape)

    @pl.when(e == 0)
    def _():
        def loads(j):
            at = p.block(back, j // 4, (j // 2) % 2, j % 2)
            b = j % 2
            return (
                pltpu.make_async_copy(x_all.at[at], tx.at[b], load_sem.at[b]),
                pltpu.make_async_copy(g_ref.at[at], tg.at[b], load_sem.at[2 + b]),
            )

        def arrive(j):
            if j % 2:
                for k in range(4):
                    pl.when(chunk == k)(gather.to_core[k][j // 2].wait_recv)

        arrive(0)
        for copy in loads(0):
            copy.start()
        for j in range(8):
            if j < 7:
                arrive(j + 1)
                for copy in loads(j + 1):
                    copy.start()
            for copy in loads(j):
                copy.wait()
            place_rows(j)
        for k in range(experts):
            save(k, 0).start()
            save(k, 1).start()

    rows_x, rows_g = xs[e], gs[e]
    gain = gates[e][:, :1]
    gate = jnp.dot(rows_x, w_ref[0, 0], preferred_element_type=f32)
    up = jnp.dot(rows_x, w_ref[0, 1], preferred_element_type=f32)
    raw = jnp.dot(rows_g, w_ref[0, 2], preferred_element_type=f32)
    sigma = 1.0 / (1.0 + jnp.exp(-gate))
    silu = gate * sigma
    act = (silu * up).astype(bf16).astype(f32)
    grads[e] = jnp.broadcast_to(jnp.sum(raw * act, axis=-1, keepdims=True), (slots, 128))
    act_gated = (act * gain).astype(bf16)
    act_grad = raw * gain
    gate_low = (act_grad * up * sigma * (1.0 + gate * (1.0 - sigma))).astype(bf16)
    up_low = (act_grad * silu).astype(bf16)
    st_ref[0, 0, 0] = act_gated
    st_ref[0, 0, 1] = gate_low
    st_ref[0, 0, 2] = up_low
    save(e, 0).wait()
    save(e, 1).wait()
    z = dot(gate_low, w_ref[0, 0], ((1,), (1,))) + dot(up_low, w_ref[0, 1], ((1,), (1,)))
    xs[e] = z.astype(bf16)
    gs[e] = dot(act_gated, w_ref[0, 2], ((1,), (1,))).astype(bf16)

    for k in range(3):
        at_step(k + 1, last, (scatter.settle_core, k), *([(scatter.settle, k - 1)] if k else []))

    @pl.when(e == last)
    def _():
        @pl.when(chunk > 0)
        def _():
            pl.semaphore_wait(scatter.free.at[0], 1)

        for pos in (3, 1, 2, 0):
            for c in (1, 0):
                j = pos * 2 + c
                hot = slots_of_rows(ranks[j])
                place = one_hot(hot)
                at = pl.ds(j * CAP, CAP)
                for i, values in enumerate((xs, gs)):
                    flat = values[:, at].reshape(experts * CAP, width)
                    total = dot(place, flat, ((0,), (0,))).astype(bf16)
                    if c:
                        scatter.give[i, pos] = total
                        scatter.to_core(chunk, i, pos).start()
                    elif pos:
                        scatter.stage[lax.rem(chunk, 2), i, pos - 1] = total
                    else:
                        scatter.acc[chunk, i] = total
                zz = lax.rem(p.z + 4 - back, 4)
                yy, xx, cc = lax.rem(p.y + pos // 2, 2), lax.rem(p.x + pos % 2, 2), lax.rem(p.c + c, 2)
                probs.own[cc, xx, yy, zz] = jnp.sum(jnp.where(hot, grads[:, at, :1], 0.0), axis=1)

    @pl.when((chunk == 3) & (e == last))
    def _():
        probs.start()
        scatter.line(2, 1)
        scatter.diagonal(3, 0)
        scatter.diagonal(3, 1)
        probs.over_x()
        scatter.across(3, 0)
        scatter.across(3, 1)
        probs.over_seq()
        gather.finish()
        scatter.line(3, 0)
        scatter.finish(0, grad_out)
        probs.finish(probs_out)
        scatter.line(3, 1)
        scatter.finish(1, sum_out)
        scatter.end()


def mixture_all(routes_all, router_rows, x, g_all, w_expert, collective_id):
    experts, _, width, hidden = w_expert.shape
    rows = x.shape[0]
    slots = 8 * CAP
    struct = jax.ShapeDtypeStruct
    V, S = pltpu.VMEM, pltpu.SemaphoreType.DMA
    slot = struct((4, experts, slots, width), bf16)
    whole = pl.BlockSpec((rows, width), lambda k, e: (0, 0))
    outs = pl.pallas_call(
        mixture_kernel,
        name="mixture",
        grid=(4, experts),
        out_shape=(
            struct((32, rows, width), bf16),
            slot,
            slot,
            struct((4, experts, 3, slots, hidden), bf16),
            struct((rows, width), f32),
            struct((rows, width), f32),
            struct((4, 2, experts, rows), f32),
        ),
        in_specs=[
            pl.BlockSpec(routes_all.shape, lambda k, e: (0, 0, 0)),
            pl.BlockSpec(router_rows.shape, lambda k, e: (0, 0)),
            ANY,
            ANY,
            pl.BlockSpec((1, 3, width, hidden), lambda k, e: (e, 0, 0, 0)),
        ],
        out_specs=(
            ANY,
            ANY,
            ANY,
            pl.BlockSpec((1, 1, 3, slots, hidden), lambda k, e: (k, e, 0, 0, 0)),
            whole,
            whole,
            pl.BlockSpec((4, 2, experts, rows), lambda k, e: (0, 0, 0, 0)),
        ),
        scratch_shapes=[
            V((2, rows, width), bf16), V((2, rows, width), bf16),
            V((experts, slots, width), bf16), V((experts, slots, width), bf16),
            V((experts, slots, 128), f32), V((experts, slots, 128), f32),
            V((8, experts, rows), jnp.int32), V((router_rows.shape[0], rows), f32),
            S((4,)), S((2, experts)),
            *Gather.scratch(), *Scatter.scratch(rows, width), *Probs.scratch((experts, rows)),
        ],
        compiler_params=pltpu.CompilerParams(
            collective_id=collective_id, has_side_effects=True, vmem_limit_bytes=62 << 20,
            dimension_semantics=("arbitrary", "arbitrary"),
        ),
    )(routes_all, router_rows, x, g_all, w_expert)
    return outs[1:]


def weights_kernel(xs_ref, gs_ref, st_ref, wg_ref):
    rows = xs_ref.shape[0] * xs_ref.shape[2]
    width = xs_ref.shape[-1]
    x = xs_ref[...].reshape(rows, width)
    g = gs_ref[...].reshape(rows, width)
    act, gate_low, up_low = (st_ref[:, 0, i].reshape(rows, -1) for i in range(3))
    hidden = act.shape[-1]
    both = dot(x, jnp.concatenate([gate_low, up_low], axis=1), ((0,), (0,)))
    wg_ref[0, 0] = both[:, :hidden]
    wg_ref[0, 1] = both[:, hidden:]
    wg_ref[0, 2] = dot(g, act, ((0,), (0,)))


def weights_all(xs, gs, st):
    chunks, experts, slots, width = xs.shape
    hidden = st.shape[-1]
    row = pl.BlockSpec((chunks, 1, slots, width), lambda e: (0, e, 0, 0))
    return pl.pallas_call(
        weights_kernel,
        name="weights",
        grid=(experts,),
        out_shape=jax.ShapeDtypeStruct((experts, 3, width, hidden), f32),
        in_specs=[row, row, pl.BlockSpec((chunks, 1, 3, slots, hidden), lambda e: (0, e, 0, 0, 0))],
        out_specs=pl.BlockSpec((1, 3, width, hidden), lambda e: (e, 0, 0, 0)),
        compiler_params=pltpu.CompilerParams(vmem_limit_bytes=60 << 20),
    )(xs, gs, st)


class HeadsAttention:
    def __init__(self, hidden, segments, routes, w_in, w_out, w_router, gains, experts):
        seq, batch = 8, 4
        place, b = lax.axis_index("seq"), lax.axis_index("batch")
        self.rows, self.width = hidden.shape
        width = self.width
        self.hs = width // HEADS
        self.hl = HEADS // seq
        cols = self.hl * self.hs
        self.cols = cols
        top = routes.shape[1]
        total = experts * seq
        ints = jnp.concatenate([routes.T, segments[None], jnp.zeros((7, self.rows), jnp.int32)], axis=0)
        small = jnp.concatenate(
            [w_router, gains.T, jnp.zeros((w_router.shape[0], 128 - total - gains.shape[0]), bf16)], axis=1
        )
        hidden_all, w_cols, w_rows, ints, small = gather_first(hidden, w_in, w_out, ints, small, 0)
        length = seq * self.rows
        self.length = length
        self.w_cols = w_cols.reshape(width, 3 * cols)
        self.w_rows = w_rows.reshape(cols, width)
        small = small.reshape(width, 128)
        self.router_all = small[:, :total]
        self.gains_all = small[:, total : total + 4].T.astype(f32)
        self.routes_all = ints[:, :top]
        segment_all = lax.dynamic_slice_in_dim(ints.reshape(seq, batch, -1, self.rows), b, 1, 1)
        segment_all = segment_all[:, 0, top].reshape(length)
        gains_all = self.gains_all
        inputs = hidden_all.reshape(length, width).astype(f32)
        self.first_normal = inputs * rms_scale(inputs)
        normed = (self.first_normal * gains_all[0]).astype(bf16)
        self.normed = normed
        projected = jnp.dot(normed, self.w_cols, preferred_element_type=f32)
        query_raw = projected[:, :cols]
        key_raw = projected[:, cols : 2 * cols]
        squares = jnp.stack([jnp.sum(query_raw * query_raw, -1), jnp.sum(key_raw * key_raw, -1)], 0)
        scales = lax.rsqrt(self.over_heads(squares, 1) / width + epsilon)
        self.query_scale = scales[0][:, None]
        self.key_scale = scales[1][:, None]
        self.query_normal = query_raw * self.query_scale
        self.key_normal = key_raw * self.key_scale
        mine = lax.dynamic_slice_in_dim(gains_all, place * cols, cols, 1)
        self.query_gain, self.key_gain = mine[1], mine[2]
        positions = jnp.arange(length, dtype=jnp.int32)
        self.cosine, self.sine = rope_tables(positions, self.hs)
        shape = (length, self.hl, self.hs)

        def rot(u):
            u = u.reshape(shape)
            return (u * self.cosine + rotate_half(u) * self.sine).astype(bf16)

        self.query = rot(self.query_normal * self.query_gain)
        self.key = rot(self.key_normal * self.key_gain)
        self.value = projected[:, 2 * cols :].astype(bf16).reshape(shape)
        self.allowed = (positions[None, :] <= positions[:, None]) & (
            segment_all[None, :] == segment_all[:, None]
        )
        scores = self.scores()
        top = jnp.max(scores, axis=-1, keepdims=True)
        weights = jnp.exp(scores - top)
        total = jnp.sum(weights, axis=-1, keepdims=True)
        acc = jnp.einsum("hqk,khd->hqd", weights.astype(bf16), self.value, preferred_element_type=f32)
        self.log_total = top + jnp.log(total)
        self.attended = jnp.transpose(acc / total, (1, 0, 2))
        self.attn_low = self.attended.reshape(length, cols).astype(bf16)
        partial = jnp.dot(self.attn_low, self.w_rows, preferred_element_type=f32).astype(bf16)
        self.mixed = scatter_seq(partial.reshape(seq, self.rows, width), 2, f32)

    def over_heads(self, sums, collective_id):
        return sum_seq(sums.reshape(2, -1, 128), collective_id).reshape(2, self.length)

    def scores(self):
        scale = self.hs ** (-0.5)
        scores = jnp.einsum("qhd,khd->hqk", self.query, self.key, preferred_element_type=f32) * scale
        return jnp.where(self.allowed[None], scores, -jnp.inf)

    def back(self, middle_low, router_grad, ffn_gain_grad):
        seq, batch = 8, 4
        length, cols, width = self.length, self.cols, self.width
        scale = self.hs ** (-0.5)
        shape = (length, self.hl, self.hs)
        grad_all = gather_seq(middle_low, 3).reshape(length, width)
        out_grad = dot(self.attn_low, grad_all, ((0,), (0,))).astype(bf16)
        attn_grad = dot(grad_all, self.w_rows, ((1,), (1,))).astype(bf16).reshape(shape)
        delta = jnp.sum(attn_grad.astype(f32) * self.attended, axis=-1)
        probs = jnp.exp(self.scores() - self.log_total)
        prob_grad = jnp.einsum("qhd,khd->hqk", attn_grad, self.value, preferred_element_type=f32)
        score_grad = (probs * (prob_grad - delta.T[..., None])).astype(bf16)
        query_grad = jnp.einsum("hqk,khd->qhd", score_grad, self.key, preferred_element_type=f32) * scale
        key_grad = jnp.einsum("hqk,qhd->khd", score_grad, self.query, preferred_element_type=f32) * scale
        value_grad = jnp.einsum("hqk,qhd->khd", probs.astype(bf16), attn_grad, preferred_element_type=f32)

        def rot_back(u):
            return (u * self.cosine - rotate_half(u * self.sine)).reshape(length, cols)

        query_norm_grad = rot_back(query_grad)
        key_norm_grad = rot_back(key_grad)
        query_gain_grad = jnp.sum(query_norm_grad * self.query_normal, axis=0)
        key_gain_grad = jnp.sum(key_norm_grad * self.key_normal, axis=0)
        query_scaled = query_norm_grad * self.query_gain
        key_scaled = key_norm_grad * self.key_gain
        dots = jnp.stack(
            [jnp.sum(query_scaled * self.query_normal, -1), jnp.sum(key_scaled * self.key_normal, -1)], 0
        )
        means = self.over_heads(dots, 4) / width
        query_raw_grad = self.query_scale * (query_scaled - self.query_normal * means[0][:, None])
        key_raw_grad = self.key_scale * (key_scaled - self.key_normal * means[1][:, None])
        projected_grad = jnp.concatenate(
            [query_raw_grad, key_raw_grad, value_grad.reshape(length, cols)], axis=1
        ).astype(bf16)
        partial = dot(projected_grad, self.w_cols, ((1,), (1,)))
        attn_gain_grad = jnp.sum(partial * self.first_normal, axis=0)
        in_grad = dot(self.normed, projected_grad, ((0,), (0,))).astype(bf16)
        own = width // (seq * batch)

        def by_batch(value, *shape):
            return jnp.swapaxes(value.reshape(2, 2, *shape), 0, 1)

        in_grad = jnp.transpose(in_grad.reshape(seq, 2, 2, own, 3 * cols), (2, 1, 0, 3, 4))
        out_grad = by_batch(out_grad, own, width)
        mine = jnp.arange(seq)[:, None] == lax.axis_index("seq")

        def own_columns(value):
            return jnp.where(mine, value[None], 0.0).reshape(width)

        gains_grad = jnp.stack(
            [attn_gain_grad, own_columns(query_gain_grad), own_columns(key_gain_grad), ffn_gain_grad], axis=1
        )
        total = router_grad.shape[1]
        small = jnp.concatenate([router_grad, gains_grad, jnp.zeros((width, 128 - total - 4), f32)], axis=1)
        small = jnp.transpose(small.reshape(4, 2, 2, 2, own, 128), (3, 2, 1, 0, 4, 5))
        normed_grad, in_shard, out_shard, small = scatter_last(
            partial.astype(bf16).reshape(seq, self.rows, width), in_grad, out_grad, small, 5
        )
        in_shard = jnp.transpose(in_shard.reshape(seq, own, 3, cols), (1, 2, 0, 3)).reshape(own, 3 * width)
        return normed_grad, in_shard, out_shard, small[:, :total], small[:, total : total + 4].T


def experts_by_tokens(ffn_in, cotangent_all, routes_all, w_expert, router_all):
    rows, width = ffn_in.shape
    xs, gs, factors, ffn_in_grad, mixture, probs = mixture_all(
        routes_all, router_all.T, ffn_in, cotangent_all.reshape(32, rows, width), w_expert, 6
    )
    prob_grad = probs.reshape(-1, rows).T
    return mixture, ffn_in_grad, prob_grad, weights_all(xs, gs, factors)


class TokensAttention:
    def __init__(self, hidden, segment_all, w_in, w_out, gains_all):
        place = lax.axis_index("seq")
        rows, width = hidden.shape
        self.rows, self.width = rows, width
        self.hs = width // HEADS
        self.sources = w_in, w_out
        self.gather_weights(w_in, w_out)
        inputs = hidden.astype(f32)
        self.normed = (inputs * rms_scale(inputs) * gains_all[0]).astype(bf16)
        projected = jnp.dot(self.normed, self.in_all, preferred_element_type=f32)
        query_raw = projected[:, :width]
        key_raw = projected[:, width : 2 * width]
        self.query_scale = rms_scale(query_raw)
        self.query_normal = query_raw * self.query_scale
        self.key_scale = rms_scale(key_raw)
        self.key_normal = key_raw * self.key_scale
        self.query_gain, self.key_gain = gains_all[1], gains_all[2]
        self.positions = place * rows + jnp.arange(rows, dtype=jnp.int32)
        self.cosine, self.sine = rope_tables(self.positions, self.hs)
        shape = (rows, HEADS, self.hs)

        def rot(u):
            u = u.reshape(shape)
            return (u * self.cosine + rotate_half(u) * self.sine).astype(bf16)

        self.query = rot(self.query_normal * self.query_gain)
        key = rot(self.key_normal * self.key_gain).reshape(rows, width)
        value = projected[:, 2 * width :].astype(bf16)
        self.kept = key, value
        self.gather_keys(key, value)
        self.segment_all = segment_all
        self.segment_own = lax.dynamic_slice_in_dim(segment_all, place * rows, rows, 0)
        length = self.key_all.shape[0]
        scores = self.scores(self.key_all.reshape(length, HEADS, self.hs), segment_all, 0)
        top = jnp.max(scores, axis=-1, keepdims=True)
        weights = jnp.exp(scores - top)
        total = jnp.sum(weights, axis=-1, keepdims=True)
        acc = jnp.einsum(
            "hqk,khd->hqd",
            weights.astype(bf16),
            self.value_all.reshape(length, HEADS, self.hs),
            preferred_element_type=f32,
        )
        self.log_total = top + jnp.log(total)
        self.attended = jnp.transpose(acc / total, (1, 0, 2))
        self.attn_low = self.attended.reshape(rows, width).astype(bf16)
        self.mixed = jnp.dot(self.attn_low, self.out_all, preferred_element_type=f32)

    def gather_weights(self, w_in, w_out):
        self.in_all = lax.all_gather(w_in, BOTH, axis=0, tiled=True)
        self.out_all = lax.all_gather(w_out, BOTH, axis=0, tiled=True)

    def gather_keys(self, key, value):
        self.key_all = lax.all_gather(key, "seq", axis=0, tiled=True)
        self.value_all = lax.all_gather(value, "seq", axis=0, tiled=True)

    def scores(self, key, segment, start):
        scale = self.hs ** (-0.5)
        scores = jnp.einsum("qhd,khd->hqk", self.query, key, preferred_element_type=f32) * scale
        key_positions = start + jnp.arange(key.shape[0], dtype=jnp.int32)
        allowed = (key_positions[None, :] <= self.positions[:, None]) & (
            segment[None, :] == self.segment_own[:, None]
        )
        return jnp.where(allowed[None], scores, -jnp.inf)

    def back(self, middle_low, router_grad, ffn_gain_grad):
        again = lax.optimization_barrier((middle_low, *self.sources, *self.kept))
        middle_low = again[0]
        self.gather_weights(*again[1:3])
        self.gather_keys(*again[3:])
        rows, width = self.rows, self.width
        scale = self.hs ** (-0.5)
        out_grad = dot(self.attn_low, middle_low, ((0,), (0,))).astype(bf16)
        out_shard = lax.psum_scatter(out_grad, BOTH, scatter_dimension=0, tiled=True).astype(f32)
        attn_grad = dot(middle_low, self.out_all, ((1,), (1,))).astype(bf16).reshape(rows, HEADS, self.hs)
        delta = jnp.sum(attn_grad.astype(f32) * self.attended, axis=-1).T
        length = self.key_all.shape[0]
        block = min(512, length)
        count = length // block

        def step(query_grad, item):
            key, value, segment, start = item
            probs = jnp.exp(self.scores(key, segment, start) - self.log_total)
            prob_grad = jnp.einsum("qhd,khd->hqk", attn_grad, value, preferred_element_type=f32)
            score_grad = (probs * (prob_grad - delta[..., None])).astype(bf16)
            query_grad = (
                query_grad + jnp.einsum("hqk,khd->qhd", score_grad, key, preferred_element_type=f32) * scale
            )
            key_grad = jnp.einsum("hqk,qhd->khd", score_grad, self.query, preferred_element_type=f32) * scale
            value_grad = jnp.einsum("hqk,qhd->khd", probs.astype(bf16), attn_grad, preferred_element_type=f32)
            return query_grad, jnp.concatenate(
                [key_grad.reshape(block, width), value_grad.reshape(block, width)], axis=1
            ).astype(bf16)

        query_grad, terms = lax.scan(
            step,
            jnp.zeros((rows, HEADS, self.hs), f32),
            (
                self.key_all.reshape(count, block, HEADS, self.hs),
                self.value_all.reshape(count, block, HEADS, self.hs),
                self.segment_all.reshape(count, block),
                jnp.arange(count, dtype=jnp.int32) * block,
            ),
        )
        kv_grad = lax.psum_scatter(
            terms.reshape(length, 2 * width), "seq", scatter_dimension=0, tiled=True
        ).astype(f32)
        key_grad = kv_grad[:, :width].reshape(rows, HEADS, self.hs)

        def rot_back(u):
            return (u * self.cosine - rotate_half(u * self.sine)).reshape(rows, width)

        query_norm_grad = rot_back(query_grad)
        key_norm_grad = rot_back(key_grad)
        query_gain_grad = jnp.sum(query_norm_grad * self.query_normal, axis=0)
        key_gain_grad = jnp.sum(key_norm_grad * self.key_normal, axis=0)
        query_raw_grad = norm_back(query_norm_grad, self.query_normal, self.query_scale, self.query_gain)
        key_raw_grad = norm_back(key_norm_grad, self.key_normal, self.key_scale, self.key_gain)
        projected_grad = jnp.concatenate([query_raw_grad, key_raw_grad, kv_grad[:, width:]], axis=1).astype(bf16)
        in_grad = dot(self.normed, projected_grad, ((0,), (0,))).astype(bf16)
        in_shard = lax.psum_scatter(in_grad, BOTH, scatter_dimension=0, tiled=True).astype(f32)
        normed_grad = dot(projected_grad, self.in_all, ((1,), (1,)))
        pair = lax.psum_scatter(
            jnp.stack([query_gain_grad, key_gain_grad], 1), BOTH, scatter_dimension=0, tiled=True
        )
        return normed_grad, in_shard, out_shard, router_grad, pair


def expert_math(slots, grads, gate_slot, w_expert):
    w_gate, w_up, w_down = w_expert[:, 0], w_expert[:, 1], w_expert[:, 2]
    gate = jnp.einsum("esd,edf->esf", slots, w_gate, preferred_element_type=f32)
    up = jnp.einsum("esd,edf->esf", slots, w_up, preferred_element_type=f32)
    sigma = jax.nn.sigmoid(gate)
    silu = gate * sigma
    act = (silu * up).astype(bf16).astype(f32)
    act_gated = (act * gate_slot).astype(bf16)
    act_raw = jnp.einsum("esd,edf->esf", grads, w_down, preferred_element_type=f32)
    gate_grad = jnp.sum(act_raw * act, axis=-1)
    act_grad = act_raw * gate_slot
    gate_low = (act_grad * up * sigma * (1.0 + gate * (1.0 - sigma))).astype(bf16)
    up_low = (act_grad * silu).astype(bf16)
    slot_grad = (
        jnp.einsum("esf,edf->esd", gate_low, w_gate, preferred_element_type=f32)
        + jnp.einsum("esf,edf->esd", up_low, w_up, preferred_element_type=f32)
    ).astype(bf16)
    result = jnp.einsum("esf,edf->esd", act_gated, w_down, preferred_element_type=f32).astype(bf16)
    expert_grad = jnp.stack(
        [
            jnp.einsum("esd,esf->edf", slots, gate_low, preferred_element_type=f32),
            jnp.einsum("esd,esf->edf", slots, up_low, preferred_element_type=f32),
            jnp.einsum("esd,esf->edf", grads, act_gated, preferred_element_type=f32),
        ],
        axis=1,
    )
    return result, slot_grad, gate_grad, expert_grad


def slot_places(hit):
    count = hit.astype(jnp.int32)
    rank = jnp.where(hit, jnp.cumsum(count, axis=1) - count, -1)
    return rank[:, :, :, None] == jnp.arange(CAP, dtype=jnp.int32)


def experts_by_slots(ffn_in, cotangent, routes, w_expert, router_all):
    seq, batch = lax.axis_size("seq"), lax.axis_size("batch")
    experts = w_expert.shape[0]
    total = experts * seq
    rows, width = ffn_in.shape
    hit = jnp.any(routes[:, :, None] == jnp.arange(total, dtype=jnp.int32), axis=1)[None]
    hot = slot_places(hit)[0]
    place_hot = hot.astype(bf16).reshape(rows, total * CAP)
    router = jax.nn.softmax(jnp.dot(ffn_in, router_all, preferred_element_type=f32), axis=-1)
    gate_slot = jnp.sum(jnp.where(hot, router[:, :, None], 0.0), axis=0).reshape(seq, experts, CAP, 1)

    def there(values):
        values = lax.all_to_all(values, "seq", split_axis=0, concat_axis=0, tiled=True)
        values = lax.all_gather(values, "batch", axis=0, tiled=True)
        values = jnp.transpose(values, (1, 0, 2, 3))
        return values.reshape(experts, batch * seq * CAP, values.shape[-1])

    def back(values):
        values = values.reshape(experts, batch * seq, CAP, values.shape[-1])
        values = jnp.transpose(values, (1, 0, 2, 3))
        values = lax.psum_scatter(values, "batch", scatter_dimension=0, tiled=True)
        values = lax.all_to_all(values, "seq", split_axis=0, concat_axis=0, tiled=True)
        return values.reshape(total * CAP, values.shape[-1])

    def slots_of(tokens):
        slots = dot(place_hot, tokens, ((0,), (0,))).astype(bf16)
        return there(slots.reshape(seq, experts, CAP, width))

    def tokens_of(slots):
        return jnp.dot(place_hot, back(slots), preferred_element_type=f32)

    result, slot_grad, gate_grad, expert_grad = expert_math(
        slots_of(ffn_in), slots_of(cotangent), there(gate_slot), w_expert
    )
    gate_grad = back(gate_grad[..., None]).reshape(1, total, CAP)
    prob_grad = jnp.sum(jnp.where(hot, gate_grad, 0.0), axis=-1)
    return tokens_of(result), tokens_of(slot_grad), prob_grad, expert_grad


def local(hidden, segments, routes, w_in, w_out, w_router, gains, w_expert, cotangent):
    seq = lax.axis_size("seq")
    total_experts = w_expert.shape[0] * seq
    by_heads = seq == 8 and lax.axis_size("batch") == 4

    inputs = hidden[0].astype(f32)
    first_scale = rms_scale(inputs)
    first_normal = inputs * first_scale
    if by_heads:
        cotangent_all = lax.all_gather(cotangent[0], BOTH, axis=0, tiled=True)
        attention = HeadsAttention(
            hidden[0], segments[0], routes[0], w_in, w_out, w_router, gains, w_expert.shape[0]
        )
        gains_all, router_all = attention.gains_all, attention.router_all
    else:
        small = lax.all_gather(jnp.concatenate([w_router, gains.T], axis=1), BOTH, axis=0, tiled=True)
        router_all = small[:, :total_experts]
        gains_all = small[:, total_experts:].T.astype(f32)
        segment_all = lax.all_gather(segments[0], "seq", axis=0, tiled=True)
        attention = TokensAttention(hidden[0], segment_all, w_in, w_out, gains_all)

    middle = inputs + attention.mixed
    second_scale = rms_scale(middle)
    second_normal = middle * second_scale
    ffn_in = (second_normal * gains_all[3]).astype(bf16)
    if by_heads:
        mixture, ffn_in_grad, prob_grad, expert_grad = experts_by_tokens(
            ffn_in, cotangent_all, attention.routes_all, w_expert, router_all
        )
    else:
        mixture, ffn_in_grad, prob_grad, expert_grad = experts_by_slots(
            ffn_in, cotangent[0], routes[0], w_expert, router_all
        )
    output = middle + mixture

    grad_out = cotangent[0].astype(f32)
    router = jax.nn.softmax(jnp.dot(ffn_in, router_all, preferred_element_type=f32), axis=-1)
    logit_grad = router * (prob_grad - jnp.sum(router * prob_grad, axis=-1, keepdims=True))
    logit_low = logit_grad.astype(bf16)
    router_grad = dot(ffn_in, logit_low, ((0,), (0,)))
    ffn_in_grad = ffn_in_grad + dot(logit_low, router_all, ((1,), (1,)))
    ffn_gain_grad = jnp.sum(ffn_in_grad * second_normal, axis=0)
    middle_grad = grad_out + norm_back(ffn_in_grad, second_normal, second_scale, gains_all[3])
    normed_grad, in_shard, out_shard, router_shard, gains_shard = attention.back(
        middle_grad.astype(bf16), router_grad, ffn_gain_grad
    )
    if not by_heads:
        attn_gain_grad = jnp.sum(normed_grad * first_normal, axis=0)
        ends = jnp.stack([attn_gain_grad, ffn_gain_grad], axis=1)
        sums = lax.psum_scatter(
            jnp.concatenate([router_shard, ends], axis=1), BOTH, scatter_dimension=0, tiled=True
        )
        router_shard, ends = sums[:, :total_experts], sums[:, total_experts:]
        gains_shard = jnp.stack([ends[:, 0], gains_shard[:, 0], gains_shard[:, 1], ends[:, 1]], axis=0)
    input_grad = middle_grad + norm_back(normed_grad, first_normal, first_scale, gains_all[0])
    return (
        output.astype(bf16)[None],
        input_grad[None],
        in_shard,
        out_shard,
        router_shard,
        gains_shard,
        expert_grad,
    )


def solution(mesh):
    placed = (
        P("batch", "seq", None),
        P("batch", "seq"),
        P("batch", "seq", None),
        P(BOTH, None),
        P(BOTH, None),
        P(BOTH, None),
        P(None, BOTH),
        P("seq", None, None, "batch"),
        P("batch", "seq", None),
    )
    return jax.shard_map(
        local,
        mesh=mesh,
        in_specs=placed,
        out_specs=(
            P("batch", "seq", None),
            P("batch", "seq", None),
            P(BOTH, None),
            P(BOTH, None),
            P(BOTH, None),
            P(None, BOTH),
            P("seq", None, None, "batch"),
        ),
        check_vma=False,
    )
```

```python
import functools

import jax
import jax.numpy as jnp
from jax import lax
from jax.experimental import pallas as pl
from jax.experimental.pallas import tpu as pltpu
from jax.sharding import PartitionSpec as P

HEADS = 16
CAP = 32
epsilon = 1e-05
BOTH = ("seq", "batch")
f32 = jnp.float32
bf16 = jnp.bfloat16
MESH = pl.DeviceIdType.MESH


def rms_scale(values):
    return lax.rsqrt(jnp.mean(values * values, axis=-1, keepdims=True) + epsilon)


def rotate_half(values):
    half = values.shape[-1] // 2
    return jnp.concatenate([-values[..., half:], values[..., :half]], axis=-1)


def rope_tables(positions, head_size):
    steps = jnp.arange(head_size // 2, dtype=f32)
    freqs = jnp.exp(steps * (-2.0 * jnp.log(10000.0) / head_size))
    angles = positions.astype(f32)[:, None] * freqs[None, :]
    angles = jnp.concatenate([angles, angles], axis=-1)
    return (jnp.cos(angles)[:, None, :], jnp.sin(angles)[:, None, :])


def norm_back(grad_out, normal, scale, gain):
    scaled = grad_out * gain
    return scale * (scaled - normal * jnp.mean(scaled * normal, axis=-1, keepdims=True))


def dot(a, b, dims):
    return lax.dot_general(a, b, (dims, ((), ())), preferred_element_type=f32)


ANY = pl.BlockSpec(memory_space=pl.ANY)
WHOLE = pl.BlockSpec(memory_space=pltpu.VMEM)


class Place:
    def __init__(self):
        s, b = lax.axis_index("seq"), lax.axis_index("batch")
        self.z, self.y = s // 2, lax.rem(s, 2)
        self.x, self.c = b // 2, lax.rem(b, 2)

    def at(self, r=0, y=0, x=0, c=0):
        z = lax.rem(self.z + r, 4)
        yy = 1 - self.y if y else self.y
        xx = 1 - self.x if x else self.x
        cc = 1 - self.c if c else self.c
        return (z * 2 + yy, xx * 2 + cc)

    def index(self, r=0, y=0, x=0, c=0):
        s, b = self.at(r, y, x, c)
        return s * 4 + b


def barrier(peers):
    sem = pltpu.get_barrier_semaphore()
    for peer in peers:
        pl.semaphore_signal(sem, inc=1, device_id=peer, device_id_type=MESH)
    pl.semaphore_wait(sem, len(peers))


class Sends:
    def __init__(self, send_sem, recv_sem):
        self.send_sem, self.recv_sem, self.copies = send_sem, recv_sem, []

    def start(self, src, dst, peer):
        k = len(self.copies)
        copy = pltpu.make_async_remote_copy(
            src_ref=src,
            dst_ref=dst,
            send_sem=self.send_sem.at[k],
            recv_sem=self.recv_sem.at[k],
            device_id=peer,
            device_id_type=MESH,
        )
        copy.start()
        self.copies.append(copy)
        return copy

    def finish(self):
        for copy in self.copies:
            copy.wait_send()


def add_rows(dst, src, start, rows):
    step = 16

    def body(i, _):
        at = pl.ds(pl.multiple_of(start + i * step, step), step)
        dst[at] = (dst[at].astype(f32) + src[at].astype(f32)).astype(dst.dtype)
        return 0

    lax.fori_loop(0, rows // step, body, 0)


def call(kernel, name, collective_id, out_shape, in_specs, out_specs, scratch, copies, local=1, vmem=32):
    return pl.pallas_call(
        kernel,
        name=name,
        out_shape=out_shape,
        in_specs=in_specs,
        out_specs=out_specs,
        scratch_shapes=[
            *scratch,
            pltpu.SemaphoreType.DMA((copies,)),
            pltpu.SemaphoreType.DMA((copies,)),
            pltpu.SemaphoreType.DMA((local,)),
        ],
        compiler_params=pltpu.CompilerParams(
            collective_id=collective_id, has_side_effects=True, vmem_limit_bytes=vmem << 20
        ),
    )


Z_ORDER = (1, 3, 2)


def gather_first_kernel(
    h_ref, wi_ref, wo_ref, ints_ref, small_ref,
    h_out, wi_out, wo_out, ints_out, small_out,
    ints, small, send_sem, recv_sem, own_sem,
):
    p = Place()
    seq, b = p.at()
    x, c = p.x, p.c
    others = [p.at(r, y) for y in (0, 1) for r in range(4) if r or y]
    barrier(others + [p.at(x=1), p.at(c=1)])
    sends = Sends(send_sem, recv_sem)
    owns = [
        pltpu.make_async_copy(h_ref, h_out.at[seq], own_sem.at[0]),
        pltpu.make_async_copy(wi_ref.at[seq], wi_out.at[seq, b], own_sem.at[1]),
        pltpu.make_async_copy(wo_ref, wo_out.at[b], own_sem.at[2]),
    ]
    for own in owns:
        own.start()
    me = p.index()
    pairs = ((ints_ref, ints), (small_ref, small))
    for src, dst in pairs:
        dst[me] = src[...]
    first = [sends.start(dst.at[me], dst.at[me], p.at(c=1)) for _, dst in pairs]
    h_z = {r: sends.start(h_ref, h_out.at[seq], p.at(r)) for r in Z_ORDER}
    h_y = [sends.start(h_ref, h_out.at[seq], p.at(y=1))]
    w_s = {}
    for r, y in ((0, 1), (1, 0), (3, 0), (2, 0), (1, 1), (3, 1), (2, 1)):
        to = p.at(r, y)
        w_s[r, y] = sends.start(wi_ref.at[to[0]], wi_out.at[seq, b], to)
    w_x = [sends.start(wi_ref.at[seq], wi_out.at[seq, b], p.at(x=1))]
    w_c = [sends.start(wi_ref.at[seq], wi_out.at[seq, b], p.at(c=1))]
    o_x = sends.start(wo_ref, wo_out.at[b], p.at(x=1))
    w_c.append(sends.start(wo_ref, wo_out.at[b], p.at(c=1)))
    for copy in first:
        copy.wait_recv()
    base = me - c
    second = [sends.start(dst.at[pl.ds(base, 2)], dst.at[pl.ds(base, 2)], p.at(x=1)) for _, dst in pairs]
    for copy in second:
        copy.wait_recv()
    base = me - b
    third = [sends.start(dst.at[pl.ds(base, 4)], dst.at[pl.ds(base, 4)], p.at(y=1)) for _, dst in pairs]
    for copy in third:
        copy.wait_recv()
    base = p.z * 8
    fourth = [
        sends.start(dst.at[pl.ds(base, 8)], dst.at[pl.ds(base, 8)], p.at(r)) for _, dst in pairs for r in Z_ORDER
    ]
    for r in Z_ORDER:
        h_z[r].wait_recv()
        s = p.at(-r % 4)[0]
        h_y.append(sends.start(h_out.at[s], h_out.at[s], p.at(y=1)))
    for r, y in ((0, 1), (1, 0), (3, 0), (2, 0), (1, 1), (3, 1), (2, 1)):
        w_s[r, y].wait_recv()
        s = p.at(-r % 4, y)[0]
        w_x.append(sends.start(wi_out.at[s, b], wi_out.at[s, b], p.at(x=1)))
        w_c.append(sends.start(wi_out.at[s, b], wi_out.at[s, b], p.at(c=1)))
    bx = p.at(x=1)[1]
    o_x.wait_recv()
    w_c.append(sends.start(wo_out.at[bx], wo_out.at[bx], p.at(c=1)))
    places = [(0, 0), (0, 1), (1, 0), (3, 0), (2, 0), (1, 1), (3, 1), (2, 1)]
    for copy, (r, y) in zip(w_x, places):
        copy.wait_recv()
        s = p.at(-r % 4, y)[0]
        w_c.append(sends.start(wi_out.at[s, bx], wi_out.at[s, bx], p.at(c=1)))
    for copy in fourth + h_y + w_c:
        copy.wait_recv()
    ints_out[...] = ints[...]
    small_out[...] = small[...]
    sends.finish()
    for own in owns:
        own.wait()


def gather_first(hidden, w_in, w_out, ints, small, collective_id):
    own = w_in.shape[0]
    parts = jnp.transpose(w_in.reshape(own, 3, 8, -1), (2, 0, 1, 3)).reshape(8, own, -1)
    struct = jax.ShapeDtypeStruct
    outs = call(
        gather_first_kernel,
        "gather_first",
        collective_id,
        (
            struct((8,) + hidden.shape, bf16),
            struct((8, 4) + parts.shape[1:], bf16),
            struct((4,) + w_out.shape, bf16),
            struct((32,) + ints.shape, ints.dtype),
            struct((32,) + small.shape, small.dtype),
        ),
        [ANY, ANY, ANY, WHOLE, WHOLE],
        (ANY, ANY, ANY, WHOLE, WHOLE),
        [
            pltpu.VMEM((32,) + ints.shape, ints.dtype),
            pltpu.VMEM((32,) + small.shape, small.dtype),
        ],
        2 + 3 + 1 + 7 + 1 + 1 + 1 + 1 + 2 + 2 + 6 + 3 + 7 + 7 + 1 + 8,
        3,
    )(hidden, parts, w_out, ints, small)
    return outs


def scatter_seq_kernel(p_ref, out_ref, acc, ry, rz, send_sem, recv_sem, own_sem):
    p = Place()
    barrier([p.at(1), p.at(2), p.at(3), p.at(y=1)])
    sends = Sends(send_sem, recv_sem)
    order = (2, 1, 3, 0)
    loads, fy, fz = [], [], []
    for n, r in enumerate(order):
        fy.append(sends.start(p_ref.at[p.at(r, 1)[0]], ry.at[n], p.at(y=1)))
        load = pltpu.make_async_copy(p_ref.at[p.at(r)[0]], acc.at[n], own_sem.at[n])
        load.start()
        loads.append(load)
    rows = acc.shape[1]
    for n, r in enumerate(order):
        loads[n].wait()
        fy[n].wait_recv()
        add_rows(acc.at[n], ry.at[n], 0, rows)
        if r:
            fz.append(sends.start(acc.at[n], rz.at[n], p.at(r)))
    for copy in fz:
        copy.wait_recv()

    def total(i, _):
        at = pl.ds(pl.multiple_of(i * 16, 16), 16)
        value = acc[3, at].astype(f32)
        for n in range(3):
            value = value + rz[n, at].astype(f32)
        out_ref[at] = value.astype(out_ref.dtype)
        return 0

    lax.fori_loop(0, rows // 16, total, 0)
    sends.finish()


def scatter_seq(parts, collective_id, dtype=bf16):
    block = parts.shape[1:]
    return call(
        scatter_seq_kernel,
        "scatter_seq",
        collective_id,
        jax.ShapeDtypeStruct(block, dtype),
        [ANY],
        WHOLE,
        [pltpu.VMEM((n,) + block, parts.dtype) for n in (4, 4, 3)],
        7,
        4,
    )(parts)


def sum_seq_kernel(x_ref, out_ref, got, send_sem, recv_sem, own_sem):
    p = Place()
    others = [p.at(r, y) for y in (0, 1) for r in range(4) if r or y]
    barrier(others)
    sends = Sends(send_sem, recv_sem)
    me = p.at()[0]
    got[me] = x_ref[...]
    copies = [sends.start(x_ref, got.at[me], to) for to in others]
    for copy in copies:
        copy.wait_recv()
    total = got[0]
    for n in range(1, 8):
        total = total + got[n]
    out_ref[...] = total
    sends.finish()


def sum_seq(x, collective_id):
    return call(
        sum_seq_kernel,
        "sum_seq",
        collective_id,
        jax.ShapeDtypeStruct(x.shape, x.dtype),
        [WHOLE],
        WHOLE,
        [pltpu.VMEM((8,) + x.shape, x.dtype)],
        7,
    )(x)


def add_blocks(dst, src):
    def body(i, _):
        dst[i] = (dst[i].astype(f32) + src[i].astype(f32)).astype(dst.dtype)
        return 0

    lax.fori_loop(0, dst.shape[0], body, 0)


def scatter_last_kernel(
    n_ref, wi_ref, wo_ref, sm_ref,
    n_out, wi_out, wo_out, sm_out,
    n_acc, n_y, n_z, wi_acc, wi_c, wi_x, wi_got, wo_acc, wo_c, wo_x, sm_acc, sm_c, sm_x, sm_y, sm_z,
    send_sem, recv_sem, own_sem,
):
    p = Place()
    c, x, y, z = p.c, p.x, p.y, p.z
    others = [p.at(r, yy) for yy in (0, 1) for r in range(4) if r or yy]
    barrier(others + [p.at(x=1), p.at(c=1)])
    sends = Sends(send_sem, recv_sem)
    core, nbr_x, nbr_y = p.at(c=1), p.at(x=1), p.at(y=1)
    order = (2, 1, 3, 0)
    loads = [
        pltpu.make_async_copy(wi_ref.at[:, 1 - x, c], wi_acc.at[0], own_sem.at[4]),
        pltpu.make_async_copy(wi_ref.at[:, x, c], wi_acc.at[1], own_sem.at[7]),
        pltpu.make_async_copy(wo_ref.at[:, c], wo_acc, own_sem.at[5]),
        pltpu.make_async_copy(sm_ref.at[:, :, :, c], sm_acc, own_sem.at[6]),
    ]
    for load in loads:
        load.start()
    wi1 = sends.start(wi_ref.at[:, 1 - x, 1 - c], wi_c.at[0], core)
    sm1 = sends.start(sm_ref.at[:, :, :, 1 - c], sm_c, core)
    wo1 = sends.start(wo_ref.at[:, 1 - c], wo_c, core)
    wi2 = sends.start(wi_ref.at[:, x, 1 - c], wi_c.at[1], core)
    fy, n_loads, fz = [], [], []
    for n, r in enumerate(order):
        fy.append(sends.start(n_ref.at[p.at(r, 1)[0]], n_y.at[n], nbr_y))
        load = pltpu.make_async_copy(n_ref.at[p.at(r)[0]], n_acc.at[n], own_sem.at[n])
        load.start()
        n_loads.append(load)
    for load in loads:
        load.wait()
    wi1.wait_recv()
    add_blocks(wi_acc.at[0], wi_c.at[0])
    wi3 = sends.start(wi_acc.at[0], wi_x, nbr_x)
    sm1.wait_recv()
    sm_acc[...] = sm_acc[...] + sm_c[...]
    sm2 = sends.start(sm_acc.at[:, :, 1 - x], sm_x, nbr_x)
    wo1.wait_recv()
    add_blocks(wo_acc, wo_c)
    wo2 = sends.start(wo_acc.at[1 - x], wo_x, nbr_x)
    wi2.wait_recv()
    add_blocks(wi_acc.at[1], wi_c.at[1])
    rows = n_acc.shape[1]
    for n, r in enumerate(order):
        n_loads[n].wait()
        fy[n].wait_recv()
        add_rows(n_acc.at[n], n_y.at[n], 0, rows)
        if r:
            fz.append(sends.start(n_acc.at[n], n_z.at[n], p.at(r)))
    wi3.wait_recv()
    add_blocks(wi_acc.at[1], wi_x)
    me = p.at()[0]
    wi4 = []
    for r, yy in ((0, 1), (1, 0), (3, 0), (2, 0), (1, 1), (3, 1), (2, 1)):
        to = p.at(r, yy)
        wi4.append(sends.start(wi_acc.at[1, to[0]], wi_got.at[me], to))
    sm2.wait_recv()
    sm_acc[:, :, x] = sm_acc[:, :, x] + sm_x[...]
    sm3 = sends.start(sm_acc.at[:, 1 - y, x], sm_y, nbr_y)
    wi_got[me] = wi_acc[1, me]
    wo2.wait_recv()
    wo_out[...] = wo_acc[x].astype(f32) + wo_x[...].astype(f32)
    sm3.wait_recv()
    sm_acc[:, y, x] = sm_acc[:, y, x] + sm_y[...]
    sm4 = [
        sends.start(sm_acc.at[lax.rem(z + r, 4), y, x], sm_z.at[n], p.at(r)) for n, r in enumerate(Z_ORDER)
    ]
    for copy in wi4:
        copy.wait_recv()
    seq, _, columns = wi_got.shape
    part = columns // 3
    for s in range(seq):
        for i in range(3):
            value = wi_got[s, :, i * part : (i + 1) * part].astype(f32)
            wi_out[:, (i * seq + s) * part : (i * seq + s + 1) * part] = value
    for copy in sm4:
        copy.wait_recv()
    sm_out[...] = sm_acc[z, y, x] + sm_z[0] + sm_z[1] + sm_z[2]
    for copy in fz:
        copy.wait_recv()

    def total(i, _):
        at = pl.ds(pl.multiple_of(i * 16, 16), 16)
        value = n_acc[3, at].astype(f32)
        for n in range(3):
            value = value + n_z[n, at].astype(f32)
        n_out[at] = value
        return 0

    lax.fori_loop(0, rows // 16, total, 0)
    sends.finish()


def scatter_last(normed, w_in, w_out, small, collective_id):
    struct = jax.ShapeDtypeStruct
    nb, ib, ob, sb = normed.shape[1:], w_in.shape[3:], w_out.shape[2:], small.shape[4:]
    V = pltpu.VMEM
    seq = w_in.shape[0]
    return call(
        scatter_last_kernel,
        "scatter_last",
        collective_id,
        (struct(nb, f32), struct((ib[0], seq * ib[1]), f32), struct(ob, f32), struct(sb, f32)),
        [ANY] * 4,
        (WHOLE,) * 4,
        [
            V((4,) + nb, bf16), V((4,) + nb, bf16), V((3,) + nb, bf16),
            V((2, seq) + ib, bf16), V((2, seq) + ib, bf16), V((seq,) + ib, bf16), V((seq,) + ib, bf16),
            V((2,) + ob, bf16), V((2,) + ob, bf16), V(ob, bf16),
            V((4, 2, 2) + sb, f32), V((4, 2, 2) + sb, f32), V((4, 2) + sb, f32), V((4,) + sb, f32), V((3,) + sb, f32),
        ],
        4 + 4 + 3 + 1 + 1 + 1 + 7 + 1 + 3,
        8,
        48,
    )(normed, w_in, w_out, small)


def slots_of_rows(ranks):
    experts, rows = ranks.shape
    slot = lax.broadcasted_iota(jnp.int32, (experts, CAP, rows), 1)
    return ranks[:, None, :] == slot


def one_hot(hot):
    experts, _, rows = hot.shape
    return jnp.where(hot, 1.0, 0.0).reshape(experts * CAP, rows).astype(bf16)


BACK = (1, 3, 2, 0)


class Flip(Place):
    def block(self, r=0, y=0, x=0, c=0):
        z = lax.rem(self.z + 4 - r, 4)
        yy, xx, cc = lax.rem(self.y + y, 2), lax.rem(self.x + x, 2), lax.rem(self.c + c, 2)
        return ((z * 2 + yy) * 2 + xx) * 2 + cc


def remote(src, dst, send, recv, peer):
    return pltpu.make_async_remote_copy(
        src_ref=src, dst_ref=dst, send_sem=send, recv_sem=recv, device_id=peer, device_id_type=MESH
    )


class Gather:
    @staticmethod
    def scratch():
        S = pltpu.SemaphoreType.DMA
        return [S((35,)), S((35,)), S]

    def __init__(self, p, x_ref, x_all, refs):
        send, recv, own_sem = refs
        rows = x_ref.shape[0]
        A, B = pl.ds(0, rows // 2), pl.ds(rows // 2, rows // 2)
        nx, ny, core = p.at(x=1), p.at(y=1), p.at(c=1)
        self.peers = [p.at(1), p.at(2), p.at(3), nx, ny, core]
        mine = p.block()
        self.own = pltpu.make_async_copy(x_ref, x_all.at[mine], own_sem)
        count = [0]

        def copy(src, dst, peer):
            i = count[0]
            count[0] += 1
            return remote(src, dst, send.at[i], recv.at[i], peer)

        self.along, self.to_x, self.to_y, self.to_core, self.by_y, self.by_x = [], [], [], [], [], []
        for k, r in enumerate(BACK):
            at, ix, iy, far = p.block(r), p.block(r, x=1), p.block(r, y=1), p.block(r, y=1, x=1)
            src = x_all.at[at]
            if r:
                self.along.append(copy(x_ref, x_all.at[mine], p.at(r)))
            else:
                src = x_ref
            self.to_x.append(copy(src, x_all.at[at], nx))
            self.to_y.append(copy(src, x_all.at[at], ny))
            self.by_y.append(copy(x_all.at[ix, A], x_all.at[ix, A], ny))
            self.by_x.append(copy(x_all.at[iy, B], x_all.at[iy, B], nx))
            self.to_core.append(
                [copy(src, x_all.at[at], core)]
                + [copy(x_all.at[i], x_all.at[i], core) for i in (ix, iy, far)]
            )

    def start(self):
        self.own.start()
        self.along[0].start()
        self.own.wait()

    def spread(self, k):
        if BACK[k]:
            self.along[k].wait_recv()
            if k < 2:
                self.along[k + 1].start()
        self.to_x[k].start()
        self.to_y[k].start()
        self.to_core[k][0].start()

    def cross(self, k):
        self.to_x[k].wait_recv()
        self.by_y[k].start()
        self.to_core[k][1].start()
        self.to_y[k].wait_recv()
        self.by_x[k].start()
        self.to_core[k][2].start()

    def close(self, k):
        self.by_y[k].wait_recv()
        self.by_x[k].wait_recv()
        self.to_core[k][3].start()

    def finish(self):
        for copy in self.along:
            copy.wait_send()
        for k in range(4):
            for copy in [self.to_x[k], self.to_y[k], self.by_y[k], self.by_x[k]] + self.to_core[k]:
                copy.wait_send()


class Scatter:
    @staticmethod
    def scratch(rows, width):
        V, S = pltpu.VMEM, pltpu.SemaphoreType.DMA
        block, half = (rows, width), (rows // 2, width)
        return [
            V((2, 4) + block, bf16), V((2, 2, 3) + block, bf16), V((2, 4) + block, bf16), V((2, 2) + half, bf16),
            V((2, 2) + block, bf16), V((4, 2) + block, bf16), V((3, 2) + block, bf16),
            S((32,)), S((32,)), S((38,)), S((38,)), pltpu.SemaphoreType.REGULAR((5,)),
        ]

    def __init__(self, p, refs):
        self.give, self.stage, self.pair, self.half, self.near, self.acc, self.far = refs[:7]
        self.core_send, self.core_recv, send, recv, self.free = refs[7:]
        self.p = p
        rows = self.give.shape[2]
        self.parts = A, B = pl.ds(0, rows // 2), pl.ds(rows // 2, rows // 2)
        nx, ny = p.at(x=1), p.at(y=1)
        self.core, self.nx, self.ny = p.at(c=1), nx, ny
        count = [0]

        def copy(src, dst, peer):
            i = count[0]
            count[0] += 1
            return remote(src, dst, send.at[i], recv.at[i], peer)

        self.by_y, self.by_x, self.to_x, self.to_y, self.to_z = [], [], [], [], []
        for k in range(4):
            out = [self.stage.at[k % 2, i] for i in (0, 1)]
            self.by_y.append([copy(out[i].at[2, A], self.half.at[i, 0], ny) for i in (0, 1)])
            self.by_x.append([copy(out[i].at[2, B], self.half.at[i, 1], nx) for i in (0, 1)])
            self.to_x.append([copy(out[i].at[0], self.near.at[i, 0], nx) for i in (0, 1)])
            self.to_y.append([copy(out[i].at[1], self.near.at[i, 1], ny) for i in (0, 1)])
            if BACK[k]:
                to = p.at((4 - BACK[k]) % 4)
                self.to_z.append([copy(self.acc.at[k, i], self.far.at[k, i], to) for i in (0, 1)])

    def to_core(self, k, i, pos):
        at = k * 8 + i * 4 + pos
        return remote(
            self.give.at[i, pos], self.pair.at[i, pos], self.core_send.at[at], self.core_recv.at[at], self.core
        )

    def add(self, dst, terms):
        step = 32

        def body(i, _):
            at = pl.ds(pl.multiple_of(i * step, step), step)
            if len(terms) == 2 and dst.dtype == bf16:
                dst[at] = terms[0][at] + terms[1][at]
                return 0
            value = terms[0][at].astype(f32)
            for term in terms[1:]:
                value = value + term[at].astype(f32)
            dst[at] = value.astype(dst.dtype)
            return 0

        lax.fori_loop(0, dst.shape[0] // step, body, 0)

    def signal(self, n, peer):
        pl.semaphore_signal(self.free.at[n], inc=1, device_id=peer, device_id_type=MESH)

    def diagonal(self, k, i):
        if k and not i:
            pl.semaphore_wait(self.free.at[1], 1)
            pl.semaphore_wait(self.free.at[2], 1)
        self.to_core(k, i, 3).wait_recv()
        at = self.stage.at[k % 2, i, 2]
        self.add(at, [at, self.pair.at[i, 3]])
        self.by_y[k][i].start()
        self.by_x[k][i].start()

    def across(self, k, i):
        A, B = self.parts
        for_x, for_y = self.stage.at[k % 2, i, 0], self.stage.at[k % 2, i, 1]
        if k and not i:
            pl.semaphore_wait(self.free.at[3], 1)
            pl.semaphore_wait(self.free.at[4], 1)
        self.to_core(k, i, 1).wait_recv()
        self.add(for_x.at[B], [for_x.at[B], self.pair.at[i, 1, B]])
        self.by_y[k][i].wait_recv()
        self.add(for_x.at[A], [for_x.at[A], self.pair.at[i, 1, A], self.half.at[i, 0]])
        self.to_x[k][i].start()
        self.to_core(k, i, 2).wait_recv()
        self.add(for_y.at[A], [for_y.at[A], self.pair.at[i, 2, A]])
        self.by_x[k][i].wait_recv()
        self.add(for_y.at[B], [for_y.at[B], self.pair.at[i, 2, B], self.half.at[i, 1]])
        self.to_y[k][i].start()
        self.to_core(k, i, 0).wait_recv()
        self.add(self.acc.at[k, i], [self.acc.at[k, i], self.pair.at[i, 0]])
        if k < 3 and i:
            self.signal(0, self.core)
            self.signal(1, self.nx)
            self.signal(2, self.ny)

    def line(self, k, i):
        self.to_x[k][i].wait_recv()
        self.to_y[k][i].wait_recv()
        self.add(self.acc.at[k, i], [self.acc.at[k, i], self.near.at[i, 0], self.near.at[i, 1]])
        if BACK[k]:
            self.to_z[k][i].start()
        if k < 3 and i:
            self.signal(3, self.nx)
            self.signal(4, self.ny)

    def settle_core(self, k):
        for i in (0, 1):
            for pos in range(4):
                self.to_core(k, i, pos).wait_send()

    def settle(self, k):
        for i in (0, 1):
            for copies in (self.by_y, self.by_x, self.to_x, self.to_y):
                copies[k][i].wait_send()

    def finish(self, i, out_ref):
        for copies in self.to_z:
            copies[i].wait_recv()
        self.add(out_ref, [self.acc.at[3, i]] + [self.far.at[n, i] for n in range(3)])

    def end(self):
        self.settle_core(3)
        self.settle(2)
        self.settle(3)
        for copies in self.to_z:
            for copy in copies:
                copy.wait_send()


class Probs:
    TURNS = ((0, 1), (1, 0), (3, 0), (2, 0), (1, 1), (3, 1), (2, 1))

    @staticmethod
    def scratch(block):
        V, S = pltpu.VMEM, pltpu.SemaphoreType.DMA
        return [
            V((2, 2, 2, 4) + block, f32), V((2, 2, 4) + block, f32), V((2, 4) + block, f32), V((2, 2, 4) + block, f32),
            V((2, 4) + block, f32), V((4, 2) + block, f32), S((9,)), S((9,)),
        ]

    def __init__(self, p, refs):
        self.p = p
        self.own, self.sum_x, self.sum_s, self.r1, self.r2, self.got, send, recv = refs
        self.peers = [p.at(r, y) for r, y in self.TURNS]
        self.first = remote(self.own.at[1 - p.c], self.r1, send.at[0], recv.at[0], p.at(c=1))
        self.second = remote(self.sum_x.at[1 - p.x], self.r2, send.at[1], recv.at[1], p.at(x=1))
        self.third = []
        for n, (r, y) in enumerate(self.TURNS):
            to = lax.rem(p.z + r, 4)
            yy = 1 - p.y if y else p.y
            self.third.append(
                remote(self.sum_s.at[yy, to], self.got.at[p.z, p.y], send.at[2 + n], recv.at[2 + n], p.at(r, y))
            )

    def start(self):
        self.first.start()

    def over_x(self):
        self.first.wait_recv()
        self.sum_x[...] = self.own[self.p.c] + self.r1[...]
        self.second.start()

    def over_seq(self):
        p = self.p
        self.second.wait_recv()
        self.sum_s[...] = self.sum_x[p.x] + self.r2[...]
        for copy in self.third:
            copy.start()
        self.got[p.z, p.y] = self.sum_s[p.y, p.z]

    def finish(self, out_ref):
        for copy in self.third:
            copy.wait_recv()
        out_ref[...] = self.got[...]
        for copy in [self.first, self.second] + self.third:
            copy.wait_send()


GATHER, SCATTER, PROBS = 3, 12, 8


def mixture_kernel(
    routes_ref, router_ref, x_ref, g_ref, w_ref,
    x_all, xs_out, gs_out, st_ref, grad_out, sum_out, probs_out,
    tx, tg, xs, gs, gates, grads, ranks, weights, load_sem, save_sem, *rest,
):
    p = Flip()
    chunk, e = pl.program_id(0), pl.program_id(1)
    experts, slots, width = xs.shape
    rows = tx.shape[1]
    gather = Gather(p, x_ref, x_all, rest[:GATHER])
    scatter = Scatter(p, rest[GATHER : GATHER + SCATTER])
    probs = Probs(p, rest[GATHER + SCATTER :])
    last = experts - 1

    def at_step(k, step, *events):
        def run():
            for event, *args in events:
                event(*args)

        pl.when((chunk == k) & (e == step))(run)

    def begin():
        barrier(gather.peers + [peer for peer, (r, y) in zip(probs.peers, probs.TURNS) if r and y])
        gather.start()
        gather.spread(3)
        gather.spread(0)

    at_step(0, 0, (begin,))
    at_step(0, 1, (gather.cross, 1), (gather.cross, 3))
    at_step(0, 3, (gather.spread, 2))
    at_step(0, 4, (gather.close, 1))
    at_step(0, 7, (gather.close, 3), (gather.cross, 2))
    at_step(1, 1, (gather.close, 2))
    for k in range(3):
        before = [(scatter.line, k - 1, 1)] if k else []
        at_step(k + 1, 0, *before, (scatter.diagonal, k, 0), (scatter.diagonal, k, 1))
        at_step(k + 1, 1, (scatter.across, k, 0))
        at_step(k + 1, 2, (scatter.across, k, 1))
        at_step(k + 1, 6, (scatter.line, k, 0))

    back = jnp.where(chunk == 0, BACK[0], jnp.where(chunk == 1, BACK[1], jnp.where(chunk == 2, BACK[2], BACK[3])))
    first = p.at()[0] * experts

    def save(k, i):
        src, dst = ((xs, xs_out), (gs, gs_out))[i]
        return pltpu.make_async_copy(src.at[k], dst.at[chunk, k], save_sem.at[i, k])

    def place_rows(j):
        y, x, c = j // 4, (j // 2) % 2, j % 2
        routes = routes_ref[p.block(back, y, x, c)]
        hits = []
        for k in range(experts):
            same = jnp.where(routes == first + k, 1.0, 0.0)
            hits.append(jnp.max(same, axis=0, keepdims=True))
        hit = jnp.concatenate(hits, axis=0)
        before = lax.broadcasted_iota(jnp.int32, (rows, rows), 0) < lax.broadcasted_iota(
            jnp.int32, (rows, rows), 1
        )
        rank = jnp.dot(hit.astype(bf16), jnp.where(before, 1.0, 0.0).astype(bf16), preferred_element_type=f32)
        rank = jnp.where(hit > 0.5, rank.astype(jnp.int32), -1)
        ranks[j] = rank
        hot = slots_of_rows(rank)
        place = one_hot(hot)
        b = j % 2
        rows_x = tx[b]
        logits = dot(router_ref[...], rows_x, ((1,), (1,)))
        powers = jnp.exp(logits - jnp.max(logits, axis=0, keepdims=True))
        weights[...] = powers / jnp.sum(powers, axis=0, keepdims=True)
        chosen = weights[pl.ds(pl.multiple_of(first, experts), experts)]
        gate = jnp.sum(jnp.where(hot, chosen[:, None, :], 0.0), axis=-1, keepdims=True)
        at = pl.ds(j * CAP, CAP)
        gates[:, at] = jnp.broadcast_to(gate, (experts, CAP, 128))
        shape = (experts, CAP, width)
        xs[:, at] = jnp.dot(place, rows_x, preferred_element_type=f32).astype(bf16).reshape(shape)
        gs[:, at] = jnp.dot(place, tg[b], preferred_element_type=f32).astype(bf16).reshape(shape)

    @pl.when(e == 0)
    def _():
        def loads(j):
            at = p.block(back, j // 4, (j // 2) % 2, j % 2)
            b = j % 2
            return (
                pltpu.make_async_copy(x_all.at[at], tx.at[b], load_sem.at[b]),
                pltpu.make_async_copy(g_ref.at[at], tg.at[b], load_sem.at[2 + b]),
            )

        def arrive(j):
            if j % 2:
                for k in range(4):
                    pl.when(chunk == k)(gather.to_core[k][j // 2].wait_recv)
            elif j == 2:
                pl.when(chunk == 0)(functools.partial(gather.cross, 0))
            elif j == 6:

                @pl.when(chunk == 0)
                def _():
                    gather.close(0)
                    gather.spread(1)

        def fetch(j):
            arrive(j)
            for copy in loads(j):
                copy.start()

        fetch(0)
        for j in range(8):
            if j < 7:
                pl.when(chunk > 0)(functools.partial(fetch, j + 1))
            for copy in loads(j):
                copy.wait()
            place_rows(j)
            if j < 7:
                pl.when(chunk == 0)(functools.partial(fetch, j + 1))
        for k in range(experts):
            save(k, 0).start()
            save(k, 1).start()

    rows_x, rows_g = xs[e], gs[e]
    gain = gates[e][:, :1]
    gate = jnp.dot(rows_x, w_ref[0, 0], preferred_element_type=f32)
    up = jnp.dot(rows_x, w_ref[0, 1], preferred_element_type=f32)
    raw = jnp.dot(rows_g, w_ref[0, 2], preferred_element_type=f32)
    sigma = 1.0 / (1.0 + jnp.exp(-gate))
    silu = gate * sigma
    act = (silu * up).astype(bf16).astype(f32)
    grads[e] = jnp.broadcast_to(jnp.sum(raw * act, axis=-1, keepdims=True), (slots, 128))
    act_gated = (act * gain).astype(bf16)
    act_grad = raw * gain
    gate_low = (act_grad * up * sigma * (1.0 + gate * (1.0 - sigma))).astype(bf16)
    up_low = (act_grad * silu).astype(bf16)
    st_ref[0, 0, 0] = act_gated
    st_ref[0, 0, 1] = gate_low
    st_ref[0, 0, 2] = up_low
    save(e, 0).wait()
    save(e, 1).wait()
    z = dot(gate_low, w_ref[0, 0], ((1,), (1,))) + dot(up_low, w_ref[0, 1], ((1,), (1,)))
    xs[e] = z.astype(bf16)
    gs[e] = dot(act_gated, w_ref[0, 2], ((1,), (1,))).astype(bf16)

    for k in range(3):
        at_step(k + 1, last, (scatter.settle_core, k), *([(scatter.settle, k - 1)] if k else []))

    @pl.when(e == last)
    def _():
        @pl.when(chunk > 0)
        def _():
            pl.semaphore_wait(scatter.free.at[0], 1)

        for pos in (3, 1, 2, 0):
            for c in (1, 0):
                j = pos * 2 + c
                hot = slots_of_rows(ranks[j])
                place = one_hot(hot)
                at = pl.ds(j * CAP, CAP)
                for i, values in enumerate((xs, gs)):
                    flat = values[:, at].reshape(experts * CAP, width)
                    total = dot(place, flat, ((0,), (0,))).astype(bf16)
                    if c:
                        scatter.give[i, pos] = total
                        scatter.to_core(chunk, i, pos).start()
                    elif pos:
                        scatter.stage[lax.rem(chunk, 2), i, pos - 1] = total
                    else:
                        scatter.acc[chunk, i] = total
                zz = lax.rem(p.z + 4 - back, 4)
                yy, xx, cc = lax.rem(p.y + pos // 2, 2), lax.rem(p.x + pos % 2, 2), lax.rem(p.c + c, 2)
                probs.own[cc, xx, yy, zz] = jnp.sum(jnp.where(hot, grads[:, at, :1], 0.0), axis=1)

    @pl.when((chunk == 3) & (e == last))
    def _():
        probs.start()
        scatter.line(2, 1)
        scatter.diagonal(3, 0)
        scatter.diagonal(3, 1)
        probs.over_x()
        scatter.across(3, 0)
        scatter.across(3, 1)
        probs.over_seq()
        gather.finish()
        scatter.line(3, 0)
        scatter.finish(0, grad_out)
        probs.finish(probs_out)
        scatter.line(3, 1)
        scatter.finish(1, sum_out)
        scatter.end()


def mixture_all(routes_all, router_rows, x, g_all, w_expert, collective_id):
    experts, _, width, hidden = w_expert.shape
    rows = x.shape[0]
    slots = 8 * CAP
    struct = jax.ShapeDtypeStruct
    V, S = pltpu.VMEM, pltpu.SemaphoreType.DMA
    slot = struct((4, experts, slots, width), bf16)
    whole = pl.BlockSpec((rows, width), lambda k, e: (0, 0))
    outs = pl.pallas_call(
        mixture_kernel,
        name="mixture",
        grid=(4, experts),
        out_shape=(
            struct((32, rows, width), bf16),
            slot,
            slot,
            struct((4, experts, 3, slots, hidden), bf16),
            struct((rows, width), f32),
            struct((rows, width), f32),
            struct((4, 2, experts, rows), f32),
        ),
        in_specs=[
            pl.BlockSpec(routes_all.shape, lambda k, e: (0, 0, 0)),
            pl.BlockSpec(router_rows.shape, lambda k, e: (0, 0)),
            ANY,
            ANY,
            pl.BlockSpec((1, 3, width, hidden), lambda k, e: (e, 0, 0, 0)),
        ],
        out_specs=(
            ANY,
            ANY,
            ANY,
            pl.BlockSpec((1, 1, 3, slots, hidden), lambda k, e: (k, e, 0, 0, 0)),
            whole,
            whole,
            pl.BlockSpec((4, 2, experts, rows), lambda k, e: (0, 0, 0, 0)),
        ),
        scratch_shapes=[
            V((2, rows, width), bf16), V((2, rows, width), bf16),
            V((experts, slots, width), bf16), V((experts, slots, width), bf16),
            V((experts, slots, 128), f32), V((experts, slots, 128), f32),
            V((8, experts, rows), jnp.int32), V((router_rows.shape[0], rows), f32),
            S((4,)), S((2, experts)),
            *Gather.scratch(), *Scatter.scratch(rows, width), *Probs.scratch((experts, rows)),
        ],
        compiler_params=pltpu.CompilerParams(
            collective_id=collective_id, has_side_effects=True, vmem_limit_bytes=62 << 20,
            dimension_semantics=("arbitrary", "arbitrary"),
        ),
    )(routes_all, router_rows, x, g_all, w_expert)
    return outs[1:]


def weights_kernel(xs_ref, gs_ref, st_ref, wg_ref):
    rows = xs_ref.shape[0] * xs_ref.shape[2]
    width = xs_ref.shape[-1]
    x = xs_ref[...].reshape(rows, width)
    g = gs_ref[...].reshape(rows, width)
    act, gate_low, up_low = (st_ref[:, 0, i].reshape(rows, -1) for i in range(3))
    hidden = act.shape[-1]
    both = dot(x, jnp.concatenate([gate_low, up_low], axis=1), ((0,), (0,)))
    wg_ref[0, 0] = both[:, :hidden]
    wg_ref[0, 1] = both[:, hidden:]
    wg_ref[0, 2] = dot(g, act, ((0,), (0,)))


def weights_all(xs, gs, st):
    chunks, experts, slots, width = xs.shape
    hidden = st.shape[-1]
    row = pl.BlockSpec((chunks, 1, slots, width), lambda e: (0, e, 0, 0))
    return pl.pallas_call(
        weights_kernel,
        name="weights",
        grid=(experts,),
        out_shape=jax.ShapeDtypeStruct((experts, 3, width, hidden), f32),
        in_specs=[row, row, pl.BlockSpec((chunks, 1, 3, slots, hidden), lambda e: (0, e, 0, 0, 0))],
        out_specs=pl.BlockSpec((1, 3, width, hidden), lambda e: (e, 0, 0, 0)),
        compiler_params=pltpu.CompilerParams(vmem_limit_bytes=60 << 20),
        cost_estimate=pl.CostEstimate(
            flops=6 * xs.size * hidden, bytes_accessed=4 * xs.size + 2 * st.size + 12 * experts * width * hidden,
            transcendentals=0,
        ),
    )(xs, gs, st)


class HeadsAttention:
    def __init__(self, hidden, segments, routes, w_in, w_out, w_router, gains, experts):
        seq, batch = 8, 4
        place, b = lax.axis_index("seq"), lax.axis_index("batch")
        self.rows, self.width = hidden.shape
        width = self.width
        self.hs = width // HEADS
        self.hl = HEADS // seq
        cols = self.hl * self.hs
        self.cols = cols
        top = routes.shape[1]
        total = experts * seq
        ints = jnp.concatenate([routes.T, segments[None], jnp.zeros((7, self.rows), jnp.int32)], axis=0)
        small = jnp.concatenate(
            [w_router, gains.T, jnp.zeros((w_router.shape[0], 128 - total - gains.shape[0]), bf16)], axis=1
        )
        hidden_all, w_cols, w_rows, ints, small = gather_first(hidden, w_in, w_out, ints, small, 0)
        length = seq * self.rows
        self.length = length
        self.w_cols = w_cols.reshape(width, 3 * cols)
        self.w_rows = w_rows.reshape(cols, width)
        small = small.reshape(width, 128)
        self.router_all = small[:, :total]
        self.gains_all = small[:, total : total + 4].T.astype(f32)
        self.routes_all = ints[:, :top]
        segment_all = lax.dynamic_slice_in_dim(ints.reshape(seq, batch, -1, self.rows), b, 1, 1)
        segment_all = segment_all[:, 0, top].reshape(length)
        gains_all = self.gains_all
        inputs = hidden_all.reshape(length, width).astype(f32)
        self.first_normal = inputs * rms_scale(inputs)
        normed = (self.first_normal * gains_all[0]).astype(bf16)
        self.normed = normed
        projected = jnp.dot(normed, self.w_cols, preferred_element_type=f32)
        query_raw = projected[:, :cols]
        key_raw = projected[:, cols : 2 * cols]
        squares = jnp.stack([jnp.sum(query_raw * query_raw, -1), jnp.sum(key_raw * key_raw, -1)], 0)
        scales = lax.rsqrt(self.over_heads(squares, 1) / width + epsilon)
        self.query_scale = scales[0][:, None]
        self.key_scale = scales[1][:, None]
        self.query_normal = query_raw * self.query_scale
        self.key_normal = key_raw * self.key_scale
        mine = lax.dynamic_slice_in_dim(gains_all, place * cols, cols, 1)
        self.query_gain, self.key_gain = mine[1], mine[2]
        positions = jnp.arange(length, dtype=jnp.int32)
        self.cosine, self.sine = rope_tables(positions, self.hs)
        shape = (length, self.hl, self.hs)

        def rot(u):
            u = u.reshape(shape)
            return (u * self.cosine + rotate_half(u) * self.sine).astype(bf16)

        self.query = rot(self.query_normal * self.query_gain)
        self.key = rot(self.key_normal * self.key_gain)
        self.value = projected[:, 2 * cols :].astype(bf16).reshape(shape)
        self.allowed = (positions[None, :] <= positions[:, None]) & (
            segment_all[None, :] == segment_all[:, None]
        )
        scores = self.scores()
        top = jnp.max(scores, axis=-1, keepdims=True)
        weights = jnp.exp(scores - top)
        total = jnp.sum(weights, axis=-1, keepdims=True)
        acc = jnp.einsum("hqk,khd->hqd", weights.astype(bf16), self.value, preferred_element_type=f32)
        self.log_total = top + jnp.log(total)
        self.attended = jnp.transpose(acc / total, (1, 0, 2))
        self.attn_low = self.attended.reshape(length, cols).astype(bf16)
        partial = jnp.dot(self.attn_low, self.w_rows, preferred_element_type=f32).astype(bf16)
        self.mixed = scatter_seq(partial.reshape(seq, self.rows, width), 2, f32)

    def over_heads(self, sums, collective_id):
        return sum_seq(sums.reshape(2, -1, 128), collective_id).reshape(2, self.length)

    def scores(self):
        scale = self.hs ** (-0.5)
        scores = jnp.einsum("qhd,khd->hqk", self.query, self.key, preferred_element_type=f32) * scale
        return jnp.where(self.allowed[None], scores, -jnp.inf)

    def back(self, middle_low, router_grad, ffn_gain_grad):
        seq, batch = 8, 4
        length, cols, width = self.length, self.cols, self.width
        scale = self.hs ** (-0.5)
        shape = (length, self.hl, self.hs)
        grad_all = lax.all_gather(middle_low, "seq", axis=0, tiled=True)
        out_grad = dot(self.attn_low, grad_all, ((0,), (0,))).astype(bf16)
        attn_grad = dot(grad_all, self.w_rows, ((1,), (1,))).astype(bf16).reshape(shape)
        delta = jnp.sum(attn_grad.astype(f32) * self.attended, axis=-1)
        probs = jnp.exp(self.scores() - self.log_total)
        prob_grad = jnp.einsum("qhd,khd->hqk", attn_grad, self.value, preferred_element_type=f32)
        score_grad = (probs * (prob_grad - delta.T[..., None])).astype(bf16)
        query_grad = jnp.einsum("hqk,khd->qhd", score_grad, self.key, preferred_element_type=f32) * scale
        key_grad = jnp.einsum("hqk,qhd->khd", score_grad, self.query, preferred_element_type=f32) * scale
        value_grad = jnp.einsum("hqk,qhd->khd", probs.astype(bf16), attn_grad, preferred_element_type=f32)

        def rot_back(u):
            return (u * self.cosine - rotate_half(u * self.sine)).reshape(length, cols)

        query_norm_grad = rot_back(query_grad)
        key_norm_grad = rot_back(key_grad)
        query_gain_grad = jnp.sum(query_norm_grad * self.query_normal, axis=0)
        key_gain_grad = jnp.sum(key_norm_grad * self.key_normal, axis=0)
        query_scaled = query_norm_grad * self.query_gain
        key_scaled = key_norm_grad * self.key_gain
        dots = jnp.stack(
            [jnp.sum(query_scaled * self.query_normal, -1), jnp.sum(key_scaled * self.key_normal, -1)], 0
        )
        means = self.over_heads(dots, 4) / width
        query_raw_grad = self.query_scale * (query_scaled - self.query_normal * means[0][:, None])
        key_raw_grad = self.key_scale * (key_scaled - self.key_normal * means[1][:, None])
        projected_grad = jnp.concatenate(
            [query_raw_grad, key_raw_grad, value_grad.reshape(length, cols)], axis=1
        ).astype(bf16)
        partial = dot(projected_grad, self.w_cols, ((1,), (1,)))
        attn_gain_grad = jnp.sum(partial * self.first_normal, axis=0)
        in_grad = dot(self.normed, projected_grad, ((0,), (0,))).astype(bf16)
        own = width // (seq * batch)

        lane = jnp.arange(router_grad.shape[1])
        mine = jnp.arange(seq)[:, None] == lax.axis_index("seq")
        total = self.router_all.shape[1]
        small = router_grad.reshape(seq, cols, -1)
        for n, value in enumerate((attn_gain_grad, query_gain_grad, key_gain_grad, ffn_gain_grad)):
            value = jnp.where(mine, value[None], 0.0) if n in (1, 2) else value.reshape(seq, cols)
            small = small + jnp.where(lane == total + n, value[:, :, None], 0.0)
        normed_grad, in_shard, out_shard, small = scatter_last(
            partial.astype(bf16).reshape(seq, self.rows, width),
            in_grad.reshape(seq, 2, 2, own, 3 * cols),
            out_grad.reshape(2, 2, own, width),
            small.reshape(4, 2, 2, 2, own, -1),
            5,
        )
        return normed_grad, in_shard, out_shard, small[:, :total], small[:, total : total + 4].T


def experts_by_tokens(ffn_in, cotangent_all, routes_all, w_expert, router_all):
    rows, width = ffn_in.shape
    xs, gs, factors, ffn_in_grad, mixture, probs = mixture_all(
        routes_all, router_all.T, ffn_in, cotangent_all.reshape(32, rows, width), w_expert, 6
    )
    prob_grad = probs.reshape(-1, rows).T
    return mixture, ffn_in_grad, prob_grad, weights_all(xs, gs, factors)


class TokensAttention:
    def __init__(self, hidden, segment_all, w_in, w_out, gains_all):
        place = lax.axis_index("seq")
        rows, width = hidden.shape
        self.rows, self.width = rows, width
        self.hs = width // HEADS
        self.sources = w_in, w_out
        self.gather_weights(w_in, w_out)
        inputs = hidden.astype(f32)
        self.normed = (inputs * rms_scale(inputs) * gains_all[0]).astype(bf16)
        projected = jnp.dot(self.normed, self.in_all, preferred_element_type=f32)
        query_raw = projected[:, :width]
        key_raw = projected[:, width : 2 * width]
        self.query_scale = rms_scale(query_raw)
        self.query_normal = query_raw * self.query_scale
        self.key_scale = rms_scale(key_raw)
        self.key_normal = key_raw * self.key_scale
        self.query_gain, self.key_gain = gains_all[1], gains_all[2]
        self.positions = place * rows + jnp.arange(rows, dtype=jnp.int32)
        self.cosine, self.sine = rope_tables(self.positions, self.hs)
        shape = (rows, HEADS, self.hs)

        def rot(u):
            u = u.reshape(shape)
            return (u * self.cosine + rotate_half(u) * self.sine).astype(bf16)

        self.query = rot(self.query_normal * self.query_gain)
        key = rot(self.key_normal * self.key_gain).reshape(rows, width)
        value = projected[:, 2 * width :].astype(bf16)
        self.kept = key, value
        self.gather_keys(key, value)
        self.segment_all = segment_all
        self.segment_own = lax.dynamic_slice_in_dim(segment_all, place * rows, rows, 0)
        length = self.key_all.shape[0]
        scores = self.scores(self.key_all.reshape(length, HEADS, self.hs), segment_all, 0)
        top = jnp.max(scores, axis=-1, keepdims=True)
        weights = jnp.exp(scores - top)
        total = jnp.sum(weights, axis=-1, keepdims=True)
        acc = jnp.einsum(
            "hqk,khd->hqd",
            weights.astype(bf16),
            self.value_all.reshape(length, HEADS, self.hs),
            preferred_element_type=f32,
        )
        self.log_total = top + jnp.log(total)
        self.attended = jnp.transpose(acc / total, (1, 0, 2))
        self.attn_low = self.attended.reshape(rows, width).astype(bf16)
        self.mixed = jnp.dot(self.attn_low, self.out_all, preferred_element_type=f32)

    def gather_weights(self, w_in, w_out):
        self.in_all = lax.all_gather(w_in, BOTH, axis=0, tiled=True)
        self.out_all = lax.all_gather(w_out, BOTH, axis=0, tiled=True)

    def gather_keys(self, key, value):
        self.key_all = lax.all_gather(key, "seq", axis=0, tiled=True)
        self.value_all = lax.all_gather(value, "seq", axis=0, tiled=True)

    def scores(self, key, segment, start):
        scale = self.hs ** (-0.5)
        scores = jnp.einsum("qhd,khd->hqk", self.query, key, preferred_element_type=f32) * scale
        key_positions = start + jnp.arange(key.shape[0], dtype=jnp.int32)
        allowed = (key_positions[None, :] <= self.positions[:, None]) & (
            segment[None, :] == self.segment_own[:, None]
        )
        return jnp.where(allowed[None], scores, -jnp.inf)

    def back(self, middle_low, router_grad, ffn_gain_grad):
        again = lax.optimization_barrier((middle_low, *self.sources, *self.kept))
        middle_low = again[0]
        self.gather_weights(*again[1:3])
        self.gather_keys(*again[3:])
        rows, width = self.rows, self.width
        scale = self.hs ** (-0.5)
        out_grad = dot(self.attn_low, middle_low, ((0,), (0,))).astype(bf16)
        out_shard = lax.psum_scatter(out_grad, BOTH, scatter_dimension=0, tiled=True).astype(f32)
        attn_grad = dot(middle_low, self.out_all, ((1,), (1,))).astype(bf16).reshape(rows, HEADS, self.hs)
        delta = jnp.sum(attn_grad.astype(f32) * self.attended, axis=-1).T
        length = self.key_all.shape[0]
        block = min(512, length)
        count = length // block

        def step(query_grad, item):
            key, value, segment, start = item
            probs = jnp.exp(self.scores(key, segment, start) - self.log_total)
            prob_grad = jnp.einsum("qhd,khd->hqk", attn_grad, value, preferred_element_type=f32)
            score_grad = (probs * (prob_grad - delta[..., None])).astype(bf16)
            query_grad = (
                query_grad + jnp.einsum("hqk,khd->qhd", score_grad, key, preferred_element_type=f32) * scale
            )
            key_grad = jnp.einsum("hqk,qhd->khd", score_grad, self.query, preferred_element_type=f32) * scale
            value_grad = jnp.einsum("hqk,qhd->khd", probs.astype(bf16), attn_grad, preferred_element_type=f32)
            return query_grad, jnp.concatenate(
                [key_grad.reshape(block, width), value_grad.reshape(block, width)], axis=1
            ).astype(bf16)

        query_grad, terms = lax.scan(
            step,
            jnp.zeros((rows, HEADS, self.hs), f32),
            (
                self.key_all.reshape(count, block, HEADS, self.hs),
                self.value_all.reshape(count, block, HEADS, self.hs),
                self.segment_all.reshape(count, block),
                jnp.arange(count, dtype=jnp.int32) * block,
            ),
        )
        kv_grad = lax.psum_scatter(
            terms.reshape(length, 2 * width), "seq", scatter_dimension=0, tiled=True
        ).astype(f32)
        key_grad = kv_grad[:, :width].reshape(rows, HEADS, self.hs)

        def rot_back(u):
            return (u * self.cosine - rotate_half(u * self.sine)).reshape(rows, width)

        query_norm_grad = rot_back(query_grad)
        key_norm_grad = rot_back(key_grad)
        query_gain_grad = jnp.sum(query_norm_grad * self.query_normal, axis=0)
        key_gain_grad = jnp.sum(key_norm_grad * self.key_normal, axis=0)
        query_raw_grad = norm_back(query_norm_grad, self.query_normal, self.query_scale, self.query_gain)
        key_raw_grad = norm_back(key_norm_grad, self.key_normal, self.key_scale, self.key_gain)
        projected_grad = jnp.concatenate([query_raw_grad, key_raw_grad, kv_grad[:, width:]], axis=1).astype(bf16)
        in_grad = dot(self.normed, projected_grad, ((0,), (0,))).astype(bf16)
        in_shard = lax.psum_scatter(in_grad, BOTH, scatter_dimension=0, tiled=True).astype(f32)
        normed_grad = dot(projected_grad, self.in_all, ((1,), (1,)))
        pair = lax.psum_scatter(
            jnp.stack([query_gain_grad, key_gain_grad], 1), BOTH, scatter_dimension=0, tiled=True
        )
        return normed_grad, in_shard, out_shard, router_grad, pair


def expert_math(slots, grads, gate_slot, w_expert):
    w_gate, w_up, w_down = w_expert[:, 0], w_expert[:, 1], w_expert[:, 2]
    gate = jnp.einsum("esd,edf->esf", slots, w_gate, preferred_element_type=f32)
    up = jnp.einsum("esd,edf->esf", slots, w_up, preferred_element_type=f32)
    sigma = jax.nn.sigmoid(gate)
    silu = gate * sigma
    act = (silu * up).astype(bf16).astype(f32)
    act_gated = (act * gate_slot).astype(bf16)
    act_raw = jnp.einsum("esd,edf->esf", grads, w_down, preferred_element_type=f32)
    gate_grad = jnp.sum(act_raw * act, axis=-1)
    act_grad = act_raw * gate_slot
    gate_low = (act_grad * up * sigma * (1.0 + gate * (1.0 - sigma))).astype(bf16)
    up_low = (act_grad * silu).astype(bf16)
    slot_grad = (
        jnp.einsum("esf,edf->esd", gate_low, w_gate, preferred_element_type=f32)
        + jnp.einsum("esf,edf->esd", up_low, w_up, preferred_element_type=f32)
    ).astype(bf16)
    result = jnp.einsum("esf,edf->esd", act_gated, w_down, preferred_element_type=f32).astype(bf16)
    expert_grad = jnp.stack(
        [
            jnp.einsum("esd,esf->edf", slots, gate_low, preferred_element_type=f32),
            jnp.einsum("esd,esf->edf", slots, up_low, preferred_element_type=f32),
            jnp.einsum("esd,esf->edf", grads, act_gated, preferred_element_type=f32),
        ],
        axis=1,
    )
    return result, slot_grad, gate_grad, expert_grad


def slot_places(hit):
    count = hit.astype(jnp.int32)
    rank = jnp.where(hit, jnp.cumsum(count, axis=1) - count, -1)
    return rank[:, :, :, None] == jnp.arange(CAP, dtype=jnp.int32)


def experts_by_slots(ffn_in, cotangent, routes, w_expert, router_all):
    seq, batch = lax.axis_size("seq"), lax.axis_size("batch")
    experts = w_expert.shape[0]
    total = experts * seq
    rows, width = ffn_in.shape
    hit = jnp.any(routes[:, :, None] == jnp.arange(total, dtype=jnp.int32), axis=1)[None]
    hot = slot_places(hit)[0]
    place_hot = hot.astype(bf16).reshape(rows, total * CAP)
    router = jax.nn.softmax(jnp.dot(ffn_in, router_all, preferred_element_type=f32), axis=-1)
    gate_slot = jnp.sum(jnp.where(hot, router[:, :, None], 0.0), axis=0).reshape(seq, experts, CAP, 1)

    def there(values):
        values = lax.all_to_all(values, "seq", split_axis=0, concat_axis=0, tiled=True)
        values = lax.all_gather(values, "batch", axis=0, tiled=True)
        values = jnp.transpose(values, (1, 0, 2, 3))
        return values.reshape(experts, batch * seq * CAP, values.shape[-1])

    def back(values):
        values = values.reshape(experts, batch * seq, CAP, values.shape[-1])
        values = jnp.transpose(values, (1, 0, 2, 3))
        values = lax.psum_scatter(values, "batch", scatter_dimension=0, tiled=True)
        values = lax.all_to_all(values, "seq", split_axis=0, concat_axis=0, tiled=True)
        return values.reshape(total * CAP, values.shape[-1])

    def slots_of(tokens):
        slots = dot(place_hot, tokens, ((0,), (0,))).astype(bf16)
        return there(slots.reshape(seq, experts, CAP, width))

    def tokens_of(slots):
        return jnp.dot(place_hot, back(slots), preferred_element_type=f32)

    result, slot_grad, gate_grad, expert_grad = expert_math(
        slots_of(ffn_in), slots_of(cotangent), there(gate_slot), w_expert
    )
    gate_grad = back(gate_grad[..., None]).reshape(1, total, CAP)
    prob_grad = jnp.sum(jnp.where(hot, gate_grad, 0.0), axis=-1)
    return tokens_of(result), tokens_of(slot_grad), prob_grad, expert_grad


def local(hidden, segments, routes, w_in, w_out, w_router, gains, w_expert, cotangent):
    seq = lax.axis_size("seq")
    total_experts = w_expert.shape[0] * seq
    by_heads = seq == 8 and lax.axis_size("batch") == 4

    inputs = hidden[0].astype(f32)
    first_scale = rms_scale(inputs)
    first_normal = inputs * first_scale
    if by_heads:
        cotangent_all = lax.all_gather(cotangent[0], BOTH, axis=0, tiled=True)
        attention = HeadsAttention(
            hidden[0], segments[0], routes[0], w_in, w_out, w_router, gains, w_expert.shape[0]
        )
        gains_all, router_all = attention.gains_all, attention.router_all
    else:
        small = lax.all_gather(jnp.concatenate([w_router, gains.T], axis=1), BOTH, axis=0, tiled=True)
        router_all = small[:, :total_experts]
        gains_all = small[:, total_experts:].T.astype(f32)
        segment_all = lax.all_gather(segments[0], "seq", axis=0, tiled=True)
        attention = TokensAttention(hidden[0], segment_all, w_in, w_out, gains_all)

    middle = inputs + attention.mixed
    second_scale = rms_scale(middle)
    second_normal = middle * second_scale
    ffn_in = (second_normal * gains_all[3]).astype(bf16)
    if by_heads:
        mixture, ffn_in_grad, prob_grad, expert_grad = experts_by_tokens(
            ffn_in, cotangent_all, attention.routes_all, w_expert, router_all
        )
    else:
        mixture, ffn_in_grad, prob_grad, expert_grad = experts_by_slots(
            ffn_in, cotangent[0], routes[0], w_expert, router_all
        )
    output = middle + mixture

    grad_out = cotangent[0].astype(f32)
    router = jax.nn.softmax(jnp.dot(ffn_in, router_all, preferred_element_type=f32), axis=-1)
    logit_grad = router * (prob_grad - jnp.sum(router * prob_grad, axis=-1, keepdims=True))
    logit_low = logit_grad.astype(bf16)
    if by_heads:
        wide = jnp.pad(logit_low, ((0, 0), (0, 128 - total_experts)))
        router_grad = dot(ffn_in, wide, ((0,), (0,)))
    else:
        router_grad = dot(ffn_in, logit_low, ((0,), (0,)))
    ffn_in_grad = ffn_in_grad + dot(logit_low, router_all, ((1,), (1,)))
    ffn_gain_grad = jnp.sum(ffn_in_grad * second_normal, axis=0)
    middle_grad = grad_out + norm_back(ffn_in_grad, second_normal, second_scale, gains_all[3])
    normed_grad, in_shard, out_shard, router_shard, gains_shard = attention.back(
        middle_grad.astype(bf16), router_grad, ffn_gain_grad
    )
    if not by_heads:
        attn_gain_grad = jnp.sum(normed_grad * first_normal, axis=0)
        ends = jnp.stack([attn_gain_grad, ffn_gain_grad], axis=1)
        sums = lax.psum_scatter(
            jnp.concatenate([router_shard, ends], axis=1), BOTH, scatter_dimension=0, tiled=True
        )
        router_shard, ends = sums[:, :total_experts], sums[:, total_experts:]
        gains_shard = jnp.stack([ends[:, 0], gains_shard[:, 0], gains_shard[:, 1], ends[:, 1]], axis=0)
    input_grad = middle_grad + norm_back(normed_grad, first_normal, first_scale, gains_all[0])
    return (
        output.astype(bf16)[None],
        input_grad[None],
        in_shard,
        out_shard,
        router_shard,
        gains_shard,
        expert_grad,
    )


def solution(mesh):
    placed = (
        P("batch", "seq", None),
        P("batch", "seq"),
        P("batch", "seq", None),
        P(BOTH, None),
        P(BOTH, None),
        P(BOTH, None),
        P(None, BOTH),
        P("seq", None, None, "batch"),
        P("batch", "seq", None),
    )
    return jax.shard_map(
        local,
        mesh=mesh,
        in_specs=placed,
        out_specs=(
            P("batch", "seq", None),
            P("batch", "seq", None),
            P(BOTH, None),
            P(BOTH, None),
            P(BOTH, None),
            P(None, BOTH),
            P("seq", None, None, "batch"),
        ),
        check_vma=False,
    )
```

```python
import functools

import jax
import jax.numpy as jnp
from jax import lax
from jax.experimental import pallas as pl
from jax.experimental.pallas import tpu as pltpu
from jax.sharding import PartitionSpec as P

HEADS = 16
CAP = 32
epsilon = 1e-05
BOTH = ("seq", "batch")
f32 = jnp.float32
bf16 = jnp.bfloat16
MESH = pl.DeviceIdType.MESH


def rms_scale(values):
    return lax.rsqrt(jnp.mean(values * values, axis=-1, keepdims=True) + epsilon)


def rotate_half(values):
    half = values.shape[-1] // 2
    return jnp.concatenate([-values[..., half:], values[..., :half]], axis=-1)


def rope_tables(positions, head_size):
    steps = jnp.arange(head_size // 2, dtype=f32)
    freqs = jnp.exp(steps * (-2.0 * jnp.log(10000.0) / head_size))
    angles = positions.astype(f32)[:, None] * freqs[None, :]
    angles = jnp.concatenate([angles, angles], axis=-1)
    return (jnp.cos(angles)[:, None, :], jnp.sin(angles)[:, None, :])


def norm_back(grad_out, normal, scale, gain):
    scaled = grad_out * gain
    return scale * (scaled - normal * jnp.mean(scaled * normal, axis=-1, keepdims=True))


def dot(a, b, dims):
    return lax.dot_general(a, b, (dims, ((), ())), preferred_element_type=f32)


ANY = pl.BlockSpec(memory_space=pl.ANY)
WHOLE = pl.BlockSpec(memory_space=pltpu.VMEM)


class Place:
    def __init__(self):
        s, b = lax.axis_index("seq"), lax.axis_index("batch")
        self.z, self.y = s // 2, lax.rem(s, 2)
        self.x, self.c = b // 2, lax.rem(b, 2)

    def at(self, r=0, y=0, x=0, c=0):
        z = lax.rem(self.z + r, 4)
        yy = 1 - self.y if y else self.y
        xx = 1 - self.x if x else self.x
        cc = 1 - self.c if c else self.c
        return (z * 2 + yy, xx * 2 + cc)

    def index(self, r=0, y=0, x=0, c=0):
        s, b = self.at(r, y, x, c)
        return s * 4 + b


def barrier(peers):
    sem = pltpu.get_barrier_semaphore()
    for peer in peers:
        pl.semaphore_signal(sem, inc=1, device_id=peer, device_id_type=MESH)
    pl.semaphore_wait(sem, len(peers))


class Sends:
    def __init__(self, send_sem, recv_sem):
        self.send_sem, self.recv_sem, self.copies = send_sem, recv_sem, []

    def start(self, src, dst, peer):
        k = len(self.copies)
        copy = pltpu.make_async_remote_copy(
            src_ref=src,
            dst_ref=dst,
            send_sem=self.send_sem.at[k],
            recv_sem=self.recv_sem.at[k],
            device_id=peer,
            device_id_type=MESH,
        )
        copy.start()
        self.copies.append(copy)
        return copy

    def finish(self):
        for copy in self.copies:
            copy.wait_send()


def add_rows(dst, src, start, rows):
    step = 16

    def body(i, _):
        at = pl.ds(pl.multiple_of(start + i * step, step), step)
        dst[at] = (dst[at].astype(f32) + src[at].astype(f32)).astype(dst.dtype)
        return 0

    lax.fori_loop(0, rows // step, body, 0)


def call(kernel, name, collective_id, out_shape, in_specs, out_specs, scratch, copies, local=1, vmem=32):
    return pl.pallas_call(
        kernel,
        name=name,
        out_shape=out_shape,
        in_specs=in_specs,
        out_specs=out_specs,
        scratch_shapes=[
            *scratch,
            pltpu.SemaphoreType.DMA((copies,)),
            pltpu.SemaphoreType.DMA((copies,)),
            pltpu.SemaphoreType.DMA((local,)),
        ],
        compiler_params=pltpu.CompilerParams(
            collective_id=collective_id, has_side_effects=True, vmem_limit_bytes=vmem << 20
        ),
    )


Z_ORDER = (1, 3, 2)


def gather_first_kernel(
    h_ref, wi_ref, wo_ref, ints_ref, small_ref,
    h_out, wi_out, wo_out, ints_out, small_out,
    ints, small, send_sem, recv_sem, own_sem,
):
    p = Place()
    seq, b = p.at()
    x, c = p.x, p.c
    others = [p.at(r, y) for y in (0, 1) for r in range(4) if r or y]
    barrier(others + [p.at(x=1), p.at(c=1)])
    sends = Sends(send_sem, recv_sem)
    owns = [
        pltpu.make_async_copy(h_ref, h_out.at[seq], own_sem.at[0]),
        pltpu.make_async_copy(wi_ref.at[seq], wi_out.at[seq, b], own_sem.at[1]),
        pltpu.make_async_copy(wo_ref, wo_out.at[b], own_sem.at[2]),
    ]
    for own in owns:
        own.start()
    me = p.index()
    pairs = ((ints_ref, ints), (small_ref, small))
    for src, dst in pairs:
        dst[me] = src[...]
    first = [sends.start(dst.at[me], dst.at[me], p.at(c=1)) for _, dst in pairs]
    h_z = {r: sends.start(h_ref, h_out.at[seq], p.at(r)) for r in Z_ORDER}
    h_y = [sends.start(h_ref, h_out.at[seq], p.at(y=1))]
    w_s = {}
    for r, y in ((0, 1), (1, 0), (3, 0), (2, 0), (1, 1), (3, 1), (2, 1)):
        to = p.at(r, y)
        w_s[r, y] = sends.start(wi_ref.at[to[0]], wi_out.at[seq, b], to)
    w_x = [sends.start(wi_ref.at[seq], wi_out.at[seq, b], p.at(x=1))]
    w_c = [sends.start(wi_ref.at[seq], wi_out.at[seq, b], p.at(c=1))]
    o_x = sends.start(wo_ref, wo_out.at[b], p.at(x=1))
    w_c.append(sends.start(wo_ref, wo_out.at[b], p.at(c=1)))
    for copy in first:
        copy.wait_recv()
    base = me - c
    second = [sends.start(dst.at[pl.ds(base, 2)], dst.at[pl.ds(base, 2)], p.at(x=1)) for _, dst in pairs]
    for copy in second:
        copy.wait_recv()
    base = me - b
    third = [sends.start(dst.at[pl.ds(base, 4)], dst.at[pl.ds(base, 4)], p.at(y=1)) for _, dst in pairs]
    for copy in third:
        copy.wait_recv()
    base = p.z * 8
    fourth = [
        sends.start(dst.at[pl.ds(base, 8)], dst.at[pl.ds(base, 8)], p.at(r)) for _, dst in pairs for r in Z_ORDER
    ]
    for r in Z_ORDER:
        h_z[r].wait_recv()
        s = p.at(-r % 4)[0]
        h_y.append(sends.start(h_out.at[s], h_out.at[s], p.at(y=1)))
    for r, y in ((0, 1), (1, 0), (3, 0), (2, 0), (1, 1), (3, 1), (2, 1)):
        w_s[r, y].wait_recv()
        s = p.at(-r % 4, y)[0]
        w_x.append(sends.start(wi_out.at[s, b], wi_out.at[s, b], p.at(x=1)))
        w_c.append(sends.start(wi_out.at[s, b], wi_out.at[s, b], p.at(c=1)))
    bx = p.at(x=1)[1]
    o_x.wait_recv()
    w_c.append(sends.start(wo_out.at[bx], wo_out.at[bx], p.at(c=1)))
    places = [(0, 0), (0, 1), (1, 0), (3, 0), (2, 0), (1, 1), (3, 1), (2, 1)]
    for copy, (r, y) in zip(w_x, places):
        copy.wait_recv()
        s = p.at(-r % 4, y)[0]
        w_c.append(sends.start(wi_out.at[s, bx], wi_out.at[s, bx], p.at(c=1)))
    for copy in fourth + h_y + w_c:
        copy.wait_recv()
    ints_out[...] = ints[...]
    small_out[...] = small[...]
    sends.finish()
    for own in owns:
        own.wait()


def gather_first(hidden, w_in, w_out, ints, small, collective_id):
    own = w_in.shape[0]
    parts = jnp.transpose(w_in.reshape(own, 3, 8, -1), (2, 0, 1, 3)).reshape(8, own, -1)
    struct = jax.ShapeDtypeStruct
    outs = call(
        gather_first_kernel,
        "gather_first",
        collective_id,
        (
            struct((8,) + hidden.shape, bf16),
            struct((8, 4) + parts.shape[1:], bf16),
            struct((4,) + w_out.shape, bf16),
            struct((32,) + ints.shape, ints.dtype),
            struct((32,) + small.shape, small.dtype),
        ),
        [ANY, ANY, ANY, WHOLE, WHOLE],
        (ANY, ANY, ANY, WHOLE, WHOLE),
        [
            pltpu.VMEM((32,) + ints.shape, ints.dtype),
            pltpu.VMEM((32,) + small.shape, small.dtype),
        ],
        2 + 3 + 1 + 7 + 1 + 1 + 1 + 1 + 2 + 2 + 6 + 3 + 7 + 7 + 1 + 8,
        3,
    )(hidden, parts, w_out, ints, small)
    return outs


def scatter_seq_kernel(p_ref, out_ref, acc, ry, rz, send_sem, recv_sem, own_sem):
    p = Place()
    barrier([p.at(1), p.at(2), p.at(3), p.at(y=1)])
    sends = Sends(send_sem, recv_sem)
    order = (2, 1, 3, 0)
    loads, fy, fz = [], [], []
    for n, r in enumerate(order):
        fy.append(sends.start(p_ref.at[p.at(r, 1)[0]], ry.at[n], p.at(y=1)))
        load = pltpu.make_async_copy(p_ref.at[p.at(r)[0]], acc.at[n], own_sem.at[n])
        load.start()
        loads.append(load)
    rows = acc.shape[1]
    for n, r in enumerate(order):
        loads[n].wait()
        fy[n].wait_recv()
        add_rows(acc.at[n], ry.at[n], 0, rows)
        if r:
            fz.append(sends.start(acc.at[n], rz.at[n], p.at(r)))
    for copy in fz:
        copy.wait_recv()

    def total(i, _):
        at = pl.ds(pl.multiple_of(i * 16, 16), 16)
        value = acc[3, at].astype(f32)
        for n in range(3):
            value = value + rz[n, at].astype(f32)
        out_ref[at] = value.astype(out_ref.dtype)
        return 0

    lax.fori_loop(0, rows // 16, total, 0)
    sends.finish()


def scatter_seq(parts, collective_id, dtype=bf16):
    block = parts.shape[1:]
    return call(
        scatter_seq_kernel,
        "scatter_seq",
        collective_id,
        jax.ShapeDtypeStruct(block, dtype),
        [ANY],
        WHOLE,
        [pltpu.VMEM((n,) + block, parts.dtype) for n in (4, 4, 3)],
        7,
        4,
    )(parts)


def sum_seq_kernel(x_ref, out_ref, got, send_sem, recv_sem, own_sem):
    p = Place()
    others = [p.at(r, y) for y in (0, 1) for r in range(4) if r or y]
    barrier(others)
    sends = Sends(send_sem, recv_sem)
    me = p.at()[0]
    got[me] = x_ref[...]
    copies = [sends.start(x_ref, got.at[me], to) for to in others]
    for copy in copies:
        copy.wait_recv()
    total = got[0]
    for n in range(1, 8):
        total = total + got[n]
    out_ref[...] = total
    sends.finish()


def sum_seq(x, collective_id):
    return call(
        sum_seq_kernel,
        "sum_seq",
        collective_id,
        jax.ShapeDtypeStruct(x.shape, x.dtype),
        [WHOLE],
        WHOLE,
        [pltpu.VMEM((8,) + x.shape, x.dtype)],
        7,
    )(x)


def add_blocks(dst, src):
    def body(i, _):
        dst[i] = (dst[i].astype(f32) + src[i].astype(f32)).astype(dst.dtype)
        return 0

    lax.fori_loop(0, dst.shape[0], body, 0)


def scatter_last_kernel(
    n_ref, wi_ref, wo_ref, sm_ref,
    n_out, wi_out, wo_out, sm_out,
    n_acc, n_y, n_z, wi_acc, wi_c, wi_x, wi_got, wo_acc, wo_c, wo_x, sm_acc, sm_c, sm_x, sm_y, sm_z,
    send_sem, recv_sem, own_sem,
):
    p = Place()
    c, x, y, z = p.c, p.x, p.y, p.z
    others = [p.at(r, yy) for yy in (0, 1) for r in range(4) if r or yy]
    barrier(others + [p.at(x=1), p.at(c=1)])
    sends = Sends(send_sem, recv_sem)
    core, nbr_x, nbr_y = p.at(c=1), p.at(x=1), p.at(y=1)
    order = (2, 1, 3, 0)
    loads = [
        pltpu.make_async_copy(wi_ref.at[:, 1 - x, c], wi_acc.at[0], own_sem.at[4]),
        pltpu.make_async_copy(wi_ref.at[:, x, c], wi_acc.at[1], own_sem.at[7]),
        pltpu.make_async_copy(wo_ref.at[:, c], wo_acc, own_sem.at[5]),
        pltpu.make_async_copy(sm_ref.at[:, :, :, c], sm_acc, own_sem.at[6]),
    ]
    for load in loads:
        load.start()
    wi1 = sends.start(wi_ref.at[:, 1 - x, 1 - c], wi_c.at[0], core)
    sm1 = sends.start(sm_ref.at[:, :, :, 1 - c], sm_c, core)
    wo1 = sends.start(wo_ref.at[:, 1 - c], wo_c, core)
    wi2 = sends.start(wi_ref.at[:, x, 1 - c], wi_c.at[1], core)
    fy, n_loads, fz = [], [], []
    for n, r in enumerate(order):
        fy.append(sends.start(n_ref.at[p.at(r, 1)[0]], n_y.at[n], nbr_y))
        load = pltpu.make_async_copy(n_ref.at[p.at(r)[0]], n_acc.at[n], own_sem.at[n])
        load.start()
        n_loads.append(load)
    for load in loads:
        load.wait()
    wi1.wait_recv()
    add_blocks(wi_acc.at[0], wi_c.at[0])
    wi3 = sends.start(wi_acc.at[0], wi_x, nbr_x)
    sm1.wait_recv()
    sm_acc[...] = sm_acc[...] + sm_c[...]
    sm2 = sends.start(sm_acc.at[:, :, 1 - x], sm_x, nbr_x)
    wo1.wait_recv()
    add_blocks(wo_acc, wo_c)
    wo2 = sends.start(wo_acc.at[1 - x], wo_x, nbr_x)
    wi2.wait_recv()
    add_blocks(wi_acc.at[1], wi_c.at[1])
    rows = n_acc.shape[1]
    for n, r in enumerate(order):
        n_loads[n].wait()
        fy[n].wait_recv()
        add_rows(n_acc.at[n], n_y.at[n], 0, rows)
        if r:
            fz.append(sends.start(n_acc.at[n], n_z.at[n], p.at(r)))
    wi3.wait_recv()
    add_blocks(wi_acc.at[1], wi_x)
    me = p.at()[0]
    wi4 = []
    for r, yy in ((0, 1), (1, 0), (3, 0), (2, 0), (1, 1), (3, 1), (2, 1)):
        to = p.at(r, yy)
        wi4.append(sends.start(wi_acc.at[1, to[0]], wi_got.at[me], to))
    sm2.wait_recv()
    sm_acc[:, :, x] = sm_acc[:, :, x] + sm_x[...]
    sm3 = sends.start(sm_acc.at[:, 1 - y, x], sm_y, nbr_y)
    wi_got[me] = wi_acc[1, me]
    wo2.wait_recv()
    wo_out[...] = wo_acc[x].astype(f32) + wo_x[...].astype(f32)
    sm3.wait_recv()
    sm_acc[:, y, x] = sm_acc[:, y, x] + sm_y[...]
    sm4 = [
        sends.start(sm_acc.at[lax.rem(z + r, 4), y, x], sm_z.at[n], p.at(r)) for n, r in enumerate(Z_ORDER)
    ]
    for copy in wi4:
        copy.wait_recv()
    seq, _, columns = wi_got.shape
    part = columns // 3
    for s in range(seq):
        for i in range(3):
            value = wi_got[s, :, i * part : (i + 1) * part].astype(f32)
            wi_out[:, (i * seq + s) * part : (i * seq + s + 1) * part] = value
    for copy in sm4:
        copy.wait_recv()
    sm_out[...] = sm_acc[z, y, x] + sm_z[0] + sm_z[1] + sm_z[2]
    for copy in fz:
        copy.wait_recv()

    def total(i, _):
        at = pl.ds(pl.multiple_of(i * 16, 16), 16)
        value = n_acc[3, at].astype(f32)
        for n in range(3):
            value = value + n_z[n, at].astype(f32)
        n_out[at] = value
        return 0

    lax.fori_loop(0, rows // 16, total, 0)
    sends.finish()


def scatter_last(normed, w_in, w_out, small, collective_id):
    struct = jax.ShapeDtypeStruct
    nb, ib, ob, sb = normed.shape[1:], w_in.shape[3:], w_out.shape[2:], small.shape[4:]
    V = pltpu.VMEM
    seq = w_in.shape[0]
    return call(
        scatter_last_kernel,
        "scatter_last",
        collective_id,
        (struct(nb, f32), struct((ib[0], seq * ib[1]), f32), struct(ob, f32), struct(sb, f32)),
        [ANY] * 4,
        (WHOLE,) * 4,
        [
            V((4,) + nb, bf16), V((4,) + nb, bf16), V((3,) + nb, bf16),
            V((2, seq) + ib, bf16), V((2, seq) + ib, bf16), V((seq,) + ib, bf16), V((seq,) + ib, bf16),
            V((2,) + ob, bf16), V((2,) + ob, bf16), V(ob, bf16),
            V((4, 2, 2) + sb, f32), V((4, 2, 2) + sb, f32), V((4, 2) + sb, f32), V((4,) + sb, f32), V((3,) + sb, f32),
        ],
        4 + 4 + 3 + 1 + 1 + 1 + 7 + 1 + 3,
        8,
        48,
    )(normed, w_in, w_out, small)


def slots_of_rows(ranks):
    experts, rows = ranks.shape
    slot = lax.broadcasted_iota(jnp.int32, (experts, CAP, rows), 1)
    return ranks[:, None, :] == slot


def one_hot(hot):
    experts, _, rows = hot.shape
    return jnp.where(hot, 1.0, 0.0).reshape(experts * CAP, rows).astype(bf16)


BACK = (1, 2, 3, 0)


class Flip(Place):
    def block(self, r=0, y=0, x=0, c=0):
        z = lax.rem(self.z + 4 - r, 4)
        yy, xx, cc = lax.rem(self.y + y, 2), lax.rem(self.x + x, 2), lax.rem(self.c + c, 2)
        return ((z * 2 + yy) * 2 + xx) * 2 + cc


def remote(src, dst, send, recv, peer):
    return pltpu.make_async_remote_copy(
        src_ref=src, dst_ref=dst, send_sem=send, recv_sem=recv, device_id=peer, device_id_type=MESH
    )


class Gather:
    @staticmethod
    def scratch():
        S = pltpu.SemaphoreType.DMA
        return [S((34,)), S((34,)), S]

    def __init__(self, p, x_ref, x_all, refs):
        send, recv, own_sem = refs
        rows = x_ref.shape[0]
        A, B = pl.ds(0, rows // 2), pl.ds(rows // 2, rows // 2)
        nx, ny, core = p.at(x=1), p.at(y=1), p.at(c=1)
        self.peers = [p.at(1), p.at(2), p.at(3), nx, ny, core]
        mine = p.block()
        self.own = pltpu.make_async_copy(x_ref, x_all.at[mine], own_sem)
        count = [0]

        def copy(src, dst, peer):
            i = count[0]
            count[0] += 1
            return remote(src, dst, send.at[i], recv.at[i], peer)

        self.along, self.to_x, self.to_y, self.by_y, self.by_x, self.to_core = {}, {}, {}, {}, {}, []
        for k, r in enumerate(BACK):
            at, ix, iy, far = p.block(r), p.block(r, x=1), p.block(r, y=1), p.block(r, y=1, x=1)
            src = x_all.at[at] if r else x_ref
            if k < 2:
                self.along[k] = copy(x_ref, x_all.at[mine], p.at(r))
            if k == 2:
                plane = [p.block(0, x=1), p.block(0, y=1), p.block(0, y=1, x=1)]
                self.shift = [copy(x_ref, x_all.at[mine], p.at(r))]
                self.shift += [copy(x_all.at[i], x_all.at[i], p.at(r)) for i in plane]
            else:
                self.to_x[k] = copy(src, x_all.at[at], nx)
                self.to_y[k] = copy(src, x_all.at[at], ny)
                self.by_y[k] = copy(x_all.at[ix, A], x_all.at[ix, A], ny)
                self.by_x[k] = copy(x_all.at[iy, B], x_all.at[iy, B], nx)
            self.to_core.append(
                [copy(src, x_all.at[at], core)] + [copy(x_all.at[i], x_all.at[i], core) for i in (ix, iy, far)]
            )

    def start(self):
        self.own.start()
        self.along[0].start()
        self.own.wait()

    def spread(self, k):
        if k == 2:
            self.shift[0].wait_recv()
            self.to_core[k][0].start()
            return
        if k == 0:
            self.along[0].wait_recv()
            self.along[1].start()
        elif k == 1:
            self.along[1].wait_recv()
            self.shift[0].start()
        self.to_x[k].start()
        self.to_y[k].start()
        self.to_core[k][0].start()

    def cross(self, k):
        if k == 2:
            for n in (1, 2):
                self.shift[n].wait_recv()
                self.to_core[k][n].start()
            return
        self.to_x[k].wait_recv()
        self.by_y[k].start()
        self.to_core[k][1].start()
        self.to_y[k].wait_recv()
        self.by_x[k].start()
        self.to_core[k][2].start()
        if k == 3:
            self.shift[1].start()
            self.shift[2].start()

    def close(self, k):
        if k == 2:
            self.shift[3].wait_recv()
        else:
            self.by_y[k].wait_recv()
            self.by_x[k].wait_recv()
            if k == 3:
                self.shift[3].start()
        self.to_core[k][3].start()

    def finish(self):
        copies = list(self.shift)
        for group in (self.along, self.to_x, self.to_y, self.by_y, self.by_x):
            copies += group.values()
        for group in self.to_core:
            copies += group
        for copy in copies:
            copy.wait_send()


class Scatter:
    @staticmethod
    def scratch(rows, width):
        V, S = pltpu.VMEM, pltpu.SemaphoreType.DMA
        block, half = (rows, width), (rows // 2, width)
        return [
            V((2, 4) + block, bf16), V((2, 2, 3) + block, bf16), V((2, 4) + block, bf16), V((2, 2) + half, bf16),
            V((2, 2) + block, bf16), V((4, 2) + block, bf16), V((3, 2) + block, bf16),
            S((32,)), S((32,)), S((38,)), S((38,)), pltpu.SemaphoreType.REGULAR((5,)),
        ]

    def __init__(self, p, refs):
        self.give, self.stage, self.pair, self.half, self.near, self.acc, self.far = refs[:7]
        self.core_send, self.core_recv, send, recv, self.free = refs[7:]
        self.p = p
        rows = self.give.shape[2]
        self.parts = A, B = pl.ds(0, rows // 2), pl.ds(rows // 2, rows // 2)
        nx, ny = p.at(x=1), p.at(y=1)
        self.core, self.nx, self.ny = p.at(c=1), nx, ny
        count = [0]

        def copy(src, dst, peer):
            i = count[0]
            count[0] += 1
            return remote(src, dst, send.at[i], recv.at[i], peer)

        self.by_y, self.by_x, self.to_x, self.to_y, self.to_z = [], [], [], [], []
        for k in range(4):
            out = [self.stage.at[k % 2, i] for i in (0, 1)]
            self.by_y.append([copy(out[i].at[2, A], self.half.at[i, 0], ny) for i in (0, 1)])
            self.by_x.append([copy(out[i].at[2, B], self.half.at[i, 1], nx) for i in (0, 1)])
            self.to_x.append([copy(out[i].at[0], self.near.at[i, 0], nx) for i in (0, 1)])
            self.to_y.append([copy(out[i].at[1], self.near.at[i, 1], ny) for i in (0, 1)])
            if BACK[k]:
                to = p.at((4 - BACK[k]) % 4)
                self.to_z.append([copy(self.acc.at[k, i], self.far.at[k, i], to) for i in (0, 1)])

    def to_core(self, k, i, pos):
        at = k * 8 + i * 4 + pos
        return remote(
            self.give.at[i, pos], self.pair.at[i, pos], self.core_send.at[at], self.core_recv.at[at], self.core
        )

    def add(self, dst, terms):
        step = 32

        def body(i, _):
            at = pl.ds(pl.multiple_of(i * step, step), step)
            if len(terms) == 2 and dst.dtype == bf16:
                dst[at] = terms[0][at] + terms[1][at]
                return 0
            value = terms[0][at].astype(f32)
            for term in terms[1:]:
                value = value + term[at].astype(f32)
            dst[at] = value.astype(dst.dtype)
            return 0

        lax.fori_loop(0, dst.shape[0] // step, body, 0)

    def signal(self, n, peer):
        pl.semaphore_signal(self.free.at[n], inc=1, device_id=peer, device_id_type=MESH)

    def diagonal(self, k, i):
        if k and not i:
            pl.semaphore_wait(self.free.at[1], 1)
            pl.semaphore_wait(self.free.at[2], 1)
        self.to_core(k, i, 3).wait_recv()
        at = self.stage.at[k % 2, i, 2]
        self.add(at, [at, self.pair.at[i, 3]])
        self.by_y[k][i].start()
        self.by_x[k][i].start()

    def across(self, k, i):
        A, B = self.parts
        for_x, for_y = self.stage.at[k % 2, i, 0], self.stage.at[k % 2, i, 1]
        if k and not i:
            pl.semaphore_wait(self.free.at[3], 1)
            pl.semaphore_wait(self.free.at[4], 1)
        self.to_core(k, i, 1).wait_recv()
        self.add(for_x.at[B], [for_x.at[B], self.pair.at[i, 1, B]])
        self.by_y[k][i].wait_recv()
        self.add(for_x.at[A], [for_x.at[A], self.pair.at[i, 1, A], self.half.at[i, 0]])
        self.to_x[k][i].start()
        self.to_core(k, i, 2).wait_recv()
        self.add(for_y.at[A], [for_y.at[A], self.pair.at[i, 2, A]])
        self.by_x[k][i].wait_recv()
        self.add(for_y.at[B], [for_y.at[B], self.pair.at[i, 2, B], self.half.at[i, 1]])
        self.to_y[k][i].start()
        self.to_core(k, i, 0).wait_recv()
        self.add(self.acc.at[k, i], [self.acc.at[k, i], self.pair.at[i, 0]])
        if k < 3 and i:
            self.signal(0, self.core)
            self.signal(1, self.nx)
            self.signal(2, self.ny)

    def line(self, k, i):
        self.to_x[k][i].wait_recv()
        self.to_y[k][i].wait_recv()
        self.add(self.acc.at[k, i], [self.acc.at[k, i], self.near.at[i, 0], self.near.at[i, 1]])
        if BACK[k]:
            self.to_z[k][i].start()
        if k < 3 and i:
            self.signal(3, self.nx)
            self.signal(4, self.ny)

    def settle_core(self, k):
        for i in (0, 1):
            for pos in range(4):
                self.to_core(k, i, pos).wait_send()

    def settle(self, k):
        for i in (0, 1):
            for copies in (self.by_y, self.by_x, self.to_x, self.to_y):
                copies[k][i].wait_send()

    def finish(self, i, out_ref):
        for copies in self.to_z:
            copies[i].wait_recv()
        self.add(out_ref, [self.acc.at[3, i]] + [self.far.at[n, i] for n in range(3)])

    def end(self):
        self.settle_core(3)
        self.settle(2)
        self.settle(3)
        for copies in self.to_z:
            for copy in copies:
                copy.wait_send()


class Probs:
    TURNS = ((0, 1), (1, 0), (3, 0), (2, 0), (1, 1), (3, 1), (2, 1))

    @staticmethod
    def scratch(block):
        V, S = pltpu.VMEM, pltpu.SemaphoreType.DMA
        return [
            V((2, 2, 2, 4) + block, f32), V((2, 2, 4) + block, f32), V((2, 4) + block, f32), V((2, 2, 4) + block, f32),
            V((2, 4) + block, f32), V((4, 2) + block, f32), S((9,)), S((9,)),
        ]

    def __init__(self, p, refs):
        self.p = p
        self.own, self.sum_x, self.sum_s, self.r1, self.r2, self.got, send, recv = refs
        self.peers = [p.at(r, y) for r, y in self.TURNS]
        self.first = remote(self.own.at[1 - p.c], self.r1, send.at[0], recv.at[0], p.at(c=1))
        self.second = remote(self.sum_x.at[1 - p.x], self.r2, send.at[1], recv.at[1], p.at(x=1))
        self.third = []
        for n, (r, y) in enumerate(self.TURNS):
            to = lax.rem(p.z + r, 4)
            yy = 1 - p.y if y else p.y
            self.third.append(
                remote(self.sum_s.at[yy, to], self.got.at[p.z, p.y], send.at[2 + n], recv.at[2 + n], p.at(r, y))
            )

    def start(self):
        self.first.start()

    def over_x(self):
        self.first.wait_recv()
        self.sum_x[...] = self.own[self.p.c] + self.r1[...]
        self.second.start()

    def over_seq(self):
        p = self.p
        self.second.wait_recv()
        self.sum_s[...] = self.sum_x[p.x] + self.r2[...]
        for copy in self.third:
            copy.start()
        self.got[p.z, p.y] = self.sum_s[p.y, p.z]

    def finish(self, out_ref):
        for copy in self.third:
            copy.wait_recv()
        out_ref[...] = self.got[...]
        for copy in [self.first, self.second] + self.third:
            copy.wait_send()


GATHER, SCATTER, PROBS = 3, 12, 8


def mixture_kernel(
    routes_ref, router_ref, x_ref, g_ref, w_ref,
    x_all, xs_out, gs_out, st_ref, grad_out, sum_out, probs_out,
    tx, tg, xs, gs, gates, grads, ranks, weights, load_sem, save_sem, *rest,
):
    p = Flip()
    chunk, e = pl.program_id(0), pl.program_id(1)
    experts, slots, width = xs.shape
    rows = tx.shape[1]
    gather = Gather(p, x_ref, x_all, rest[:GATHER])
    scatter = Scatter(p, rest[GATHER : GATHER + SCATTER])
    probs = Probs(p, rest[GATHER + SCATTER :])
    last = experts - 1

    def at_step(k, step, *events):
        def run():
            for event, *args in events:
                event(*args)

        pl.when((chunk == k) & (e == step))(run)

    def begin():
        barrier(gather.peers + [peer for peer, (r, y) in zip(probs.peers, probs.TURNS) if r and y])
        gather.start()
        gather.spread(3)
        gather.spread(0)

    at_step(0, 0, (begin,))
    at_step(0, 1, (gather.cross, 3))
    at_step(0, 3, (gather.cross, 1))
    at_step(0, 4, (gather.close, 3))
    at_step(0, 6, (gather.close, 1))
    at_step(1, 1, (gather.spread, 2))
    at_step(1, 4, (gather.cross, 2))
    at_step(1, 7, (gather.close, 2))
    for k in range(3):
        before = [(scatter.line, k - 1, 1)] if k else []
        at_step(k + 1, 0, *before, (scatter.diagonal, k, 0), (scatter.diagonal, k, 1))
        at_step(k + 1, 1, (scatter.across, k, 0))
        at_step(k + 1, 4, (scatter.across, k, 1))
        at_step(k + 1, 6, (scatter.line, k, 0))
    at_step(3, last, (scatter.line, 2, 1))

    back = jnp.where(chunk == 0, BACK[0], jnp.where(chunk == 1, BACK[1], jnp.where(chunk == 2, BACK[2], BACK[3])))
    first = p.at()[0] * experts

    def save(k, i):
        src, dst = ((xs, xs_out), (gs, gs_out))[i]
        return pltpu.make_async_copy(src.at[k], dst.at[chunk, k], save_sem.at[i, k])

    def place_rows(j):
        y, x, c = j // 4, (j // 2) % 2, j % 2
        routes = routes_ref[p.block(back, y, x, c)]
        hits = []
        for k in range(experts):
            same = jnp.where(routes == first + k, 1.0, 0.0)
            hits.append(jnp.max(same, axis=0, keepdims=True))
        hit = jnp.concatenate(hits, axis=0)
        before = lax.broadcasted_iota(jnp.int32, (rows, rows), 0) < lax.broadcasted_iota(
            jnp.int32, (rows, rows), 1
        )
        rank = jnp.dot(hit.astype(bf16), jnp.where(before, 1.0, 0.0).astype(bf16), preferred_element_type=f32)
        rank = jnp.where(hit > 0.5, rank.astype(jnp.int32), -1)
        ranks[j] = rank
        hot = slots_of_rows(rank)
        place = one_hot(hot)
        b = j % 2
        rows_x = tx[b]
        logits = dot(router_ref[...], rows_x, ((1,), (1,)))
        powers = jnp.exp(logits - jnp.max(logits, axis=0, keepdims=True))
        weights[...] = powers / jnp.sum(powers, axis=0, keepdims=True)
        chosen = weights[pl.ds(pl.multiple_of(first, experts), experts)]
        gate = jnp.sum(jnp.where(hot, chosen[:, None, :], 0.0), axis=-1, keepdims=True)
        at = pl.ds(j * CAP, CAP)
        gates[:, at] = jnp.broadcast_to(gate, (experts, CAP, 128))
        shape = (experts, CAP, width)
        xs[:, at] = jnp.dot(place, rows_x, preferred_element_type=f32).astype(bf16).reshape(shape)
        gs[:, at] = jnp.dot(place, tg[b], preferred_element_type=f32).astype(bf16).reshape(shape)

    @pl.when(e == 0)
    def _():
        def loads(j):
            at = p.block(back, j // 4, (j // 2) % 2, j % 2)
            b = j % 2
            return (
                pltpu.make_async_copy(x_all.at[at], tx.at[b], load_sem.at[b]),
                pltpu.make_async_copy(g_ref.at[at], tg.at[b], load_sem.at[2 + b]),
            )

        def arrive(j):
            if j % 2:
                for k in range(4):
                    pl.when(chunk == k)(gather.to_core[k][j // 2].wait_recv)
            elif j == 2:
                pl.when(chunk == 0)(functools.partial(gather.cross, 0))
            elif j == 6:

                @pl.when(chunk == 0)
                def _():
                    gather.close(0)
                    gather.spread(1)

        def fetch(j):
            arrive(j)
            for copy in loads(j):
                copy.start()

        fetch(0)
        for j in range(8):
            if j < 7:
                pl.when(chunk > 0)(functools.partial(fetch, j + 1))
            for copy in loads(j):
                copy.wait()
            place_rows(j)
            if j < 7:
                pl.when(chunk == 0)(functools.partial(fetch, j + 1))
        for k in range(experts):
            save(k, 0).start()
            save(k, 1).start()

    rows_x, rows_g = xs[e], gs[e]
    gain = gates[e][:, :1]
    gate = jnp.dot(rows_x, w_ref[0, 0], preferred_element_type=f32)
    up = jnp.dot(rows_x, w_ref[0, 1], preferred_element_type=f32)
    raw = jnp.dot(rows_g, w_ref[0, 2], preferred_element_type=f32)
    sigma = 1.0 / (1.0 + jnp.exp(-gate))
    silu = gate * sigma
    act = (silu * up).astype(bf16).astype(f32)
    grads[e] = jnp.broadcast_to(jnp.sum(raw * act, axis=-1, keepdims=True), (slots, 128))
    act_gated = (act * gain).astype(bf16)
    act_grad = raw * gain
    gate_low = (act_grad * up * sigma * (1.0 + gate * (1.0 - sigma))).astype(bf16)
    up_low = (act_grad * silu).astype(bf16)
    st_ref[0, 0, 0] = act_gated
    st_ref[0, 0, 1] = gate_low
    st_ref[0, 0, 2] = up_low
    save(e, 0).wait()
    save(e, 1).wait()
    z = dot(gate_low, w_ref[0, 0], ((1,), (1,))) + dot(up_low, w_ref[0, 1], ((1,), (1,)))
    xs[e] = z.astype(bf16)
    gs[e] = dot(act_gated, w_ref[0, 2], ((1,), (1,))).astype(bf16)

    for k in range(3):
        at_step(k + 1, last, (scatter.settle_core, k), *([(scatter.settle, k - 1)] if k else []))

    @pl.when(e == last)
    def _():
        @pl.when(chunk > 0)
        def _():
            pl.semaphore_wait(scatter.free.at[0], 1)

        for pos in (3, 1, 2, 0):
            for c in (1, 0):
                j = pos * 2 + c
                hot = slots_of_rows(ranks[j])
                place = one_hot(hot)
                at = pl.ds(j * CAP, CAP)
                for i, values in enumerate((xs, gs)):
                    flat = values[:, at].reshape(experts * CAP, width)
                    total = dot(place, flat, ((0,), (0,))).astype(bf16)
                    if c:
                        scatter.give[i, pos] = total
                        scatter.to_core(chunk, i, pos).start()
                    elif pos:
                        scatter.stage[lax.rem(chunk, 2), i, pos - 1] = total
                    else:
                        scatter.acc[chunk, i] = total
                zz = lax.rem(p.z + 4 - back, 4)
                yy, xx, cc = lax.rem(p.y + pos // 2, 2), lax.rem(p.x + pos % 2, 2), lax.rem(p.c + c, 2)
                probs.own[cc, xx, yy, zz] = jnp.sum(jnp.where(hot, grads[:, at, :1], 0.0), axis=1)

    @pl.when((chunk == 3) & (e == last))
    def _():
        probs.start()
        scatter.diagonal(3, 0)
        scatter.diagonal(3, 1)
        probs.over_x()
        scatter.across(3, 0)
        scatter.across(3, 1)
        probs.over_seq()
        gather.finish()
        scatter.line(3, 0)
        scatter.finish(0, grad_out)
        probs.finish(probs_out)
        scatter.line(3, 1)
        scatter.finish(1, sum_out)
        scatter.end()


def mixture_all(routes_all, router_rows, x, g_all, w_expert, collective_id):
    experts, _, width, hidden = w_expert.shape
    rows = x.shape[0]
    slots = 8 * CAP
    struct = jax.ShapeDtypeStruct
    V, S = pltpu.VMEM, pltpu.SemaphoreType.DMA
    slot = struct((4, experts, slots, width), bf16)
    whole = pl.BlockSpec((rows, width), lambda k, e: (0, 0))
    outs = pl.pallas_call(
        mixture_kernel,
        name="mixture",
        grid=(4, experts),
        out_shape=(
            struct((32, rows, width), bf16),
            slot,
            slot,
            struct((4, experts, 3, slots, hidden), bf16),
            struct((rows, width), f32),
            struct((rows, width), f32),
            struct((4, 2, experts, rows), f32),
        ),
        in_specs=[
            pl.BlockSpec(routes_all.shape, lambda k, e: (0, 0, 0)),
            pl.BlockSpec(router_rows.shape, lambda k, e: (0, 0)),
            ANY,
            ANY,
            pl.BlockSpec((1, 3, width, hidden), lambda k, e: (e, 0, 0, 0)),
        ],
        out_specs=(
            ANY,
            ANY,
            ANY,
            pl.BlockSpec((1, 1, 3, slots, hidden), lambda k, e: (k, e, 0, 0, 0)),
            whole,
            whole,
            pl.BlockSpec((4, 2, experts, rows), lambda k, e: (0, 0, 0, 0)),
        ),
        scratch_shapes=[
            V((2, rows, width), bf16), V((2, rows, width), bf16),
            V((experts, slots, width), bf16), V((experts, slots, width), bf16),
            V((experts, slots, 128), f32), V((experts, slots, 128), f32),
            V((8, experts, rows), jnp.int32), V((router_rows.shape[0], rows), f32),
            S((4,)), S((2, experts)),
            *Gather.scratch(), *Scatter.scratch(rows, width), *Probs.scratch((experts, rows)),
        ],
        compiler_params=pltpu.CompilerParams(
            collective_id=collective_id, has_side_effects=True, vmem_limit_bytes=62 << 20,
            dimension_semantics=("arbitrary", "arbitrary"),
        ),
    )(routes_all, router_rows, x, g_all, w_expert)
    return outs[1:]


def weights_kernel(xs_ref, gs_ref, st_ref, wg_ref):
    rows = xs_ref.shape[0] * xs_ref.shape[2]
    width = xs_ref.shape[-1]
    x = xs_ref[...].reshape(rows, width)
    g = gs_ref[...].reshape(rows, width)
    act, gate_low, up_low = (st_ref[:, 0, i].reshape(rows, -1) for i in range(3))
    hidden = act.shape[-1]
    both = dot(x, jnp.concatenate([gate_low, up_low], axis=1), ((0,), (0,)))
    wg_ref[0, 0] = both[:, :hidden]
    wg_ref[0, 1] = both[:, hidden:]
    wg_ref[0, 2] = dot(g, act, ((0,), (0,)))


def weights_all(xs, gs, st):
    chunks, experts, slots, width = xs.shape
    hidden = st.shape[-1]
    row = pl.BlockSpec((chunks, 1, slots, width), lambda e: (0, e, 0, 0))
    return pl.pallas_call(
        weights_kernel,
        name="weights",
        grid=(experts,),
        out_shape=jax.ShapeDtypeStruct((experts, 3, width, hidden), f32),
        in_specs=[row, row, pl.BlockSpec((chunks, 1, 3, slots, hidden), lambda e: (0, e, 0, 0, 0))],
        out_specs=pl.BlockSpec((1, 3, width, hidden), lambda e: (e, 0, 0, 0)),
        compiler_params=pltpu.CompilerParams(vmem_limit_bytes=60 << 20),
        cost_estimate=pl.CostEstimate(
            flops=6 * xs.size * hidden, bytes_accessed=4 * xs.size + 2 * st.size + 12 * experts * width * hidden,
            transcendentals=0,
        ),
    )(xs, gs, st)


class HeadsAttention:
    def __init__(self, hidden, segments, routes, w_in, w_out, w_router, gains, experts):
        seq, batch = 8, 4
        place, b = lax.axis_index("seq"), lax.axis_index("batch")
        self.rows, self.width = hidden.shape
        width = self.width
        self.hs = width // HEADS
        self.hl = HEADS // seq
        cols = self.hl * self.hs
        self.cols = cols
        top = routes.shape[1]
        total = experts * seq
        ints = jnp.concatenate([routes.T, segments[None], jnp.zeros((7, self.rows), jnp.int32)], axis=0)
        small = jnp.concatenate(
            [w_router, gains.T, jnp.zeros((w_router.shape[0], 128 - total - gains.shape[0]), bf16)], axis=1
        )
        hidden_all, w_cols, w_rows, ints, small = gather_first(hidden, w_in, w_out, ints, small, 0)
        length = seq * self.rows
        self.length = length
        self.w_cols = w_cols.reshape(width, 3 * cols)
        self.w_rows = w_rows.reshape(cols, width)
        small = small.reshape(width, 128)
        self.router_all = small[:, :total]
        self.gains_all = small[:, total : total + 4].T.astype(f32)
        self.routes_all = ints[:, :top]
        segment_all = lax.dynamic_slice_in_dim(ints.reshape(seq, batch, -1, self.rows), b, 1, 1)
        segment_all = segment_all[:, 0, top].reshape(length)
        gains_all = self.gains_all
        inputs = hidden_all.reshape(length, width).astype(f32)
        self.first_normal = inputs * rms_scale(inputs)
        normed = (self.first_normal * gains_all[0]).astype(bf16)
        self.normed = normed
        projected = jnp.dot(normed, self.w_cols, preferred_element_type=f32)
        query_raw = projected[:, :cols]
        key_raw = projected[:, cols : 2 * cols]
        squares = jnp.stack([jnp.sum(query_raw * query_raw, -1), jnp.sum(key_raw * key_raw, -1)], 0)
        scales = lax.rsqrt(self.over_heads(squares, 1) / width + epsilon)
        self.query_scale = scales[0][:, None]
        self.key_scale = scales[1][:, None]
        self.query_normal = query_raw * self.query_scale
        self.key_normal = key_raw * self.key_scale
        mine = lax.dynamic_slice_in_dim(gains_all, place * cols, cols, 1)
        self.query_gain, self.key_gain = mine[1], mine[2]
        positions = jnp.arange(length, dtype=jnp.int32)
        self.cosine, self.sine = rope_tables(positions, self.hs)
        shape = (length, self.hl, self.hs)

        def rot(u):
            u = u.reshape(shape)
            return (u * self.cosine + rotate_half(u) * self.sine).astype(bf16)

        self.query = rot(self.query_normal * self.query_gain)
        self.key = rot(self.key_normal * self.key_gain)
        self.value = projected[:, 2 * cols :].astype(bf16).reshape(shape)
        self.allowed = (positions[None, :] <= positions[:, None]) & (
            segment_all[None, :] == segment_all[:, None]
        )
        scores = self.scores()
        top = jnp.max(scores, axis=-1, keepdims=True)
        weights = jnp.exp(scores - top)
        total = jnp.sum(weights, axis=-1, keepdims=True)
        acc = jnp.einsum("hqk,khd->hqd", weights.astype(bf16), self.value, preferred_element_type=f32)
        self.log_total = top + jnp.log(total)
        self.attended = jnp.transpose(acc / total, (1, 0, 2))
        self.attn_low = self.attended.reshape(length, cols).astype(bf16)
        partial = jnp.dot(self.attn_low, self.w_rows, preferred_element_type=f32).astype(bf16)
        self.mixed = scatter_seq(partial.reshape(seq, self.rows, width), 2, f32)

    def over_heads(self, sums, collective_id):
        return sum_seq(sums.reshape(2, -1, 128), collective_id).reshape(2, self.length)

    def scores(self):
        scale = self.hs ** (-0.5)
        scores = jnp.einsum("qhd,khd->hqk", self.query, self.key, preferred_element_type=f32) * scale
        return jnp.where(self.allowed[None], scores, -jnp.inf)

    def back(self, middle_low, router_grad, ffn_gain_grad):
        seq, batch = 8, 4
        length, cols, width = self.length, self.cols, self.width
        scale = self.hs ** (-0.5)
        shape = (length, self.hl, self.hs)
        grad_all = lax.all_gather(middle_low, "seq", axis=0, tiled=True)
        out_grad = dot(self.attn_low, grad_all, ((0,), (0,))).astype(bf16)
        attn_grad = dot(grad_all, self.w_rows, ((1,), (1,))).astype(bf16).reshape(shape)
        delta = jnp.sum(attn_grad.astype(f32) * self.attended, axis=-1)
        probs = jnp.exp(self.scores() - self.log_total)
        prob_grad = jnp.einsum("qhd,khd->hqk", attn_grad, self.value, preferred_element_type=f32)
        score_grad = (probs * (prob_grad - delta.T[..., None])).astype(bf16)
        query_grad = jnp.einsum("hqk,khd->qhd", score_grad, self.key, preferred_element_type=f32) * scale
        key_grad = jnp.einsum("hqk,qhd->khd", score_grad, self.query, preferred_element_type=f32) * scale
        value_grad = jnp.einsum("hqk,qhd->khd", probs.astype(bf16), attn_grad, preferred_element_type=f32)

        def rot_back(u):
            return (u * self.cosine - rotate_half(u * self.sine)).reshape(length, cols)

        query_norm_grad = rot_back(query_grad)
        key_norm_grad = rot_back(key_grad)
        query_gain_grad = jnp.sum(query_norm_grad * self.query_normal, axis=0)
        key_gain_grad = jnp.sum(key_norm_grad * self.key_normal, axis=0)
        query_scaled = query_norm_grad * self.query_gain
        key_scaled = key_norm_grad * self.key_gain
        dots = jnp.stack(
            [jnp.sum(query_scaled * self.query_normal, -1), jnp.sum(key_scaled * self.key_normal, -1)], 0
        )
        means = self.over_heads(dots, 4) / width
        query_raw_grad = self.query_scale * (query_scaled - self.query_normal * means[0][:, None])
        key_raw_grad = self.key_scale * (key_scaled - self.key_normal * means[1][:, None])
        projected_grad = jnp.concatenate(
            [query_raw_grad, key_raw_grad, value_grad.reshape(length, cols)], axis=1
        ).astype(bf16)
        partial = dot(projected_grad, self.w_cols, ((1,), (1,)))
        in_grad = lax.optimization_barrier(dot(self.normed, projected_grad, ((0,), (0,))).astype(bf16))
        terms = in_grad.astype(f32) * self.w_cols.astype(f32)
        attn_gain_grad = jnp.sum(terms, axis=1) / self.gains_all[0]
        own = width // (seq * batch)

        lane = jnp.arange(router_grad.shape[1])
        mine = jnp.arange(seq)[:, None] == lax.axis_index("seq")
        total = self.router_all.shape[1]
        small = router_grad.reshape(seq, cols, -1)
        for n, value in enumerate((attn_gain_grad, query_gain_grad, key_gain_grad, ffn_gain_grad)):
            value = jnp.where(mine, value[None], 0.0) if n in (1, 2) else value.reshape(seq, cols)
            small = small + jnp.where(lane == total + n, value[:, :, None], 0.0)
        normed_grad, in_shard, out_shard, small = scatter_last(
            partial.astype(bf16).reshape(seq, self.rows, width),
            in_grad.reshape(seq, 2, 2, own, 3 * cols),
            out_grad.reshape(2, 2, own, width),
            small.reshape(4, 2, 2, 2, own, -1),
            5,
        )
        return normed_grad, in_shard, out_shard, small[:, :total], small[:, total : total + 4].T


def experts_by_tokens(ffn_in, cotangent_all, routes_all, w_expert, router_all):
    rows, width = ffn_in.shape
    xs, gs, factors, ffn_in_grad, mixture, probs = mixture_all(
        routes_all, router_all.T, ffn_in, cotangent_all.reshape(32, rows, width), w_expert, 6
    )
    prob_grad = probs.reshape(-1, rows).T
    return mixture, ffn_in_grad, prob_grad, weights_all(xs, gs, factors)


class TokensAttention:
    def __init__(self, hidden, segment_all, w_in, w_out, gains_all):
        place = lax.axis_index("seq")
        rows, width = hidden.shape
        self.rows, self.width = rows, width
        self.hs = width // HEADS
        self.sources = w_in, w_out
        self.gather_weights(w_in, w_out)
        inputs = hidden.astype(f32)
        self.normed = (inputs * rms_scale(inputs) * gains_all[0]).astype(bf16)
        projected = jnp.dot(self.normed, self.in_all, preferred_element_type=f32)
        query_raw = projected[:, :width]
        key_raw = projected[:, width : 2 * width]
        self.query_scale = rms_scale(query_raw)
        self.query_normal = query_raw * self.query_scale
        self.key_scale = rms_scale(key_raw)
        self.key_normal = key_raw * self.key_scale
        self.query_gain, self.key_gain = gains_all[1], gains_all[2]
        self.positions = place * rows + jnp.arange(rows, dtype=jnp.int32)
        self.cosine, self.sine = rope_tables(self.positions, self.hs)
        shape = (rows, HEADS, self.hs)

        def rot(u):
            u = u.reshape(shape)
            return (u * self.cosine + rotate_half(u) * self.sine).astype(bf16)

        self.query = rot(self.query_normal * self.query_gain)
        key = rot(self.key_normal * self.key_gain).reshape(rows, width)
        value = projected[:, 2 * width :].astype(bf16)
        self.kept = key, value
        self.gather_keys(key, value)
        self.segment_all = segment_all
        self.segment_own = lax.dynamic_slice_in_dim(segment_all, place * rows, rows, 0)
        length = self.key_all.shape[0]
        scores = self.scores(self.key_all.reshape(length, HEADS, self.hs), segment_all, 0)
        top = jnp.max(scores, axis=-1, keepdims=True)
        weights = jnp.exp(scores - top)
        total = jnp.sum(weights, axis=-1, keepdims=True)
        acc = jnp.einsum(
            "hqk,khd->hqd",
            weights.astype(bf16),
            self.value_all.reshape(length, HEADS, self.hs),
            preferred_element_type=f32,
        )
        self.log_total = top + jnp.log(total)
        self.attended = jnp.transpose(acc / total, (1, 0, 2))
        self.attn_low = self.attended.reshape(rows, width).astype(bf16)
        self.mixed = jnp.dot(self.attn_low, self.out_all, preferred_element_type=f32)

    def gather_weights(self, w_in, w_out):
        self.in_all = lax.all_gather(w_in, BOTH, axis=0, tiled=True)
        self.out_all = lax.all_gather(w_out, BOTH, axis=0, tiled=True)

    def gather_keys(self, key, value):
        self.key_all = lax.all_gather(key, "seq", axis=0, tiled=True)
        self.value_all = lax.all_gather(value, "seq", axis=0, tiled=True)

    def scores(self, key, segment, start):
        scale = self.hs ** (-0.5)
        scores = jnp.einsum("qhd,khd->hqk", self.query, key, preferred_element_type=f32) * scale
        key_positions = start + jnp.arange(key.shape[0], dtype=jnp.int32)
        allowed = (key_positions[None, :] <= self.positions[:, None]) & (
            segment[None, :] == self.segment_own[:, None]
        )
        return jnp.where(allowed[None], scores, -jnp.inf)

    def back(self, middle_low, router_grad, ffn_gain_grad):
        again = lax.optimization_barrier((middle_low, *self.sources, *self.kept))
        middle_low = again[0]
        self.gather_weights(*again[1:3])
        self.gather_keys(*again[3:])
        rows, width = self.rows, self.width
        scale = self.hs ** (-0.5)
        out_grad = dot(self.attn_low, middle_low, ((0,), (0,))).astype(bf16)
        out_shard = lax.psum_scatter(out_grad, BOTH, scatter_dimension=0, tiled=True).astype(f32)
        attn_grad = dot(middle_low, self.out_all, ((1,), (1,))).astype(bf16).reshape(rows, HEADS, self.hs)
        delta = jnp.sum(attn_grad.astype(f32) * self.attended, axis=-1).T
        length = self.key_all.shape[0]
        block = min(512, length)
        count = length // block

        def step(query_grad, item):
            key, value, segment, start = item
            probs = jnp.exp(self.scores(key, segment, start) - self.log_total)
            prob_grad = jnp.einsum("qhd,khd->hqk", attn_grad, value, preferred_element_type=f32)
            score_grad = (probs * (prob_grad - delta[..., None])).astype(bf16)
            query_grad = (
                query_grad + jnp.einsum("hqk,khd->qhd", score_grad, key, preferred_element_type=f32) * scale
            )
            key_grad = jnp.einsum("hqk,qhd->khd", score_grad, self.query, preferred_element_type=f32) * scale
            value_grad = jnp.einsum("hqk,qhd->khd", probs.astype(bf16), attn_grad, preferred_element_type=f32)
            return query_grad, jnp.concatenate(
                [key_grad.reshape(block, width), value_grad.reshape(block, width)], axis=1
            ).astype(bf16)

        query_grad, terms = lax.scan(
            step,
            jnp.zeros((rows, HEADS, self.hs), f32),
            (
                self.key_all.reshape(count, block, HEADS, self.hs),
                self.value_all.reshape(count, block, HEADS, self.hs),
                self.segment_all.reshape(count, block),
                jnp.arange(count, dtype=jnp.int32) * block,
            ),
        )
        kv_grad = lax.psum_scatter(
            terms.reshape(length, 2 * width), "seq", scatter_dimension=0, tiled=True
        ).astype(f32)
        key_grad = kv_grad[:, :width].reshape(rows, HEADS, self.hs)

        def rot_back(u):
            return (u * self.cosine - rotate_half(u * self.sine)).reshape(rows, width)

        query_norm_grad = rot_back(query_grad)
        key_norm_grad = rot_back(key_grad)
        query_gain_grad = jnp.sum(query_norm_grad * self.query_normal, axis=0)
        key_gain_grad = jnp.sum(key_norm_grad * self.key_normal, axis=0)
        query_raw_grad = norm_back(query_norm_grad, self.query_normal, self.query_scale, self.query_gain)
        key_raw_grad = norm_back(key_norm_grad, self.key_normal, self.key_scale, self.key_gain)
        projected_grad = jnp.concatenate([query_raw_grad, key_raw_grad, kv_grad[:, width:]], axis=1).astype(bf16)
        in_grad = dot(self.normed, projected_grad, ((0,), (0,))).astype(bf16)
        in_shard = lax.psum_scatter(in_grad, BOTH, scatter_dimension=0, tiled=True).astype(f32)
        normed_grad = dot(projected_grad, self.in_all, ((1,), (1,)))
        pair = lax.psum_scatter(
            jnp.stack([query_gain_grad, key_gain_grad], 1), BOTH, scatter_dimension=0, tiled=True
        )
        return normed_grad, in_shard, out_shard, router_grad, pair


def expert_math(slots, grads, gate_slot, w_expert):
    w_gate, w_up, w_down = w_expert[:, 0], w_expert[:, 1], w_expert[:, 2]
    gate = jnp.einsum("esd,edf->esf", slots, w_gate, preferred_element_type=f32)
    up = jnp.einsum("esd,edf->esf", slots, w_up, preferred_element_type=f32)
    sigma = jax.nn.sigmoid(gate)
    silu = gate * sigma
    act = (silu * up).astype(bf16).astype(f32)
    act_gated = (act * gate_slot).astype(bf16)
    act_raw = jnp.einsum("esd,edf->esf", grads, w_down, preferred_element_type=f32)
    gate_grad = jnp.sum(act_raw * act, axis=-1)
    act_grad = act_raw * gate_slot
    gate_low = (act_grad * up * sigma * (1.0 + gate * (1.0 - sigma))).astype(bf16)
    up_low = (act_grad * silu).astype(bf16)
    slot_grad = (
        jnp.einsum("esf,edf->esd", gate_low, w_gate, preferred_element_type=f32)
        + jnp.einsum("esf,edf->esd", up_low, w_up, preferred_element_type=f32)
    ).astype(bf16)
    result = jnp.einsum("esf,edf->esd", act_gated, w_down, preferred_element_type=f32).astype(bf16)
    expert_grad = jnp.stack(
        [
            jnp.einsum("esd,esf->edf", slots, gate_low, preferred_element_type=f32),
            jnp.einsum("esd,esf->edf", slots, up_low, preferred_element_type=f32),
            jnp.einsum("esd,esf->edf", grads, act_gated, preferred_element_type=f32),
        ],
        axis=1,
    )
    return result, slot_grad, gate_grad, expert_grad


def slot_places(hit):
    count = hit.astype(jnp.int32)
    rank = jnp.where(hit, jnp.cumsum(count, axis=1) - count, -1)
    return rank[:, :, :, None] == jnp.arange(CAP, dtype=jnp.int32)


def experts_by_slots(ffn_in, cotangent, routes, w_expert, router_all):
    seq, batch = lax.axis_size("seq"), lax.axis_size("batch")
    experts = w_expert.shape[0]
    total = experts * seq
    rows, width = ffn_in.shape
    hit = jnp.any(routes[:, :, None] == jnp.arange(total, dtype=jnp.int32), axis=1)[None]
    hot = slot_places(hit)[0]
    place_hot = hot.astype(bf16).reshape(rows, total * CAP)
    router = jax.nn.softmax(jnp.dot(ffn_in, router_all, preferred_element_type=f32), axis=-1)
    gate_slot = jnp.sum(jnp.where(hot, router[:, :, None], 0.0), axis=0).reshape(seq, experts, CAP, 1)

    def there(values):
        values = lax.all_to_all(values, "seq", split_axis=0, concat_axis=0, tiled=True)
        values = lax.all_gather(values, "batch", axis=0, tiled=True)
        values = jnp.transpose(values, (1, 0, 2, 3))
        return values.reshape(experts, batch * seq * CAP, values.shape[-1])

    def back(values):
        values = values.reshape(experts, batch * seq, CAP, values.shape[-1])
        values = jnp.transpose(values, (1, 0, 2, 3))
        values = lax.psum_scatter(values, "batch", scatter_dimension=0, tiled=True)
        values = lax.all_to_all(values, "seq", split_axis=0, concat_axis=0, tiled=True)
        return values.reshape(total * CAP, values.shape[-1])

    def slots_of(tokens):
        slots = dot(place_hot, tokens, ((0,), (0,))).astype(bf16)
        return there(slots.reshape(seq, experts, CAP, width))

    def tokens_of(slots):
        return jnp.dot(place_hot, back(slots), preferred_element_type=f32)

    result, slot_grad, gate_grad, expert_grad = expert_math(
        slots_of(ffn_in), slots_of(cotangent), there(gate_slot), w_expert
    )
    gate_grad = back(gate_grad[..., None]).reshape(1, total, CAP)
    prob_grad = jnp.sum(jnp.where(hot, gate_grad, 0.0), axis=-1)
    return tokens_of(result), tokens_of(slot_grad), prob_grad, expert_grad


def local(hidden, segments, routes, w_in, w_out, w_router, gains, w_expert, cotangent):
    seq = lax.axis_size("seq")
    total_experts = w_expert.shape[0] * seq
    by_heads = seq == 8 and lax.axis_size("batch") == 4

    inputs = hidden[0].astype(f32)
    first_scale = rms_scale(inputs)
    first_normal = inputs * first_scale
    if by_heads:
        cotangent_all = lax.all_gather(cotangent[0], BOTH, axis=0, tiled=True)
        attention = HeadsAttention(
            hidden[0], segments[0], routes[0], w_in, w_out, w_router, gains, w_expert.shape[0]
        )
        gains_all, router_all = attention.gains_all, attention.router_all
    else:
        small = lax.all_gather(jnp.concatenate([w_router, gains.T], axis=1), BOTH, axis=0, tiled=True)
        router_all = small[:, :total_experts]
        gains_all = small[:, total_experts:].T.astype(f32)
        segment_all = lax.all_gather(segments[0], "seq", axis=0, tiled=True)
        attention = TokensAttention(hidden[0], segment_all, w_in, w_out, gains_all)

    middle = inputs + attention.mixed
    second_scale = rms_scale(middle)
    second_normal = middle * second_scale
    ffn_in = (second_normal * gains_all[3]).astype(bf16)
    if by_heads:
        mixture, ffn_in_grad, prob_grad, expert_grad = experts_by_tokens(
            ffn_in, cotangent_all, attention.routes_all, w_expert, router_all
        )
    else:
        mixture, ffn_in_grad, prob_grad, expert_grad = experts_by_slots(
            ffn_in, cotangent[0], routes[0], w_expert, router_all
        )
    output = middle + mixture

    grad_out = cotangent[0].astype(f32)
    router = jax.nn.softmax(jnp.dot(ffn_in, router_all, preferred_element_type=f32), axis=-1)
    logit_grad = router * (prob_grad - jnp.sum(router * prob_grad, axis=-1, keepdims=True))
    logit_low = logit_grad.astype(bf16)
    if by_heads:
        wide = jnp.pad(logit_low, ((0, 0), (0, 128 - total_experts)))
        router_grad = dot(ffn_in, wide, ((0,), (0,)))
    else:
        router_grad = dot(ffn_in, logit_low, ((0,), (0,)))
    ffn_in_grad = ffn_in_grad + dot(logit_low, router_all, ((1,), (1,)))
    ffn_gain_grad = jnp.sum(ffn_in_grad * second_normal, axis=0)
    middle_grad = grad_out + norm_back(ffn_in_grad, second_normal, second_scale, gains_all[3])
    normed_grad, in_shard, out_shard, router_shard, gains_shard = attention.back(
        middle_grad.astype(bf16), router_grad, ffn_gain_grad
    )
    if not by_heads:
        attn_gain_grad = jnp.sum(normed_grad * first_normal, axis=0)
        ends = jnp.stack([attn_gain_grad, ffn_gain_grad], axis=1)
        sums = lax.psum_scatter(
            jnp.concatenate([router_shard, ends], axis=1), BOTH, scatter_dimension=0, tiled=True
        )
        router_shard, ends = sums[:, :total_experts], sums[:, total_experts:]
        gains_shard = jnp.stack([ends[:, 0], gains_shard[:, 0], gains_shard[:, 1], ends[:, 1]], axis=0)
    input_grad = middle_grad + norm_back(normed_grad, first_normal, first_scale, gains_all[0])
    return (
        output.astype(bf16)[None],
        input_grad[None],
        in_shard,
        out_shard,
        router_shard,
        gains_shard,
        expert_grad,
    )


def solution(mesh):
    placed = (
        P("batch", "seq", None),
        P("batch", "seq"),
        P("batch", "seq", None),
        P(BOTH, None),
        P(BOTH, None),
        P(BOTH, None),
        P(None, BOTH),
        P("seq", None, None, "batch"),
        P("batch", "seq", None),
    )
    return jax.shard_map(
        local,
        mesh=mesh,
        in_specs=placed,
        out_specs=(
            P("batch", "seq", None),
            P("batch", "seq", None),
            P(BOTH, None),
            P(BOTH, None),
            P(BOTH, None),
            P(None, BOTH),
            P("seq", None, None, "batch"),
        ),
        check_vma=False,
    )
```
